32 devices in a mesh: area: 2 (over x), row: 4 (over z), col: 4 (over y, core).
Axes of the slice: x: 2, y: 2, z: 4, core: 2. Of those that a mesh axis runs over, the one named last changes fastest.
Arguments:
- area_xy: float32 [2, 4096], P(None, 'area'), as said below
- sampling_var: float32 [4096], P('area'), may hold values from 8 to 128
- inducer_xy: float32 [2, 8192], replicated, as said below
- order: int32 [8192], replicated, may hold values from 0 to 8191, each once
- prior: float32 [8192], P(('row', 'col')), may hold values from 1 to 10
Outputs:
- panel_rows: float32 [512, 8192], P(None, ('row', 'col'))
- schur: float32 [8192, 8192], P('area', ('row', 'col'))
The draws below stay inside these ranges and needn't reach their ends.
Inputs may be any that keep to these rules, and one draw needn't show every extreme that they name: order names each Gram index's inducing point, each of 0 to 8191 once. `area_xy`: each area's coordinates lie between 0 and 12 / sqrt(8192). `inducer_xy`: each inducing point's coordinates lie between 0 and 12 / sqrt(8192).
All inputs are finite; a program needn't handle non-finite values.
Results may differ from the reference program's by a relative error of at most 0.00068.
Values sent between devices are 32-bit elements; how exact they have to be, the bound alone decides.
No kernel may reach another device: no remote copies, remote signals or barrier semaphores. Data moves between devices by JAX's collectives and lax.ppermute only.
A program may use at most 128 MiB of HBM per device.

```python
import math
import jax
import jax.numpy as jnp
from jax import lax

M = 8192
NB = 512
AREAS = 4096


def draw_area_xy(key, part):
    key = jax.random.fold_in(key, 11)
    side = 12.0 / math.sqrt(M)
    unit = jax.random.uniform(key, (2, AREAS), jnp.float32)
    return side * unit


def draw_inducer_xy(key, part):
    key = jax.random.fold_in(key, 23)
    side = 12.0 / math.sqrt(M)
    unit = jax.random.uniform(key, (2, M), jnp.float32)
    return side * unit


def block_scale(rng, dims, shards, smallest, high):
    loudness, own = 1.0, jax.random.fold_in(rng, 6)
    for dim, shards_of in shards:
        draws = jnp.exp(jax.random.uniform(jax.random.fold_in(own, dim), (shards_of,), jnp.float32, smallest / len(shards), high / len(shards)))
        loudness = loudness * jnp.repeat(draws, dims[dim] // shards_of).reshape([-1 if axis == dim else 1 for axis in range(len(dims))])
    return loudness


def setup_inputs(seed: int = 0) -> dict:
    arg_keys = jax.random.split(jax.random.key(seed), 6)
    return {
        "area_xy": draw_area_xy(jax.random.fold_in(arg_keys[5], 71), 0),
        "sampling_var": jnp.clip(jnp.exp(math.log(128.0) - 2.7725887 * jax.random.uniform(arg_keys[1], (AREAS,), jnp.float32) ** block_scale(arg_keys[1], (AREAS,), ((0, 2),), -0.2, 0.2)), 8.0, 128.0),
        "inducer_xy": draw_inducer_xy(jax.random.fold_in(arg_keys[5], 71), 0),
        "order": jax.random.permutation(arg_keys[3], M).astype(jnp.int32),
        "prior": jnp.clip(jnp.exp(math.log(10.0) - 2.3025851 * jax.random.uniform(arg_keys[4], (M,), jnp.float32) ** block_scale(arg_keys[4], (M,), ((0, 16),), -0.2, 0.2)), 1.0, 10.0),
    }


def kernel_rows(coords, weights_root, points, length_scale):
    delta_x = coords[0][:, None] - points[0][None, :]
    delta_y = coords[1][:, None] - points[1][None, :]
    distance = jnp.sqrt(delta_x * delta_x + delta_y * delta_y)
    return (weights_root[:, None] * jnp.exp(-distance / length_scale)).astype(jnp.bfloat16)

def reference(area_xy, sampling_var, inducer_xy, order, prior):
    length_scale = 2.0 / math.sqrt(M)
    weights_root = jnp.sqrt(1.0 / (0.5 + sampling_var))
    points = jnp.take(inducer_xy, order.astype(jnp.int32), axis=1)
    block = math.gcd(AREAS, 2048)

    def accumulate(running, step_index):
        first_area = (step_index * block).astype(jnp.int32)
        coords = lax.dynamic_slice_in_dim(area_xy, first_area, block, 1)
        weights_part = lax.dynamic_slice_in_dim(weights_root, first_area, block, 0)
        rows_part = kernel_rows(coords, weights_part, points, length_scale).astype(jnp.float32)
        return (running + jnp.dot(rows_part.T.astype(jnp.float32), rows_part.astype(jnp.float32), preferred_element_type=jnp.float32), None)
    gram, _ = lax.scan(accumulate, jnp.zeros((M, M), jnp.float32), jnp.arange(AREAS // block, dtype=jnp.int32))
    diagonal_ids = jnp.arange(M, dtype=jnp.int32)
    precision = (gram * (M / AREAS)).at[diagonal_ids, diagonal_ids].add(prior)
    lower = jnp.linalg.cholesky(precision[:NB, :NB])
    inverse = jax.scipy.linalg.solve_triangular(lower, jnp.eye(NB, dtype=jnp.float32), lower=True)
    panel_rows = jnp.dot(inverse.astype(jnp.float32), precision[:NB, :].astype(jnp.float32), precision=lax.Precision.HIGHEST, preferred_element_type=jnp.float32)
    update = jnp.dot(panel_rows.T.astype(jnp.float32), panel_rows.astype(jnp.float32), precision=lax.Precision.HIGHEST, preferred_element_type=jnp.float32)
    return (panel_rows, precision - update)
```

```python
import functools
import math

import jax
import jax.numpy as jnp
from jax import lax
from jax.experimental import pallas as pl
from jax.experimental.pallas import tpu as pltpu
from jax.sharding import PartitionSpec as P

NB = 512
LANES = 128
STRIP = 8
BLK = 128
CHUNK = 512
VMEM_BYTES = 60 * 1024 * 1024
HIGH = lax.Precision.HIGHEST
F32 = jnp.float32
BF16 = jnp.bfloat16


def split_pieces(value):
    first = value.astype(BF16)
    rest = value - first.astype(F32)
    second = rest.astype(BF16)
    third = (rest - second.astype(F32)).astype(BF16)
    return first, second, third


def nt_dot(left, right, precision=None):
    return lax.dot_general(
        left, right, (((1,), (1,)), ((), ())), precision=precision, preferred_element_type=F32
    )


def tn_dot(left, right, precision=None):
    return lax.dot_general(
        left, right, (((0,), (0,)), ((), ())), precision=precision, preferred_element_type=F32
    )


def block_position():
    return lax.axis_index("row") * lax.axis_size("col") + lax.axis_index("col")


def points_kernel(scale, starts_ref, order_ref, table_ref, x_ref, y_ref, columns_ref):
    tables = table_ref[...]
    quotients = tables.shape[1]
    pieces_x = split_pieces(tables[0] * scale)
    pieces_y = split_pieces(tables[1] * scale)
    columns_ref[...] = jnp.concatenate(
        [jnp.concatenate(pieces_x, axis=0), jnp.concatenate(pieces_y, axis=0)], axis=1
    ).T
    quotient_ids = lax.broadcasted_iota(jnp.int32, (quotients, LANES), 0)
    lane_ids = lax.broadcasted_iota(jnp.int32, (LANES, LANES), 0)
    on_diagonal = lane_ids == lax.broadcasted_iota(jnp.int32, (LANES, LANES), 1)
    ones = jnp.ones((3 * LANES, LANES), BF16)

    def spread(row):
        diagonals = [
            jnp.where(on_diagonal, jnp.broadcast_to(piece.astype(F32), (LANES, LANES)), 0.0)
            for piece in split_pieces(row)
        ]
        return jnp.dot(
            jnp.concatenate(diagonals, axis=1).astype(BF16), ones, preferred_element_type=F32
        )

    def one_block(step, carry):
        row = jnp.where(
            step < starts_ref[0],
            step,
            jnp.where(
                step < starts_ref[1], starts_ref[2] + step - starts_ref[0], starts_ref[3] + step - starts_ref[1]
            ),
        )
        ids = order_ref[pl.ds(row, 1), :]
        hit = jnp.where(quotient_ids == lax.shift_right_logical(ids, 7), 1.0, 0.0).astype(BF16)
        values = jnp.dot(
            columns_ref[...], jnp.concatenate([hit, hit, hit], axis=0), preferred_element_type=F32
        )
        mine = lane_ids == lax.bitwise_and(ids, LANES - 1)
        rows = pl.ds(pl.multiple_of(step * LANES, LANES), LANES)
        x_ref[rows, :] = spread(jnp.sum(jnp.where(mine, values[:LANES], 0.0), axis=0, keepdims=True))
        y_ref[rows, :] = spread(jnp.sum(jnp.where(mine, values[LANES:], 0.0), axis=0, keepdims=True))
        return carry

    lax.fori_loop(0, x_ref.shape[0] // LANES, one_block, 0)


def gram_points(order, inducer_xy, scale, col_width, row_height):
    quotients = order.shape[0] // LANES
    starts = jnp.stack(
        [
            jnp.int32(NB // LANES),
            jnp.int32((NB + col_width) // LANES),
            block_position() * (col_width // LANES),
            lax.axis_index("area") * (row_height // LANES),
        ]
    ).astype(jnp.int32)
    count = NB + col_width + row_height
    shape = jax.ShapeDtypeStruct((count, LANES), F32)
    return pl.pallas_call(
        functools.partial(points_kernel, scale),
        out_shape=(shape, shape),
        in_specs=[
            pl.BlockSpec(memory_space=pltpu.SMEM),
            pl.BlockSpec(memory_space=pltpu.VMEM),
            pl.BlockSpec(memory_space=pltpu.VMEM),
        ],
        out_specs=[pl.BlockSpec(memory_space=pltpu.VMEM)] * 2,
        scratch_shapes=[pltpu.VMEM((2 * LANES, 3 * quotients), BF16)],
        compiler_params=pltpu.CompilerParams(vmem_limit_bytes=VMEM_BYTES),
        name="points",
    )(starts, order.reshape(quotients, LANES), inducer_xy.reshape(2, quotients, LANES))


def fill_kernel(dest, dest_area, x_ref, y_ref, first_row, row_count, area_ref, first_area, area_count):
    for pair in range(area_count // 256):
        areas = []
        for half in range(2):
            lanes = pl.ds(first_area + pair * 256 + half * LANES, LANES)
            areas.append(
                [jnp.broadcast_to(area_ref[k : k + 1, lanes], (16, LANES)) for k in range(3)]
            )
        for group in range(row_count // 16):
            rows = pl.ds(first_row + group * 16, 16)
            point_x, point_y = x_ref[rows, :], y_ref[rows, :]
            for half in range(2):
                area_x, area_y, log_weight = areas[half]
                delta_x, delta_y = area_x - point_x, area_y - point_y
                square = jnp.maximum(delta_x * delta_x + delta_y * delta_y, 1e-30)
                value = jnp.exp2(log_weight - square * lax.rsqrt(square))
                dest[
                    pl.ds(group * 16, 16), pl.ds(dest_area + pair * 256 + half * LANES, LANES)
                ] = value.astype(BF16)


def head_kernel(
    factor, offset_ref, x_ref, y_ref, area_ref, first_prior_ref, prior_ref, head_ref, cols_ref, system_ref
):
    col_width = cols_ref.shape[0]
    total = area_ref.shape[1]
    system_ref[...] = jnp.zeros_like(system_ref)

    def step(index, carry):
        first = pl.multiple_of(index * CHUNK, CHUNK)
        here = pl.ds(first, CHUNK)
        fill_kernel(head_ref, first, x_ref, y_ref, 0, NB, area_ref, first, CHUNK)
        fill_kernel(cols_ref, first, x_ref, y_ref, NB, col_width, area_ref, first, CHUNK)
        left = head_ref[:, here]
        system_ref[:, :NB] += nt_dot(left, left)
        system_ref[:, NB:] += nt_dot(left, cols_ref[:, here])
        return carry

    lax.fori_loop(0, total // CHUNK, step, 0)
    rows = lax.broadcasted_iota(jnp.int32, (NB, NB), 0)
    cols = lax.broadcasted_iota(jnp.int32, (NB, NB), 1)
    system_ref[:, :NB] = system_ref[:, :NB] * factor + jnp.where(
        rows == cols, first_prior_ref[...], 0.0
    )
    rows = lax.broadcasted_iota(jnp.int32, (NB, col_width), 0)
    cols = lax.broadcasted_iota(jnp.int32, (NB, col_width), 1) + offset_ref[0]
    system_ref[:, NB:] = system_ref[:, NB:] * factor + jnp.where(rows == cols, prior_ref[...], 0.0)


def whole_row(value, index):
    return jnp.broadcast_to(value[index : index + 1, :], (STRIP, LANES))


def whole_lane(value, index):
    return jnp.broadcast_to(value[:, index : index + 1], (STRIP, LANES))


def inverse_factor(block_ref, inverse_ref):
    count = BLK // STRIP
    row_ids = lax.broadcasted_iota(jnp.int32, (STRIP, LANES), 0)
    lane_ids = lax.broadcasted_iota(jnp.int32, (STRIP, LANES), 1)
    tops = [block_ref[i * STRIP : (i + 1) * STRIP, :] for i in range(count)]
    units = [jnp.where(lane_ids == row_ids + i * STRIP, 1.0, 0.0).astype(F32) for i in range(count)]
    for p in range(count):
        diag_cols = [whole_lane(tops[p], p * STRIP + j) for j in range(STRIP)]
        entry = {
            (i, j): whole_row(diag_cols[j], i) for j in range(STRIP) for i in range(j, STRIP)
        }
        top_rows = [whole_row(tops[p], j) for j in range(STRIP)]
        unit_rows = [whole_row(units[p], j) for j in range(STRIP)]
        roots = []
        for j in range(STRIP):
            root = lax.rsqrt(entry[j, j])
            roots.append(root)
            for i in range(j + 1, STRIP):
                entry[i, j] = entry[i, j] * root
            for k in range(j + 1, STRIP):
                for i in range(k, STRIP):
                    entry[i, k] = entry[i, k] - entry[i, j] * entry[k, j]
        for j in range(STRIP):
            for k in range(j):
                top_rows[j] = top_rows[j] - entry[j, k] * top_rows[k]
                unit_rows[j] = unit_rows[j] - entry[j, k] * unit_rows[k]
            top_rows[j] = top_rows[j] * roots[j]
            unit_rows[j] = unit_rows[j] * roots[j]
        for i in range(p + 1, count):
            cols = [whole_lane(tops[i], p * STRIP + j) for j in range(STRIP)]
            top, unit = tops[i], units[i]
            for j in range(STRIP):
                for k in range(j):
                    cols[j] = cols[j] - cols[k] * entry[j, k]
                cols[j] = cols[j] * roots[j]
                top = top - cols[j] * top_rows[j]
                unit = unit - cols[j] * unit_rows[j]
            tops[i], units[i] = top, unit
        final = unit_rows[STRIP - 1]
        for j in range(STRIP - 1):
            final = jnp.where(row_ids == j, unit_rows[j], final)
        inverse_ref[p * STRIP : (p + 1) * STRIP, :] = final


def factor_kernel(system_ref, first_prior_ref, panel_ref, solved_ref, weighted_ref, work, block, inverses):
    count = NB // BLK
    work[...] = system_ref[...].reshape(work.shape)

    def eliminate(k, carry):
        block[...] = work[k, :, pl.ds(pl.multiple_of(k * BLK, BLK), BLK)]
        inverse_factor(block, inverses.at[k])
        row = jnp.dot(inverses[k], work[k], precision=HIGH, preferred_element_type=F32)
        work[k] = row
        for i in range(1, count):

            @pl.when(i > k)
            def _():
                work[i] -= tn_dot(row[:, i * BLK : (i + 1) * BLK], row, HIGH)

        return carry

    lax.fori_loop(0, count, eliminate, 0)
    for k in range(count - 1, -1, -1):
        mine = pl.ds(k * BLK, BLK)
        panel = work[k, :, NB:]
        panel_ref[mine, :] = panel
        if k < count - 1:
            panel = panel - jnp.dot(
                work[k, :, (k + 1) * BLK : NB],
                solved_ref[(k + 1) * BLK :, :],
                precision=HIGH,
                preferred_element_type=F32,
            )
        solved_ref[mine, :] = tn_dot(inverses[k], panel, HIGH)
    rows = lax.broadcasted_iota(jnp.int32, (NB, NB), 0)
    cols = lax.broadcasted_iota(jnp.int32, (NB, NB), 1)
    column = jnp.sum(jnp.where(rows == cols, first_prior_ref[...], 0.0), axis=1, keepdims=True)
    weighted_ref[...] = solved_ref[...] * column


def schur_kernel(
    factor,
    offset_ref,
    x_ref,
    y_ref,
    area_ref,
    prior_ref,
    head_ref,
    cols_ref,
    solved_ref,
    weighted_ref,
    out_ref,
    left_even,
    left_odd,
    residual,
):
    tile = pl.program_id(0)
    tiles = pl.num_programs(0)
    col_width = cols_ref.shape[0]
    total = area_ref.shape[1]
    steps = total // CHUNK
    first_points = NB + col_width
    tile_rows = out_ref.shape[0]

    @pl.when(tile == 0)
    def _():
        high = solved_ref[...].astype(BF16)
        low = (solved_ref[...] - high.astype(F32)).astype(BF16)

        def step(index, carry):
            first = pl.multiple_of(index * CHUNK, CHUNK)
            here = pl.ds(first, CHUNK)
            right = head_ref[:, here]
            removed = tn_dot(high, right) + tn_dot(low, right)
            residual[:, here] = (cols_ref[:, here].astype(F32) - removed).astype(BF16)
            fill_kernel(left_even, first, x_ref, y_ref, first_points, tile_rows, area_ref, first, CHUNK)
            return carry

        lax.fori_loop(0, steps, step, 0)

    def run(source, dest):
        out_ref[...] = jnp.zeros_like(out_ref)

        def step(index, carry):
            first = pl.multiple_of(index * CHUNK, CHUNK)
            here = pl.ds(first, CHUNK)
            out_ref[...] += nt_dot(source[:, here], residual[:, here])
            if dest is not None:
                next_row = pl.multiple_of(first_points + (tile + 1) * tile_rows, 16)
                fill_kernel(dest, first, x_ref, y_ref, next_row, tile_rows, area_ref, first, CHUNK)
            return carry

        lax.fori_loop(0, steps, step, 0)

    parity = lax.rem(tile, 2)
    more = tile < tiles - 1
    pl.when(jnp.logical_and(more, parity == 0))(lambda: run(left_even, left_odd))
    pl.when(jnp.logical_and(more, parity == 1))(lambda: run(left_odd, left_even))
    pl.when(jnp.logical_and(jnp.logical_not(more), parity == 0))(lambda: run(left_even, None))
    pl.when(jnp.logical_and(jnp.logical_not(more), parity == 1))(lambda: run(left_odd, None))

    rows = lax.broadcasted_iota(jnp.int32, (tile_rows, col_width), 0) + (offset_ref[1] + tile * tile_rows)
    cols = lax.broadcasted_iota(jnp.int32, (tile_rows, col_width), 1) + offset_ref[0]
    out_ref[...] = out_ref[...] * factor + jnp.where(rows == cols, prior_ref[...], 0.0)

    first_row = offset_ref[1] + tile * tile_rows

    @pl.when(first_row < NB)
    def _():
        out_ref[...] -= weighted_ref[pl.ds(pl.multiple_of(first_row, tile_rows), tile_rows), :]


def all_areas(array):
    axis = array.ndim - 1
    if lax.axis_size("area") == 2:
        other = lax.ppermute(array, "area", [(0, 1), (1, 0)])
        first = lax.axis_index("area") == 0
        return jnp.concatenate(
            [jnp.where(first, array, other), jnp.where(first, other, array)], axis=axis
        )
    return lax.all_gather(array, "area", axis=axis, tiled=True)


def per_device(area_xy, sampling_var, inducer_xy, order, prior):
    size_total = order.shape[0]
    length_scale = 2.0 / math.sqrt(size_total)
    scale = math.log2(math.e) / length_scale
    col_width = prior.shape[0]
    row_height = size_total // lax.axis_size("area")
    areas_total = area_xy.shape[1] * lax.axis_size("area")
    factor = size_total / areas_total

    own = jnp.concatenate([area_xy * scale, -0.5 * jnp.log2(0.5 + sampling_var)[None, :]], axis=0)
    areas = all_areas(own)
    first_prior = lax.all_gather(prior, ("row", "col"), axis=0, tiled=True)[:NB].reshape(1, NB)
    own_prior = prior.reshape(1, col_width)
    point_x, point_y = gram_points(order, inducer_xy, scale, col_width, row_height)
    offsets = jnp.stack(
        [block_position() * col_width, lax.axis_index("area") * row_height]
    ).astype(jnp.int32)

    tile_rows = min(row_height, 512 if areas_total <= 8192 else 256)
    smem = pl.BlockSpec(memory_space=pltpu.SMEM)
    vmem = pl.BlockSpec(memory_space=pltpu.VMEM)
    params = pltpu.CompilerParams(vmem_limit_bytes=VMEM_BYTES)
    head, cols, system = pl.pallas_call(
        functools.partial(head_kernel, factor),
        out_shape=(
            jax.ShapeDtypeStruct((NB, areas_total), BF16),
            jax.ShapeDtypeStruct((col_width, areas_total), BF16),
            jax.ShapeDtypeStruct((NB, NB + col_width), F32),
        ),
        in_specs=[smem] + [vmem] * 5,
        out_specs=[vmem] * 3,
        compiler_params=params,
        name="head",
    )(offsets, point_x, point_y, areas, first_prior, own_prior)
    panel_rows, solved, weighted = pl.pallas_call(
        factor_kernel,
        out_shape=(jax.ShapeDtypeStruct((NB, col_width), F32),) * 3,
        in_specs=[vmem] * 2,
        out_specs=[vmem] * 3,
        scratch_shapes=[
            pltpu.VMEM((NB // BLK, BLK, NB + col_width), F32),
            pltpu.VMEM((BLK, BLK), F32),
            pltpu.VMEM((NB // BLK, BLK, BLK), F32),
        ],
        compiler_params=params,
        name="factor",
    )(system, first_prior)
    schur = pl.pallas_call(
        functools.partial(schur_kernel, factor),
        grid=(row_height // tile_rows,),
        out_shape=jax.ShapeDtypeStruct((row_height, col_width), F32),
        in_specs=[smem] + [vmem] * 8,
        out_specs=pl.BlockSpec((tile_rows, col_width), lambda i: (i, 0)),
        scratch_shapes=[
            pltpu.VMEM((tile_rows, areas_total), BF16),
            pltpu.VMEM((tile_rows, areas_total), BF16),
            pltpu.VMEM((col_width, areas_total), BF16),
        ],
        compiler_params=params,
        name="schur",
    )(offsets, point_x, point_y, areas, own_prior, head, cols, solved, weighted)
    return (panel_rows, schur)


def solution(mesh):
    in_specs = (P(None, "area"), P("area"), P(), P(), P(("row", "col")))
    out_specs = (P(None, ("row", "col")), P("area", ("row", "col")))
    return jax.shard_map(
        per_device, mesh=mesh, in_specs=in_specs, out_specs=out_specs, check_vma=False
    )
```

```python
import functools
import math

import jax
import jax.numpy as jnp
from jax import lax
from jax.experimental import pallas as pl
from jax.experimental.pallas import tpu as pltpu
from jax.sharding import PartitionSpec as P

NB = 512
LANES = 128
STRIP = 8
BLK = 128
CHUNK = 1024
SPAN = 2048
VMEM_BYTES = 60 * 1024 * 1024
HIGH = lax.Precision.HIGHEST
F32 = jnp.float32
BF16 = jnp.bfloat16


def split_pieces(value):
    first = value.astype(BF16)
    rest = value - first.astype(F32)
    second = rest.astype(BF16)
    third = (rest - second.astype(F32)).astype(BF16)
    return first, second, third


def nt_dot(left, right, precision=None):
    return lax.dot_general(
        left, right, (((1,), (1,)), ((), ())), precision=precision, preferred_element_type=F32
    )


def tn_dot(left, right, precision=None):
    return lax.dot_general(
        left, right, (((0,), (0,)), ((), ())), precision=precision, preferred_element_type=F32
    )


def block_position():
    return lax.axis_index("row") * lax.axis_size("col") + lax.axis_index("col")


def points_kernel(scale, starts_ref, order_ref, table_ref, x_ref, y_ref, columns_ref):
    tables = table_ref[...]
    quotients = tables.shape[1]
    pieces_x = split_pieces(tables[0] * scale)
    pieces_y = split_pieces(tables[1] * scale)
    columns_ref[...] = jnp.concatenate(
        [jnp.concatenate(pieces_x, axis=0), jnp.concatenate(pieces_y, axis=0)], axis=1
    ).T
    quotient_ids = lax.broadcasted_iota(jnp.int32, (quotients, LANES), 0)
    lane_ids = lax.broadcasted_iota(jnp.int32, (LANES, LANES), 0)
    on_diagonal = lane_ids == lax.broadcasted_iota(jnp.int32, (LANES, LANES), 1)
    ones = jnp.ones((3 * LANES, LANES), BF16)

    def spread(row):
        diagonals = [
            jnp.where(on_diagonal, jnp.broadcast_to(piece.astype(F32), (LANES, LANES)), 0.0)
            for piece in split_pieces(row)
        ]
        return jnp.dot(
            jnp.concatenate(diagonals, axis=1).astype(BF16), ones, preferred_element_type=F32
        )

    def one_block(step):
        row = jnp.where(
            step < starts_ref[0],
            step,
            jnp.where(
                step < starts_ref[1], starts_ref[2] + step - starts_ref[0], starts_ref[3] + step - starts_ref[1]
            ),
        )
        ids = order_ref[pl.ds(row, 1), :]
        hit = jnp.where(quotient_ids == lax.shift_right_logical(ids, 7), 1.0, 0.0).astype(BF16)
        values = jnp.dot(
            columns_ref[...], jnp.concatenate([hit, hit, hit], axis=0), preferred_element_type=F32
        )
        mine = lane_ids == lax.bitwise_and(ids, LANES - 1)
        x_row = jnp.sum(jnp.where(mine, values[:LANES], 0.0), axis=0, keepdims=True)
        y_row = jnp.sum(jnp.where(mine, values[LANES:], 0.0), axis=0, keepdims=True)
        return spread(x_row), spread(y_row)

    blocks = x_ref.shape[0] // LANES
    unroll = next(count for count in (8, 7, 5, 4, 3, 2, 1) if blocks % count == 0)

    def several(group, carry):
        done = [one_block(group * unroll + i) for i in range(unroll)]
        for i, (x_block, y_block) in enumerate(done):
            rows = pl.ds(pl.multiple_of((group * unroll + i) * LANES, LANES), LANES)
            x_ref[rows, :] = x_block
            y_ref[rows, :] = y_block
        return carry

    lax.fori_loop(0, blocks // unroll, several, 0)


def gram_points(order, inducer_xy, scale, col_width, row_height):
    quotients = order.shape[0] // LANES
    starts = jnp.stack(
        [
            jnp.int32(NB // LANES),
            jnp.int32((NB + col_width) // LANES),
            block_position() * (col_width // LANES),
            lax.axis_index("area") * (row_height // LANES),
        ]
    ).astype(jnp.int32)
    count = NB + col_width + row_height
    shape = jax.ShapeDtypeStruct((count, LANES), F32)
    return pl.pallas_call(
        functools.partial(points_kernel, scale),
        out_shape=(shape, shape),
        in_specs=[
            pl.BlockSpec(memory_space=pltpu.SMEM),
            pl.BlockSpec(memory_space=pltpu.VMEM),
            pl.BlockSpec(memory_space=pltpu.VMEM),
        ],
        out_specs=[pl.BlockSpec(memory_space=pltpu.VMEM)] * 2,
        scratch_shapes=[pltpu.VMEM((2 * LANES, 3 * quotients), BF16)],
        compiler_params=pltpu.CompilerParams(vmem_limit_bytes=VMEM_BYTES),
        name="points",
    )(starts, order.reshape(quotients, LANES), inducer_xy.reshape(2, quotients, LANES))


def fill_kernel(dest, dest_area, x_ref, y_ref, first_row, row_count, area_ref, first_area, area_count):
    for pair in range(area_count // 256):
        areas = []
        for half in range(2):
            lanes = pl.ds(first_area + pair * 256 + half * LANES, LANES)
            areas.append(
                [jnp.broadcast_to(area_ref[k : k + 1, lanes], (16, LANES)) for k in range(3)]
            )
        for group in range(row_count // 16):
            rows = pl.ds(first_row + group * 16, 16)
            point_x, point_y = x_ref[rows, :], y_ref[rows, :]
            for half in range(2):
                area_x, area_y, log_weight = areas[half]
                delta_x, delta_y = area_x - point_x, area_y - point_y
                square = jnp.maximum(delta_x * delta_x + delta_y * delta_y, 1e-30)
                value = jnp.exp(log_weight - square * lax.rsqrt(square))
                dest[
                    pl.ds(group * 16, 16), pl.ds(dest_area + pair * 256 + half * LANES, LANES)
                ] = value.astype(BF16)


def head_kernel(
    factor, offset_ref, x_ref, y_ref, area_ref, prior_ref, head_ref, cols_ref, system_ref
):
    col_width = cols_ref.shape[0]
    total = area_ref.shape[1]
    system_ref[...] = jnp.zeros_like(system_ref)

    def step(index, carry):
        first = pl.multiple_of(index * CHUNK, CHUNK)
        here = pl.ds(first, CHUNK)
        fill_kernel(head_ref, first, x_ref, y_ref, 0, NB, area_ref, first, CHUNK)
        fill_kernel(cols_ref, first, x_ref, y_ref, NB, col_width, area_ref, first, CHUNK)
        left = head_ref[:, here]
        system_ref[:, :NB] += nt_dot(left, left)
        system_ref[:, NB:] += nt_dot(left, cols_ref[:, here])
        return carry

    lax.fori_loop(0, total // CHUNK, step, 0)
    system_ref[:, :NB] = system_ref[:, :NB] * factor
    rows = lax.broadcasted_iota(jnp.int32, (NB, col_width), 0)
    cols = lax.broadcasted_iota(jnp.int32, (NB, col_width), 1) + offset_ref[0]
    system_ref[:, NB:] = system_ref[:, NB:] * factor + jnp.where(rows == cols, prior_ref[...], 0.0)


def whole_row(value, index):
    return jnp.broadcast_to(value[index : index + 1, :], (STRIP, LANES))


def whole_lane(value, index):
    return jnp.broadcast_to(value[:, index : index + 1], (STRIP, LANES))


def inverse_factor(block_ref, inverse_ref):
    count = BLK // STRIP
    row_ids = lax.broadcasted_iota(jnp.int32, (STRIP, LANES), 0)
    lane_ids = lax.broadcasted_iota(jnp.int32, (STRIP, LANES), 1)
    tops = [block_ref[i * STRIP : (i + 1) * STRIP, :] for i in range(count)]
    units = [jnp.where(lane_ids == row_ids + i * STRIP, 1.0, 0.0).astype(F32) for i in range(count)]
    for p in range(count):
        diag_cols = [whole_lane(tops[p], p * STRIP + j) for j in range(STRIP)]
        entry = {
            (i, j): whole_row(diag_cols[j], i) for j in range(STRIP) for i in range(j, STRIP)
        }
        top_rows = [whole_row(tops[p], j) for j in range(STRIP)]
        unit_rows = [whole_row(units[p], j) for j in range(STRIP)]
        roots = []
        for j in range(STRIP):
            root = lax.rsqrt(entry[j, j])
            roots.append(root)
            for i in range(j + 1, STRIP):
                entry[i, j] = entry[i, j] * root
            for k in range(j + 1, STRIP):
                for i in range(k, STRIP):
                    entry[i, k] = entry[i, k] - entry[i, j] * entry[k, j]
        for j in range(STRIP):
            for k in range(j):
                top_rows[j] = top_rows[j] - entry[j, k] * top_rows[k]
                unit_rows[j] = unit_rows[j] - entry[j, k] * unit_rows[k]
            top_rows[j] = top_rows[j] * roots[j]
            unit_rows[j] = unit_rows[j] * roots[j]
        for i in range(p + 1, count):
            cols = [whole_lane(tops[i], p * STRIP + j) for j in range(STRIP)]
            top, unit = tops[i], units[i]
            for j in range(STRIP):
                for k in range(j):
                    cols[j] = cols[j] - cols[k] * entry[j, k]
                cols[j] = cols[j] * roots[j]
                top = top - cols[j] * top_rows[j]
                unit = unit - cols[j] * unit_rows[j]
            tops[i], units[i] = top, unit
        final = unit_rows[STRIP - 1]
        for j in range(STRIP - 1):
            final = jnp.where(row_ids == j, unit_rows[j], final)
        inverse_ref[p * STRIP : (p + 1) * STRIP, :] = final


def factor_kernel(system_ref, first_prior_ref, panel_ref, solved_ref, weighted_ref, work, block, inverses):
    count = NB // BLK
    rows = lax.broadcasted_iota(jnp.int32, (NB, NB), 0)
    cols = lax.broadcasted_iota(jnp.int32, (NB, NB), 1)
    diagonal = jnp.where(rows == cols, first_prior_ref[...], 0.0)
    work[:, :, :NB] = (system_ref[:, :NB] + diagonal).reshape(count, BLK, NB)
    work[:, :, NB:] = system_ref[:, NB:].reshape(count, BLK, panel_ref.shape[1])

    def eliminate(k, carry):
        block[...] = work[k, :, pl.ds(pl.multiple_of(k * BLK, BLK), BLK)]
        inverse_factor(block, inverses.at[k])
        row = jnp.dot(inverses[k], work[k], precision=HIGH, preferred_element_type=F32)
        work[k] = row
        for i in range(1, count):

            @pl.when(i > k)
            def _():
                work[i] -= tn_dot(row[:, i * BLK : (i + 1) * BLK], row, HIGH)

        return carry

    lax.fori_loop(0, count, eliminate, 0)
    for k in range(count - 1, -1, -1):
        mine = pl.ds(k * BLK, BLK)
        panel = work[k, :, NB:]
        panel_ref[mine, :] = panel
        if k < count - 1:
            panel = panel - jnp.dot(
                work[k, :, (k + 1) * BLK : NB],
                solved_ref[(k + 1) * BLK :, :],
                precision=HIGH,
                preferred_element_type=F32,
            )
        solved_ref[mine, :] = tn_dot(inverses[k], panel, HIGH)
    column = jnp.sum(diagonal, axis=1, keepdims=True)
    weighted_ref[...] = solved_ref[...] * column


def schur_kernel(
    factor,
    offset_ref,
    x_ref,
    y_ref,
    area_ref,
    prior_ref,
    head_ref,
    cols_ref,
    solved_ref,
    weighted_ref,
    out_ref,
    left_even,
    left_odd,
    residual,
):
    tile = pl.program_id(0)
    tiles = pl.num_programs(0)
    col_width = cols_ref.shape[0]
    total = area_ref.shape[1]
    steps = total // CHUNK
    first_points = NB + col_width
    tile_rows = out_ref.shape[0]

    @pl.when(tile == 0)
    def _():
        high = solved_ref[...].astype(BF16)
        low = (solved_ref[...] - high.astype(F32)).astype(BF16)

        def step(index, carry):
            first = pl.multiple_of(index * CHUNK, CHUNK)
            here = pl.ds(first, CHUNK)
            right = head_ref[:, here]
            removed = tn_dot(high, right) + tn_dot(low, right)
            residual[here, :] = (cols_ref[:, here].astype(F32) - removed).astype(BF16).T
            fill_kernel(left_even, first, x_ref, y_ref, first_points, tile_rows, area_ref, first, CHUNK)
            return carry

        lax.fori_loop(0, steps, step, 0)

    def run(source, dest):
        for first in range(0, total, SPAN):
            here = slice(first, first + SPAN)
            part = jnp.dot(source[:, here], residual[here, :], preferred_element_type=F32)
            out_ref[...] = part if first == 0 else out_ref[...] + part
            if dest is not None:
                next_row = pl.multiple_of(first_points + (tile + 1) * tile_rows, 16)
                fill_kernel(dest, first, x_ref, y_ref, next_row, tile_rows, area_ref, first, SPAN)

    parity = lax.rem(tile, 2)
    more = tile < tiles - 1
    pl.when(jnp.logical_and(more, parity == 0))(lambda: run(left_even, left_odd))
    pl.when(jnp.logical_and(more, parity == 1))(lambda: run(left_odd, left_even))
    pl.when(jnp.logical_and(jnp.logical_not(more), parity == 0))(lambda: run(left_even, None))
    pl.when(jnp.logical_and(jnp.logical_not(more), parity == 1))(lambda: run(left_odd, None))

    rows = lax.broadcasted_iota(jnp.int32, (tile_rows, col_width), 0) + (offset_ref[1] + tile * tile_rows)
    cols = lax.broadcasted_iota(jnp.int32, (tile_rows, col_width), 1) + offset_ref[0]
    out_ref[...] = out_ref[...] * factor + jnp.where(rows == cols, prior_ref[...], 0.0)

    first_row = offset_ref[1] + tile * tile_rows

    @pl.when(first_row < NB)
    def _():
        out_ref[...] -= weighted_ref[pl.ds(pl.multiple_of(first_row, tile_rows), tile_rows), :]


def all_areas(array):
    axis = array.ndim - 1
    if lax.axis_size("area") == 2:
        other = lax.ppermute(array, "area", [(0, 1), (1, 0)])
        first = lax.axis_index("area") == 0
        return jnp.concatenate(
            [jnp.where(first, array, other), jnp.where(first, other, array)], axis=axis
        )
    return lax.all_gather(array, "area", axis=axis, tiled=True)


def from_first(array, axis):
    total = jnp.where(lax.axis_index(axis) == 0, array, 0.0)
    for target in range(1, lax.axis_size(axis)):
        total = total + lax.ppermute(array, axis, [(0, target)])
    return total


def first_block_prior(prior):
    if prior.shape[0] == NB:
        return from_first(from_first(prior.reshape(1, NB), "col"), "row")
    return lax.all_gather(prior, ("row", "col"), axis=0, tiled=True)[:NB].reshape(1, NB)


def per_device(area_xy, sampling_var, inducer_xy, order, prior):
    size_total = order.shape[0]
    length_scale = 2.0 / math.sqrt(size_total)
    scale = 1.0 / length_scale
    col_width = prior.shape[0]
    row_height = size_total // lax.axis_size("area")
    areas_total = area_xy.shape[1] * lax.axis_size("area")
    factor = size_total / areas_total

    own = jnp.concatenate([area_xy * scale, -0.5 * jnp.log(0.5 + sampling_var)[None, :]], axis=0)
    areas = all_areas(own)
    first_prior = first_block_prior(prior)
    own_prior = prior.reshape(1, col_width)
    point_x, point_y = gram_points(order, inducer_xy, scale, col_width, row_height)
    offsets = jnp.stack(
        [block_position() * col_width, lax.axis_index("area") * row_height]
    ).astype(jnp.int32)

    tile_rows = min(row_height, 512 if areas_total <= 8192 else 256)
    smem = pl.BlockSpec(memory_space=pltpu.SMEM)
    vmem = pl.BlockSpec(memory_space=pltpu.VMEM)
    params = pltpu.CompilerParams(vmem_limit_bytes=VMEM_BYTES)
    head, cols, system = pl.pallas_call(
        functools.partial(head_kernel, factor),
        out_shape=(
            jax.ShapeDtypeStruct((NB, areas_total), BF16),
            jax.ShapeDtypeStruct((col_width, areas_total), BF16),
            jax.ShapeDtypeStruct((NB, NB + col_width), F32),
        ),
        in_specs=[smem] + [vmem] * 4,
        out_specs=[vmem] * 3,
        compiler_params=params,
        name="head",
    )(offsets, point_x, point_y, areas, own_prior)
    panel_rows, solved, weighted = pl.pallas_call(
        factor_kernel,
        out_shape=(jax.ShapeDtypeStruct((NB, col_width), F32),) * 3,
        in_specs=[vmem] * 2,
        out_specs=[vmem] * 3,
        scratch_shapes=[
            pltpu.VMEM((NB // BLK, BLK, NB + col_width), F32),
            pltpu.VMEM((BLK, BLK), F32),
            pltpu.VMEM((NB // BLK, BLK, BLK), F32),
        ],
        compiler_params=params,
        name="factor",
    )(system, first_prior)
    schur = pl.pallas_call(
        functools.partial(schur_kernel, factor),
        grid=(row_height // tile_rows,),
        out_shape=jax.ShapeDtypeStruct((row_height, col_width), F32),
        in_specs=[smem] + [vmem] * 8,
        out_specs=pl.BlockSpec((tile_rows, col_width), lambda i: (i, 0)),
        scratch_shapes=[
            pltpu.VMEM((tile_rows, areas_total), BF16),
            pltpu.VMEM((tile_rows, areas_total), BF16),
            pltpu.VMEM((areas_total, col_width), BF16),
        ],
        compiler_params=params,
        name="schur",
    )(offsets, point_x, point_y, areas, own_prior, head, cols, solved, weighted)
    return (panel_rows, schur)


def solution(mesh):
    in_specs = (P(None, "area"), P("area"), P(), P(), P(("row", "col")))
    out_specs = (P(None, ("row", "col")), P("area", ("row", "col")))
    return jax.shard_map(
        per_device, mesh=mesh, in_specs=in_specs, out_specs=out_specs, check_vma=False
    )
```

```python
import functools
import math

import jax
import jax.numpy as jnp
from jax import lax
from jax.experimental import pallas as pl
from jax.experimental.pallas import tpu as pltpu
from jax.sharding import PartitionSpec as P

NB = 512
LANES = 128
STRIP = 8
BLK = 128
CHUNK = 1024
SPAN = 512
VMEM_BYTES = 60 * 1024 * 1024
HIGH = lax.Precision.HIGHEST
F32 = jnp.float32
BF16 = jnp.bfloat16


def split_pieces(value):
    first = value.astype(BF16)
    rest = value - first.astype(F32)
    second = rest.astype(BF16)
    third = (rest - second.astype(F32)).astype(BF16)
    return first, second, third


def nt_dot(left, right, precision=None):
    return lax.dot_general(
        left, right, (((1,), (1,)), ((), ())), precision=precision, preferred_element_type=F32
    )


def tn_dot(left, right, precision=None):
    return lax.dot_general(
        left, right, (((0,), (0,)), ((), ())), precision=precision, preferred_element_type=F32
    )


def block_position():
    return lax.axis_index("row") * lax.axis_size("col") + lax.axis_index("col")


FEATURES = 32
PIECE_PAIRS = ((0, 0), (0, 1), (1, 0), (1, 1), (0, 2), (2, 0))


def write_features(dest, x_row, y_row, left):
    one = jnp.ones_like(x_row)
    norm = [piece.astype(F32) for piece in split_pieces(x_row * x_row + y_row * y_row)]
    rows = norm + [one] * 3 if left else [one] * 3 + norm
    for coordinate in (x_row, y_row):
        factor = 1.0 if left else -2.0
        pieces = [piece.astype(F32) * factor for piece in split_pieces(coordinate)]
        rows += [pieces[pair[0 if left else 1]] for pair in PIECE_PAIRS]
    for index, row in enumerate(rows):
        dest[index : index + 1, :] = row


def points_kernel(scale, center, starts_ref, order_ref, table_ref, features_ref, columns_ref, places, features):
    tables = table_ref[...]
    quotients = tables.shape[1]
    pieces_x = split_pieces(tables[0] * scale - center)
    pieces_y = split_pieces(tables[1] * scale - center)
    columns_ref[...] = jnp.concatenate(
        [jnp.concatenate(pieces_x, axis=0), jnp.concatenate(pieces_y, axis=0)], axis=1
    ).T
    quotient_ids = lax.broadcasted_iota(jnp.int32, (quotients, LANES), 0)
    lane_ids = lax.broadcasted_iota(jnp.int32, (LANES, LANES), 0)

    def one_block(step):
        row = jnp.where(
            step < starts_ref[0],
            step,
            jnp.where(
                step < starts_ref[1], starts_ref[2] + step - starts_ref[0], starts_ref[3] + step - starts_ref[1]
            ),
        )
        ids = order_ref[pl.ds(row, 1), :]
        hit = jnp.where(quotient_ids == lax.shift_right_logical(ids, 7), 1.0, 0.0).astype(BF16)
        values = jnp.dot(
            columns_ref[...], jnp.concatenate([hit, hit, hit], axis=0), preferred_element_type=F32
        )
        mine = lane_ids == lax.bitwise_and(ids, LANES - 1)
        return [
            jnp.sum(jnp.where(mine, values[k * LANES : (k + 1) * LANES], 0.0), axis=0, keepdims=True)
            for k in range(2)
        ]

    blocks = features_ref.shape[0] // LANES
    for step in range(blocks):
        x_row, y_row = one_block(step)
        places[0:1, step * LANES : (step + 1) * LANES] = x_row
        places[1:2, step * LANES : (step + 1) * LANES] = y_row
    features[...] = jnp.zeros_like(features)
    write_features(features, places[0:1, :], places[1:2, :], True)
    for step in range(blocks):
        mine = slice(step * LANES, (step + 1) * LANES)
        features_ref[mine, :] = features[:, mine].T.astype(BF16)


def gram_points(order, inducer_xy, scale, center, col_width, row_height):
    quotients = order.shape[0] // LANES
    starts = jnp.stack(
        [
            jnp.int32(NB // LANES),
            jnp.int32((NB + col_width) // LANES),
            block_position() * (col_width // LANES),
            lax.axis_index("area") * (row_height // LANES),
        ]
    ).astype(jnp.int32)
    count = NB + col_width + row_height
    return pl.pallas_call(
        functools.partial(points_kernel, scale, center),
        out_shape=jax.ShapeDtypeStruct((count, FEATURES), BF16),
        in_specs=[
            pl.BlockSpec(memory_space=pltpu.SMEM),
            pl.BlockSpec(memory_space=pltpu.VMEM),
            pl.BlockSpec(memory_space=pltpu.VMEM),
        ],
        out_specs=pl.BlockSpec(memory_space=pltpu.VMEM),
        scratch_shapes=[
            pltpu.VMEM((2 * LANES, 3 * quotients), BF16),
            pltpu.VMEM((2, count), F32),
            pltpu.VMEM((FEATURES, count), F32),
        ],
        compiler_params=pltpu.CompilerParams(vmem_limit_bytes=VMEM_BYTES),
        name="points",
    )(starts, order.reshape(quotients, LANES), inducer_xy.reshape(2, quotients, LANES))


def fill_kernel(dest, points, area_features, log_weights, first, count):
    for start in range(0, count, 256):
        lanes = pl.ds(first + start, 256)
        squares = jnp.dot(points, area_features[:, lanes], preferred_element_type=F32)
        weights = [
            jnp.broadcast_to(log_weights[2:3, pl.ds(first + start + half, LANES)], (16, LANES))
            for half in (0, LANES)
        ]
        for row in range(0, points.shape[0], 16):
            for half in range(2):
                square = jnp.maximum(
                    squares[row : row + 16, half * LANES : (half + 1) * LANES], 1e-30
                )
                value = jnp.exp2(weights[half] - square * lax.rsqrt(square))
                dest[row : row + 16, pl.ds(first + start + half * LANES, LANES)] = value.astype(BF16)


def head_kernel(
    factor, offset_ref, points_ref, area_ref, prior_ref, head_ref, cols_ref, system_ref, area_features_ref, features
):
    col_width = cols_ref.shape[0]
    total = area_ref.shape[1]
    features[...] = jnp.zeros_like(features)
    write_features(features, area_ref[0:1, :], area_ref[1:2, :], False)
    area_features_ref[...] = features[...].astype(BF16)
    log_weights = area_ref
    system_ref[...] = jnp.zeros_like(system_ref)

    def step(index, carry):
        first = pl.multiple_of(index * CHUNK, CHUNK)
        here = pl.ds(first, CHUNK)
        fill_kernel(head_ref, points_ref[:NB, :], area_features_ref, log_weights, first, CHUNK)
        fill_kernel(
            cols_ref, points_ref[NB : NB + col_width, :], area_features_ref, log_weights, first, CHUNK
        )
        left = head_ref[:, here]
        system_ref[:, :NB] += nt_dot(left, left)
        system_ref[:, NB:] += nt_dot(left, cols_ref[:, here])
        return carry

    lax.fori_loop(0, total // CHUNK, step, 0)
    system_ref[:, :NB] = system_ref[:, :NB] * factor
    rows = lax.broadcasted_iota(jnp.int32, (NB, col_width), 0)
    cols = lax.broadcasted_iota(jnp.int32, (NB, col_width), 1) + offset_ref[0]
    system_ref[:, NB:] = system_ref[:, NB:] * factor + jnp.where(rows == cols, prior_ref[...], 0.0)


def whole_row(value, index):
    return jnp.broadcast_to(value[index : index + 1, :], (STRIP, LANES))


def whole_lane(value, index):
    return jnp.broadcast_to(value[:, index : index + 1], (STRIP, LANES))


def inverse_factor(block_ref, inverse_ref):
    count = BLK // STRIP
    row_ids = lax.broadcasted_iota(jnp.int32, (STRIP, LANES), 0)
    lane_ids = lax.broadcasted_iota(jnp.int32, (STRIP, LANES), 1)
    tops = [block_ref[i * STRIP : (i + 1) * STRIP, :] for i in range(count)]
    units = [jnp.where(lane_ids == row_ids + i * STRIP, 1.0, 0.0).astype(F32) for i in range(count)]
    for p in range(count):
        diag_cols = [whole_lane(tops[p], p * STRIP + j) for j in range(STRIP)]
        entry = {
            (i, j): whole_row(diag_cols[j], i) for j in range(STRIP) for i in range(j, STRIP)
        }
        top_rows = [whole_row(tops[p], j) for j in range(STRIP)]
        unit_rows = [whole_row(units[p], j) for j in range(STRIP)]
        roots = []
        for j in range(STRIP):
            root = lax.rsqrt(entry[j, j])
            roots.append(root)
            for i in range(j + 1, STRIP):
                entry[i, j] = entry[i, j] * root
            for k in range(j + 1, STRIP):
                for i in range(k, STRIP):
                    entry[i, k] = entry[i, k] - entry[i, j] * entry[k, j]
        for j in range(STRIP):
            for k in range(j):
                top_rows[j] = top_rows[j] - entry[j, k] * top_rows[k]
                unit_rows[j] = unit_rows[j] - entry[j, k] * unit_rows[k]
            top_rows[j] = top_rows[j] * roots[j]
            unit_rows[j] = unit_rows[j] * roots[j]
        for i in range(p + 1, count):
            cols = [whole_lane(tops[i], p * STRIP + j) for j in range(STRIP)]
            top, unit = tops[i], units[i]
            for j in range(STRIP):
                for k in range(j):
                    cols[j] = cols[j] - cols[k] * entry[j, k]
                cols[j] = cols[j] * roots[j]
                top = top - cols[j] * top_rows[j]
                unit = unit - cols[j] * unit_rows[j]
            tops[i], units[i] = top, unit
        final = unit_rows[STRIP - 1]
        for j in range(STRIP - 1):
            final = jnp.where(row_ids == j, unit_rows[j], final)
        inverse_ref[p * STRIP : (p + 1) * STRIP, :] = final


def factor_kernel(system_ref, first_prior_ref, panel_ref, solved_ref, weighted_ref, work, block, inverses):
    count = NB // BLK
    rows = lax.broadcasted_iota(jnp.int32, (NB, NB), 0)
    cols = lax.broadcasted_iota(jnp.int32, (NB, NB), 1)
    diagonal = jnp.where(rows == cols, first_prior_ref[...], 0.0)
    work[:, :, :NB] = (system_ref[:, :NB] + diagonal).reshape(count, BLK, NB)
    work[:, :, NB:] = system_ref[:, NB:].reshape(count, BLK, panel_ref.shape[1])

    def eliminate(k, carry):
        block[...] = work[k, :, pl.ds(pl.multiple_of(k * BLK, BLK), BLK)]
        inverse_factor(block, inverses.at[k])
        row = jnp.dot(inverses[k], work[k], precision=HIGH, preferred_element_type=F32)
        work[k] = row
        for i in range(1, count):

            @pl.when(i > k)
            def _():
                work[i] -= tn_dot(row[:, i * BLK : (i + 1) * BLK], row, HIGH)

        return carry

    lax.fori_loop(0, count, eliminate, 0)
    for k in range(count - 1, -1, -1):
        mine = pl.ds(k * BLK, BLK)
        panel = work[k, :, NB:]
        panel_ref[mine, :] = panel
        if k < count - 1:
            panel = panel - jnp.dot(
                work[k, :, (k + 1) * BLK : NB],
                solved_ref[(k + 1) * BLK :, :],
                precision=HIGH,
                preferred_element_type=F32,
            )
        solved_ref[mine, :] = tn_dot(inverses[k], panel, HIGH)
    column = jnp.sum(diagonal, axis=1, keepdims=True)
    weighted_ref[...] = solved_ref[...] * column


def schur_kernel(
    factor,
    offset_ref,
    points_ref,
    area_ref,
    area_features_ref,
    prior_ref,
    head_ref,
    cols_ref,
    solved_ref,
    weighted_ref,
    out_ref,
    left_even,
    left_odd,
    residual,
):
    tile = pl.program_id(0)
    tiles = pl.num_programs(0)
    col_width = cols_ref.shape[0]
    total = area_ref.shape[1]
    steps = total // CHUNK
    first_points = NB + col_width
    tile_rows = out_ref.shape[0]
    log_weights = area_ref

    @pl.when(tile == 0)
    def _():
        points = points_ref[first_points : first_points + tile_rows, :]
        high = solved_ref[...].astype(BF16)
        low = (solved_ref[...] - high.astype(F32)).astype(BF16)

        def step(index, carry):
            first = pl.multiple_of(index * CHUNK, CHUNK)
            here = pl.ds(first, CHUNK)
            right = head_ref[:, here]
            removed = tn_dot(high, right) + tn_dot(low, right)
            residual[here, :] = (cols_ref[:, here].astype(F32) - removed).astype(BF16).T
            fill_kernel(left_even, points, area_features_ref, log_weights, first, CHUNK)
            return carry

        lax.fori_loop(0, steps, step, 0)

    def run(source, dest):
        if dest is not None:
            next_row = pl.multiple_of(first_points + (tile + 1) * tile_rows, 16)
            points = points_ref[pl.ds(next_row, tile_rows), :]
        for first in range(0, total, SPAN):
            here = slice(first, first + SPAN)
            part = jnp.dot(source[:, here], residual[here, :], preferred_element_type=F32)
            out_ref[...] = part if first == 0 else out_ref[...] + part
            if dest is not None:
                fill_kernel(dest, points, area_features_ref, log_weights, first, SPAN)

    parity = lax.rem(tile, 2)
    more = tile < tiles - 1
    pl.when(jnp.logical_and(more, parity == 0))(lambda: run(left_even, left_odd))
    pl.when(jnp.logical_and(more, parity == 1))(lambda: run(left_odd, left_even))
    pl.when(jnp.logical_and(jnp.logical_not(more), parity == 0))(lambda: run(left_even, None))
    pl.when(jnp.logical_and(jnp.logical_not(more), parity == 1))(lambda: run(left_odd, None))

    rows = lax.broadcasted_iota(jnp.int32, (tile_rows, col_width), 0) + (offset_ref[1] + tile * tile_rows)
    cols = lax.broadcasted_iota(jnp.int32, (tile_rows, col_width), 1) + offset_ref[0]
    out_ref[...] = out_ref[...] * factor + jnp.where(rows == cols, prior_ref[...], 0.0)

    first_row = offset_ref[1] + tile * tile_rows

    @pl.when(first_row < NB)
    def _():
        out_ref[...] -= weighted_ref[pl.ds(pl.multiple_of(first_row, tile_rows), tile_rows), :]


def all_areas(array):
    axis = array.ndim - 1
    if lax.axis_size("area") == 2:
        other = lax.ppermute(array, "area", [(0, 1), (1, 0)])
        first = lax.axis_index("area") == 0
        return jnp.concatenate(
            [jnp.where(first, array, other), jnp.where(first, other, array)], axis=axis
        )
    return lax.all_gather(array, "area", axis=axis, tiled=True)


def from_first(array, axis):
    total = jnp.where(lax.axis_index(axis) == 0, array, 0.0)
    for target in range(1, lax.axis_size(axis)):
        total = total + lax.ppermute(array, axis, [(0, target)])
    return total


def first_block_prior(prior):
    if prior.shape[0] == NB:
        return from_first(from_first(prior.reshape(1, NB), "col"), "row")
    return lax.all_gather(prior, ("row", "col"), axis=0, tiled=True)[:NB].reshape(1, NB)


def per_device(area_xy, sampling_var, inducer_xy, order, prior):
    size_total = order.shape[0]
    length_scale = 2.0 / math.sqrt(size_total)
    scale = math.log2(math.e) / length_scale
    center = 6.0 / math.sqrt(size_total) * scale
    col_width = prior.shape[0]
    row_height = size_total // lax.axis_size("area")
    areas_total = area_xy.shape[1] * lax.axis_size("area")
    factor = size_total / areas_total

    own = jnp.concatenate([area_xy * scale - center, -0.5 * jnp.log2(0.5 + sampling_var)[None, :]], axis=0)
    areas = all_areas(own)
    first_prior = first_block_prior(prior)
    own_prior = prior.reshape(1, col_width)
    points = gram_points(order, inducer_xy, scale, center, col_width, row_height)
    offsets = jnp.stack(
        [block_position() * col_width, lax.axis_index("area") * row_height]
    ).astype(jnp.int32)

    tile_rows = min(row_height, 512 if areas_total <= 8192 else 256)
    smem = pl.BlockSpec(memory_space=pltpu.SMEM)
    vmem = pl.BlockSpec(memory_space=pltpu.VMEM)
    params = pltpu.CompilerParams(vmem_limit_bytes=VMEM_BYTES)
    head, cols, system, area_features = pl.pallas_call(
        functools.partial(head_kernel, factor),
        out_shape=(
            jax.ShapeDtypeStruct((NB, areas_total), BF16),
            jax.ShapeDtypeStruct((col_width, areas_total), BF16),
            jax.ShapeDtypeStruct((NB, NB + col_width), F32),
            jax.ShapeDtypeStruct((FEATURES, areas_total), BF16),
        ),
        in_specs=[smem] + [vmem] * 3,
        out_specs=[vmem] * 4,
        scratch_shapes=[pltpu.VMEM((FEATURES, areas_total), F32)],
        compiler_params=params,
        name="head",
    )(offsets, points, areas, own_prior)
    panel_rows, solved, weighted = pl.pallas_call(
        factor_kernel,
        out_shape=(jax.ShapeDtypeStruct((NB, col_width), F32),) * 3,
        in_specs=[vmem] * 2,
        out_specs=[vmem] * 3,
        scratch_shapes=[
            pltpu.VMEM((NB // BLK, BLK, NB + col_width), F32),
            pltpu.VMEM((BLK, BLK), F32),
            pltpu.VMEM((NB // BLK, BLK, BLK), F32),
        ],
        compiler_params=params,
        name="factor",
    )(system, first_prior)
    schur = pl.pallas_call(
        functools.partial(schur_kernel, factor),
        grid=(row_height // tile_rows,),
        out_shape=jax.ShapeDtypeStruct((row_height, col_width), F32),
        in_specs=[smem] + [vmem] * 8,
        out_specs=pl.BlockSpec((tile_rows, col_width), lambda i: (i, 0)),
        scratch_shapes=[
            pltpu.VMEM((tile_rows, areas_total), BF16),
            pltpu.VMEM((tile_rows, areas_total), BF16),
            pltpu.VMEM((areas_total, col_width), BF16),
        ],
        compiler_params=params,
        name="schur",
    )(offsets, points, areas, area_features, own_prior, head, cols, solved, weighted)
    return (panel_rows, schur)


def solution(mesh):
    in_specs = (P(None, "area"), P("area"), P(), P(), P(("row", "col")))
    out_specs = (P(None, ("row", "col")), P("area", ("row", "col")))
    return jax.shard_map(
        per_device, mesh=mesh, in_specs=in_specs, out_specs=out_specs, check_vma=False
    )
```

```python
import functools
import math

import jax
import jax.numpy as jnp
from jax import lax
from jax.experimental import pallas as pl
from jax.experimental.pallas import tpu as pltpu
from jax.sharding import PartitionSpec as P

NB = 512
LANES = 128
STRIP = 8
PANEL = 4
BLK = 128
CHUNK = 1024
SPAN = 512
VMEM_BYTES = 60 * 1024 * 1024
HIGH = lax.Precision.HIGHEST
F32 = jnp.float32
BF16 = jnp.bfloat16


def split_pieces(value):
    first = value.astype(BF16)
    rest = value - first.astype(F32)
    second = rest.astype(BF16)
    third = (rest - second.astype(F32)).astype(BF16)
    return first, second, third


def nt_dot(left, right, precision=None):
    return lax.dot_general(
        left, right, (((1,), (1,)), ((), ())), precision=precision, preferred_element_type=F32
    )


def tn_dot(left, right, precision=None):
    return lax.dot_general(
        left, right, (((0,), (0,)), ((), ())), precision=precision, preferred_element_type=F32
    )


def block_position():
    return lax.axis_index("row") * lax.axis_size("col") + lax.axis_index("col")


FEATURES = 32
PIECE_PAIRS = ((0, 0), (0, 1), (1, 0), (1, 1), (0, 2), (2, 0))


def write_features(dest, x_row, y_row, left):
    one = jnp.ones_like(x_row)
    norm = [piece.astype(F32) for piece in split_pieces(x_row * x_row + y_row * y_row)]
    rows = norm + [one] * 3 if left else [one] * 3 + norm
    for coordinate in (x_row, y_row):
        factor = 1.0 if left else -2.0
        pieces = [piece.astype(F32) * factor for piece in split_pieces(coordinate)]
        rows += [pieces[pair[0 if left else 1]] for pair in PIECE_PAIRS]
    for index, row in enumerate(rows):
        dest[index : index + 1, :] = row


def points_kernel(scale, center, starts_ref, order_ref, table_ref, features_ref, columns_ref, places, features):
    tables = table_ref[...]
    quotients = tables.shape[1]
    pieces_x = split_pieces(tables[0] * scale - center)
    pieces_y = split_pieces(tables[1] * scale - center)
    columns_ref[...] = jnp.concatenate(
        [jnp.concatenate(pieces_x, axis=0), jnp.concatenate(pieces_y, axis=0)], axis=1
    ).T
    quotient_ids = lax.broadcasted_iota(jnp.int32, (quotients, LANES), 0)
    lane_ids = lax.broadcasted_iota(jnp.int32, (LANES, LANES), 0)

    def one_block(step):
        row = jnp.where(
            step < starts_ref[0],
            step,
            jnp.where(
                step < starts_ref[1], starts_ref[2] + step - starts_ref[0], starts_ref[3] + step - starts_ref[1]
            ),
        )
        ids = order_ref[pl.ds(row, 1), :]
        hit = jnp.where(quotient_ids == lax.shift_right_logical(ids, 7), 1.0, 0.0).astype(BF16)
        values = jnp.dot(
            columns_ref[...], jnp.concatenate([hit, hit, hit], axis=0), preferred_element_type=F32
        )
        mine = lane_ids == lax.bitwise_and(ids, LANES - 1)
        return [
            jnp.sum(jnp.where(mine, values[k * LANES : (k + 1) * LANES], 0.0), axis=0, keepdims=True)
            for k in range(2)
        ]

    blocks = features_ref.shape[0] // LANES
    for step in range(blocks):
        x_row, y_row = one_block(step)
        places[0:1, step * LANES : (step + 1) * LANES] = x_row
        places[1:2, step * LANES : (step + 1) * LANES] = y_row
    features[...] = jnp.zeros_like(features)
    write_features(features, places[0:1, :], places[1:2, :], True)
    for step in range(blocks):
        mine = slice(step * LANES, (step + 1) * LANES)
        features_ref[mine, :] = features[:, mine].T.astype(BF16)


def gram_points(order, inducer_xy, scale, center, col_width, row_height):
    quotients = order.shape[0] // LANES
    starts = jnp.stack(
        [
            jnp.int32(NB // LANES),
            jnp.int32((NB + col_width) // LANES),
            block_position() * (col_width // LANES),
            lax.axis_index("area") * (row_height // LANES),
        ]
    ).astype(jnp.int32)
    count = NB + col_width + row_height
    return pl.pallas_call(
        functools.partial(points_kernel, scale, center),
        out_shape=jax.ShapeDtypeStruct((count, FEATURES), BF16),
        in_specs=[
            pl.BlockSpec(memory_space=pltpu.SMEM),
            pl.BlockSpec(memory_space=pltpu.VMEM),
            pl.BlockSpec(memory_space=pltpu.VMEM),
        ],
        out_specs=pl.BlockSpec(memory_space=pltpu.VMEM),
        scratch_shapes=[
            pltpu.VMEM((2 * LANES, 3 * quotients), BF16),
            pltpu.VMEM((2, count), F32),
            pltpu.VMEM((FEATURES, count), F32),
        ],
        compiler_params=pltpu.CompilerParams(vmem_limit_bytes=VMEM_BYTES),
        name="points",
    )(starts, order.reshape(quotients, LANES), inducer_xy.reshape(2, quotients, LANES))


def fill_kernel(dest, points, area_features, log_weights, first, count):
    for start in range(0, count, 256):
        lanes = pl.ds(first + start, 256)
        squares = jnp.dot(points, area_features[:, lanes], preferred_element_type=F32)
        weights = [
            jnp.broadcast_to(log_weights[2:3, pl.ds(first + start + half, LANES)], (16, LANES))
            for half in (0, LANES)
        ]
        for row in range(0, points.shape[0], 16):
            for half in range(2):
                square = jnp.maximum(
                    squares[row : row + 16, half * LANES : (half + 1) * LANES], 1e-30
                )
                value = jnp.exp2(weights[half] - square * lax.rsqrt(square))
                dest[row : row + 16, pl.ds(first + start + half * LANES, LANES)] = value.astype(BF16)


def whole_row(value, index):
    return jnp.broadcast_to(value[index : index + 1, :], (STRIP, LANES))


def whole_lane(value, index):
    return jnp.broadcast_to(value[:, index : index + 1], (STRIP, LANES))


def inverse_factor(block_ref, inverse_ref, beside):
    count = BLK // STRIP
    row_ids = lax.broadcasted_iota(jnp.int32, (STRIP, LANES), 0)
    lane_ids = lax.broadcasted_iota(jnp.int32, (STRIP, LANES), 1)
    tops = [block_ref[i * STRIP : (i + 1) * STRIP, :] for i in range(count)]
    units = [jnp.where(lane_ids == row_ids + i * STRIP, 1.0, 0.0).astype(F32) for i in range(count)]
    for p in range(count):
        panel_end = (p // PANEL + 1) * PANEL
        diag_cols = [whole_lane(tops[p], p * STRIP + j) for j in range(STRIP)]
        entry = {
            (i, j): whole_row(diag_cols[j], i) for j in range(STRIP) for i in range(j, STRIP)
        }
        top_rows = [whole_row(tops[p], j) for j in range(STRIP)]
        unit_rows = [whole_row(units[p], j) for j in range(STRIP)]
        roots = []
        for j in range(STRIP):
            root = lax.rsqrt(entry[j, j])
            roots.append(root)
            for i in range(j + 1, STRIP):
                entry[i, j] = entry[i, j] * root
            for k in range(j + 1, STRIP):
                for i in range(k, STRIP):
                    entry[i, k] = entry[i, k] - entry[i, j] * entry[k, j]
        for j in range(STRIP):
            for k in range(j):
                top_rows[j] = top_rows[j] - entry[j, k] * top_rows[k]
                unit_rows[j] = unit_rows[j] - entry[j, k] * unit_rows[k]
            top_rows[j] = top_rows[j] * roots[j]
            unit_rows[j] = unit_rows[j] * roots[j]
        for i in range(p + 1, panel_end):
            cols = [whole_lane(tops[i], p * STRIP + j) for j in range(STRIP)]
            top, unit = tops[i], units[i]
            for j in range(STRIP):
                for k in range(j):
                    cols[j] = cols[j] - cols[k] * entry[j, k]
                cols[j] = cols[j] * roots[j]
                top = top - cols[j] * top_rows[j]
                unit = unit - cols[j] * unit_rows[j]
            tops[i], units[i] = top, unit
        top, unit = top_rows[STRIP - 1], unit_rows[STRIP - 1]
        for j in range(STRIP - 1):
            top = jnp.where(row_ids == j, top_rows[j], top)
            unit = jnp.where(row_ids == j, unit_rows[j], unit)
        tops[p], units[p] = top, unit
        inverse_ref[p * STRIP : (p + 1) * STRIP, :] = unit
        beside(p)
        if p + 1 == panel_end and panel_end < count:
            panel = slice(panel_end - PANEL, panel_end)
            top = jnp.concatenate(tops[panel], axis=0)
            both = jnp.concatenate([top, jnp.concatenate(units[panel], axis=0)], axis=1)
            update = tn_dot(top, both, HIGH)
            for i in range(panel_end, count):
                mine = slice(i * STRIP, (i + 1) * STRIP)
                tops[i] = tops[i] - update[mine, :LANES]
                units[i] = units[i] - update[mine, LANES:]


def schur_kernel(
    factor,
    ahead,
    offset_ref,
    points_ref,
    area_ref,
    first_prior_ref,
    prior_ref,
    panel_ref,
    out_ref,
    head,
    cols,
    features,
    area_features,
    system,
    block,
    inverses,
    solved,
    weighted,
    residual,
    *lefts,
):
    tile = pl.program_id(0)
    col_width = cols.shape[0]
    total = area_ref.shape[1]
    first_points = NB + col_width
    tile_rows = out_ref.shape[0]
    tiles = (points_ref.shape[0] - first_points) // tile_rows

    def fill_left(index, first, count):
        start = first_points + index * tile_rows
        points = points_ref[start : start + tile_rows, :]
        fill_kernel(lefts[index % len(lefts)], points, area_features, area_ref, first, count)

    def products():
        features[...] = jnp.zeros_like(features)
        write_features(features, area_ref[0:1, :], area_ref[1:2, :], False)
        area_features[...] = features[...].astype(BF16)
        system[...] = jnp.zeros_like(system)
        group = min(4, total // CHUNK)

        def accumulate(first):
            here = pl.ds(first, CHUNK)
            left = head[:, here]
            system[:, :NB] += nt_dot(left, left)
            system[:, NB:] += nt_dot(left, cols[:, here])

        def step(index, carry):
            base = pl.multiple_of(index * (group * CHUNK), group * CHUNK)
            for part in range(group):
                first = base + part * CHUNK
                if part:
                    accumulate(first - CHUNK)
                fill_kernel(head, points_ref[:NB, :], area_features, area_ref, first, CHUNK)
                fill_kernel(
                    cols, points_ref[NB : NB + col_width, :], area_features, area_ref, first, CHUNK
                )
            accumulate(base + (group - 1) * CHUNK)
            return carry

        lax.fori_loop(0, total // (group * CHUNK), step, 0)

    def solve():
        rows = lax.broadcasted_iota(jnp.int32, (NB, NB), 0)
        lanes = lax.broadcasted_iota(jnp.int32, (NB, NB), 1)
        diagonal = jnp.where(rows == lanes, first_prior_ref[...], 0.0)
        system[:, :NB] = system[:, :NB] * factor + diagonal
        rows = lax.broadcasted_iota(jnp.int32, (NB, col_width), 0)
        lanes = lax.broadcasted_iota(jnp.int32, (NB, col_width), 1) + offset_ref[0]
        system[:, NB:] = system[:, NB:] * factor + jnp.where(rows == lanes, prior_ref[...], 0.0)
        weighted[...] = jnp.broadcast_to(jnp.sum(diagonal, axis=1, keepdims=True), weighted.shape)
        count = NB // BLK
        strips = BLK // STRIP
        quarter = total // count
        pieces = [(index, start) for index in range(ahead) for start in range(0, quarter, 256)]

        def eliminate(k, carry):
            mine = pl.ds(pl.multiple_of(k * BLK, BLK), BLK)
            block[...] = system[mine, mine]
            base = pl.multiple_of(k * quarter, quarter)

            def beside(p):
                for index, start in pieces[p * len(pieces) // strips : (p + 1) * len(pieces) // strips]:
                    fill_left(index, base + start, 256)

            inverse_factor(block, inverses.at[k], beside)
            row = jnp.dot(inverses[k], system[mine, :], precision=HIGH, preferred_element_type=F32)
            system[mine, :] = row
            for i in range(1, count):

                @pl.when(i > k)
                def _():
                    system[i * BLK : (i + 1) * BLK, :] -= tn_dot(row[:, i * BLK : (i + 1) * BLK], row, HIGH)

            return carry

        lax.fori_loop(0, count, eliminate, 0)
        for k in range(count - 1, -1, -1):
            mine = slice(k * BLK, (k + 1) * BLK)
            panel = system[mine, NB:]
            panel_ref[mine, :] = panel
            if k < count - 1:
                panel = panel - jnp.dot(
                    system[mine, (k + 1) * BLK : NB],
                    solved[(k + 1) * BLK :, :],
                    precision=HIGH,
                    preferred_element_type=F32,
                )
            solved[mine, :] = tn_dot(inverses[k], panel, HIGH)
        weighted[...] = weighted[...] * solved[...]

    def reduce_columns():
        high = solved[...].astype(BF16)
        low = (solved[...] - high.astype(F32)).astype(BF16)

        def step(index, carry):
            here = pl.ds(pl.multiple_of(index * CHUNK, CHUNK), CHUNK)
            right = head[:, here]
            removed = tn_dot(high, right) + tn_dot(low, right)
            residual[here, :] = (cols[:, here].astype(F32) - removed).astype(BF16).T
            return carry

        lax.fori_loop(0, total // CHUNK, step, 0)

    @pl.when(tile == 0)
    def _():
        products()
        solve()
        reduce_columns()

    def run(index):
        left = lefts[index % len(lefts)]
        for first in range(0, total, SPAN):
            here = slice(first, first + SPAN)
            part = jnp.dot(left[:, here], residual[here, :], preferred_element_type=F32)
            out_ref[...] = part if first == 0 else out_ref[...] + part
            if index + ahead < tiles:
                fill_left(index + ahead, first, SPAN)

    for index in range(tiles):
        pl.when(tile == index)(functools.partial(run, index))

    first_row = offset_ref[1] + tile * tile_rows
    rows = lax.broadcasted_iota(jnp.int32, (tile_rows, col_width), 0) + first_row
    lanes = lax.broadcasted_iota(jnp.int32, (tile_rows, col_width), 1) + offset_ref[0]
    out_ref[...] = out_ref[...] * factor + jnp.where(rows == lanes, prior_ref[...], 0.0)

    @pl.when(first_row < NB)
    def _():
        out_ref[...] -= weighted[pl.ds(pl.multiple_of(first_row, tile_rows), tile_rows), :]


def all_areas(array):
    axis = array.ndim - 1
    if lax.axis_size("area") == 2:
        other = lax.ppermute(array, "area", [(0, 1), (1, 0)])
        first = lax.axis_index("area") == 0
        return jnp.concatenate(
            [jnp.where(first, array, other), jnp.where(first, other, array)], axis=axis
        )
    return lax.all_gather(array, "area", axis=axis, tiled=True)


def first_block_prior(prior):
    if prior.shape[0] == NB:
        mine = jnp.where(block_position() == 0, prior, 0.0)
        return lax.psum(mine, ("row", "col")).reshape(1, NB)
    return lax.all_gather(prior, ("row", "col"), axis=0, tiled=True)[:NB].reshape(1, NB)


def per_device(area_xy, sampling_var, inducer_xy, order, prior):
    size_total = order.shape[0]
    length_scale = 2.0 / math.sqrt(size_total)
    scale = math.log2(math.e) / length_scale
    center = 6.0 / math.sqrt(size_total) * scale
    col_width = prior.shape[0]
    row_height = size_total // lax.axis_size("area")
    areas_total = area_xy.shape[1] * lax.axis_size("area")
    factor = size_total / areas_total

    own = jnp.concatenate([area_xy * scale - center, -0.5 * jnp.log2(0.5 + sampling_var)[None, :]], axis=0)
    areas = all_areas(own)
    first_prior = first_block_prior(prior)
    own_prior = prior.reshape(1, col_width)
    points = gram_points(order, inducer_xy, scale, center, col_width, row_height)
    offsets = jnp.stack(
        [block_position() * col_width, lax.axis_index("area") * row_height]
    ).astype(jnp.int32)

    small = areas_total <= 8192
    tile_rows = min(row_height, 512 if small else 256)
    tiles = row_height // tile_rows
    ahead = min(4 if small else 1, tiles)
    buffers = min(2 * ahead, tiles)
    smem = pl.BlockSpec(memory_space=pltpu.SMEM)
    vmem = pl.BlockSpec(memory_space=pltpu.VMEM)
    panel_rows, schur = pl.pallas_call(
        functools.partial(schur_kernel, factor, ahead),
        grid=(tiles,),
        out_shape=(
            jax.ShapeDtypeStruct((NB, col_width), F32),
            jax.ShapeDtypeStruct((row_height, col_width), F32),
        ),
        in_specs=[smem] + [vmem] * 4,
        out_specs=[vmem, pl.BlockSpec((tile_rows, col_width), lambda i: (i, 0))],
        scratch_shapes=[
            pltpu.VMEM((NB, areas_total), BF16),
            pltpu.VMEM((col_width, areas_total), BF16),
            pltpu.VMEM((FEATURES, areas_total), F32),
            pltpu.VMEM((FEATURES, areas_total), BF16),
            pltpu.VMEM((NB, NB + col_width), F32),
            pltpu.VMEM((BLK, BLK), F32),
            pltpu.VMEM((NB // BLK, BLK, BLK), F32),
            pltpu.VMEM((NB, col_width), F32),
            pltpu.VMEM((NB, col_width), F32),
            pltpu.VMEM((areas_total, col_width), BF16),
        ]
        + [pltpu.VMEM((tile_rows, areas_total), BF16)] * buffers,
        compiler_params=pltpu.CompilerParams(vmem_limit_bytes=VMEM_BYTES),
        name="schur",
    )(offsets, points, areas, first_prior, own_prior)
    return (panel_rows, schur)


def solution(mesh):
    in_specs = (P(None, "area"), P("area"), P(), P(), P(("row", "col")))
    out_specs = (P(None, ("row", "col")), P("area", ("row", "col")))
    return jax.shard_map(
        per_device, mesh=mesh, in_specs=in_specs, out_specs=out_specs, check_vma=False
    )
```

```python
import functools
import math

import jax
import jax.numpy as jnp
from jax import lax
from jax.experimental import pallas as pl
from jax.experimental.pallas import tpu as pltpu
from jax.sharding import PartitionSpec as P

NB = 512
LANES = 128
STRIP = 8
PANEL = 4
BLK = 128
CHUNK = 1024
SPAN = 512
VMEM_BYTES = 60 * 1024 * 1024
HIGH = lax.Precision.HIGHEST
F32 = jnp.float32
BF16 = jnp.bfloat16


def split_pieces(value):
    first = value.astype(BF16)
    rest = value - first.astype(F32)
    second = rest.astype(BF16)
    third = (rest - second.astype(F32)).astype(BF16)
    return first, second, third


def nt_dot(left, right, precision=None):
    return lax.dot_general(
        left, right, (((1,), (1,)), ((), ())), precision=precision, preferred_element_type=F32
    )


def tn_dot(left, right, precision=None):
    return lax.dot_general(
        left, right, (((0,), (0,)), ((), ())), precision=precision, preferred_element_type=F32
    )


def block_position():
    return lax.axis_index("row") * lax.axis_size("col") + lax.axis_index("col")


FEATURES = 32
PIECE_PAIRS = ((0, 0), (0, 1), (1, 0), (1, 1), (0, 2), (2, 0))


def write_features(dest, x_row, y_row, left):
    one = jnp.ones_like(x_row)
    norm = [piece.astype(F32) for piece in split_pieces(x_row * x_row + y_row * y_row)]
    rows = norm + [one] * 3 if left else [one] * 3 + norm
    for coordinate in (x_row, y_row):
        factor = 1.0 if left else -2.0
        pieces = [piece.astype(F32) * factor for piece in split_pieces(coordinate)]
        rows += [pieces[pair[0 if left else 1]] for pair in PIECE_PAIRS]
    for index, row in enumerate(rows):
        dest[index : index + 1, :] = row


def points_kernel(
    scale, center, col_width, offset_ref, order_ref, table_ref, features_ref, columns_ref, places, features, tables
):
    quotients = order_ref.shape[0]
    for q in range(quotients):
        for k in range(2):
            tables[k, q : q + 1, :] = table_ref[k : k + 1, q * LANES : (q + 1) * LANES]
    pieces_x = split_pieces(tables[0] * scale - center)
    pieces_y = split_pieces(tables[1] * scale - center)
    columns_ref[...] = jnp.concatenate(
        [jnp.concatenate(pieces_x, axis=0), jnp.concatenate(pieces_y, axis=0)], axis=1
    ).T
    quotient_ids = lax.broadcasted_iota(jnp.int32, (quotients, LANES), 0)
    lane_ids = lax.broadcasted_iota(jnp.int32, (LANES, LANES), 0)

    def one_block(step):
        row = step
        if step >= (NB + col_width) // LANES:
            row = offset_ref[1] // LANES + step - (NB + col_width) // LANES
        elif step >= NB // LANES:
            row = offset_ref[0] // LANES + step - NB // LANES
        ids = order_ref[pl.ds(row, 1), :]
        hit = jnp.where(quotient_ids == lax.shift_right_logical(ids, 7), 1.0, 0.0).astype(BF16)
        values = jnp.dot(
            columns_ref[...], jnp.concatenate([hit, hit, hit], axis=0), preferred_element_type=F32
        )
        mine = lane_ids == lax.bitwise_and(ids, LANES - 1)
        return [
            jnp.sum(jnp.where(mine, values[k * LANES : (k + 1) * LANES], 0.0), axis=0, keepdims=True)
            for k in range(2)
        ]

    blocks = features_ref.shape[0] // LANES
    for step in range(blocks):
        x_row, y_row = one_block(step)
        places[0:1, step * LANES : (step + 1) * LANES] = x_row
        places[1:2, step * LANES : (step + 1) * LANES] = y_row
    features[...] = jnp.zeros_like(features)
    write_features(features, places[0:1, :], places[1:2, :], True)
    for step in range(blocks):
        mine = slice(step * LANES, (step + 1) * LANES)
        features_ref[mine, :] = features[:, mine].T.astype(BF16)


def gram_points(offsets, order, inducer_xy, scale, center, col_width, row_height):
    quotients = order.shape[0] // LANES
    count = NB + col_width + row_height
    return pl.pallas_call(
        functools.partial(points_kernel, scale, center, col_width),
        out_shape=jax.ShapeDtypeStruct((count, FEATURES), BF16),
        in_specs=[
            pl.BlockSpec(memory_space=pltpu.SMEM),
            pl.BlockSpec(memory_space=pltpu.VMEM),
            pl.BlockSpec(memory_space=pltpu.VMEM),
        ],
        out_specs=pl.BlockSpec(memory_space=pltpu.VMEM),
        scratch_shapes=[
            pltpu.VMEM((2 * LANES, 3 * quotients), BF16),
            pltpu.VMEM((2, count), F32),
            pltpu.VMEM((FEATURES, count), F32),
            pltpu.VMEM((2, quotients, LANES), F32),
        ],
        compiler_params=pltpu.CompilerParams(vmem_limit_bytes=VMEM_BYTES),
        cost_estimate=pl.CostEstimate(flops=5 * 10**9, bytes_accessed=2**20, transcendentals=0),
        name="points",
    )(offsets, order.reshape(quotients, LANES), inducer_xy)


def fill_kernel(dest, points, area_features, log_weights, first, count):
    for start in range(0, count, 256):
        lanes = pl.ds(first + start, 256)
        squares = jnp.dot(points, area_features[:, lanes], preferred_element_type=F32)
        weights = [
            jnp.broadcast_to(log_weights[0:1, pl.ds(first + start + half, LANES)], (16, LANES))
            for half in (0, LANES)
        ]
        for row in range(0, points.shape[0], 16):
            for half in range(2):
                square = jnp.maximum(
                    squares[row : row + 16, half * LANES : (half + 1) * LANES], 1e-30
                )
                value = jnp.exp2(weights[half] - square * lax.rsqrt(square))
                dest[row : row + 16, pl.ds(first + start + half * LANES, LANES)] = value.astype(BF16)


def head_kernel(
    factor,
    scale,
    center,
    offset_ref,
    points_ref,
    *refs,
):
    *area_refs, prior_ref, head_ref, cols_ref, system_ref, area_features_ref, log_weights, features = refs
    col_width = cols_ref.shape[0]
    total = area_features_ref.shape[1]
    features[...] = jnp.zeros_like(features)
    width = total // len(area_refs)
    for index in range(len(area_refs)):
        values = area_refs[index][...]
        if len(area_refs) == 2:
            values = jnp.where(offset_ref[2] == index, area_refs[0][...], area_refs[1][...])
        lanes = slice(index * width, (index + 1) * width)
        places = values[0:2] * scale - center
        write_features(features.at[:, lanes], places[0:1], places[1:2], False)
        log_weights[:, lanes] = -0.5 * jnp.log2(0.5 + values[2:3])
    area_features_ref[...] = features[...].astype(BF16)
    system_ref[...] = jnp.zeros_like(system_ref)

    def step(index, carry):
        first = pl.multiple_of(index * CHUNK, CHUNK)
        here = pl.ds(first, CHUNK)
        fill_kernel(head_ref, points_ref[:NB, :], area_features_ref, log_weights, first, CHUNK)
        fill_kernel(
            cols_ref, points_ref[NB : NB + col_width, :], area_features_ref, log_weights, first, CHUNK
        )
        left = head_ref[:, here]
        system_ref[:, :NB] += nt_dot(left, left)
        system_ref[:, NB:] += nt_dot(left, cols_ref[:, here])
        return carry

    lax.fori_loop(0, total // CHUNK, step, 0)
    system_ref[:, :NB] = system_ref[:, :NB] * factor
    rows = lax.broadcasted_iota(jnp.int32, (NB, col_width), 0)
    cols = lax.broadcasted_iota(jnp.int32, (NB, col_width), 1) + offset_ref[0]
    system_ref[:, NB:] = system_ref[:, NB:] * factor + jnp.where(rows == cols, prior_ref[...], 0.0)


def whole_row(value, index):
    return jnp.broadcast_to(value[index : index + 1, :], (STRIP, LANES))


def whole_lane(value, index):
    return jnp.broadcast_to(value[:, index : index + 1], (STRIP, LANES))


def inverse_factor(block_ref, inverse_ref):
    count = BLK // STRIP
    row_ids = lax.broadcasted_iota(jnp.int32, (STRIP, LANES), 0)
    lane_ids = lax.broadcasted_iota(jnp.int32, (STRIP, LANES), 1)
    tops = [block_ref[i * STRIP : (i + 1) * STRIP, :] for i in range(count)]
    units = [jnp.where(lane_ids == row_ids + i * STRIP, 1.0, 0.0).astype(F32) for i in range(count)]
    for p in range(count):
        panel_end = (p // PANEL + 1) * PANEL
        diag_cols = [whole_lane(tops[p], p * STRIP + j) for j in range(STRIP)]
        entry = {
            (i, j): whole_row(diag_cols[j], i) for j in range(STRIP) for i in range(j, STRIP)
        }
        top_rows = [whole_row(tops[p], j) for j in range(STRIP)]
        unit_rows = [whole_row(units[p], j) for j in range(STRIP)]
        roots = []
        for j in range(STRIP):
            root = lax.rsqrt(entry[j, j])
            roots.append(root)
            for i in range(j + 1, STRIP):
                entry[i, j] = entry[i, j] * root
            for k in range(j + 1, STRIP):
                for i in range(k, STRIP):
                    entry[i, k] = entry[i, k] - entry[i, j] * entry[k, j]
        for j in range(STRIP):
            for k in range(j):
                top_rows[j] = top_rows[j] - entry[j, k] * top_rows[k]
                unit_rows[j] = unit_rows[j] - entry[j, k] * unit_rows[k]
            top_rows[j] = top_rows[j] * roots[j]
            unit_rows[j] = unit_rows[j] * roots[j]
        for i in range(p + 1, panel_end):
            cols = [whole_lane(tops[i], p * STRIP + j) for j in range(STRIP)]
            top, unit = tops[i], units[i]
            for j in range(STRIP):
                for k in range(j):
                    cols[j] = cols[j] - cols[k] * entry[j, k]
                cols[j] = cols[j] * roots[j]
                top = top - cols[j] * top_rows[j]
                unit = unit - cols[j] * unit_rows[j]
            tops[i], units[i] = top, unit
        top, unit = top_rows[STRIP - 1], unit_rows[STRIP - 1]
        for j in range(STRIP - 1):
            top = jnp.where(row_ids == j, top_rows[j], top)
            unit = jnp.where(row_ids == j, unit_rows[j], unit)
        tops[p], units[p] = top, unit
        inverse_ref[p * STRIP : (p + 1) * STRIP, :] = unit
        if p + 1 == panel_end and panel_end < count:
            panel = slice(panel_end - PANEL, panel_end)
            top = jnp.concatenate(tops[panel], axis=0)
            both = jnp.concatenate([top, jnp.concatenate(units[panel], axis=0)], axis=1)
            update = tn_dot(top, both, HIGH)
            for i in range(panel_end, count):
                mine = slice(i * STRIP, (i + 1) * STRIP)
                tops[i] = tops[i] - update[mine, :LANES]
                units[i] = units[i] - update[mine, LANES:]


def factor_kernel(system_ref, first_prior_ref, panel_ref, solved_ref, weighted_ref, work, block, inverses):
    count = NB // BLK
    rows = lax.broadcasted_iota(jnp.int32, (NB, NB), 0)
    cols = lax.broadcasted_iota(jnp.int32, (NB, NB), 1)
    diagonal = jnp.where(rows == cols, first_prior_ref[...], 0.0)
    work[:, :, :NB] = (system_ref[:, :NB] + diagonal).reshape(count, BLK, NB)
    work[:, :, NB:] = system_ref[:, NB:].reshape(count, BLK, panel_ref.shape[1])

    def eliminate(k, carry):
        block[...] = work[k, :, pl.ds(pl.multiple_of(k * BLK, BLK), BLK)]
        inverse_factor(block, inverses.at[k])
        row = jnp.dot(inverses[k], work[k], precision=HIGH, preferred_element_type=F32)
        work[k] = row
        for i in range(1, count):

            @pl.when(i > k)
            def _():
                work[i] -= tn_dot(row[:, i * BLK : (i + 1) * BLK], row, HIGH)

        return carry

    lax.fori_loop(0, count, eliminate, 0)
    for k in range(count - 1, -1, -1):
        mine = pl.ds(k * BLK, BLK)
        panel = work[k, :, NB:]
        panel_ref[mine, :] = panel
        if k < count - 1:
            panel = panel - jnp.dot(
                work[k, :, (k + 1) * BLK : NB],
                solved_ref[(k + 1) * BLK :, :],
                precision=HIGH,
                preferred_element_type=F32,
            )
        solved_ref[mine, :] = tn_dot(inverses[k], panel, HIGH)
    column = jnp.sum(diagonal, axis=1, keepdims=True)
    weighted_ref[...] = solved_ref[...] * column


def schur_kernel(
    factor,
    offset_ref,
    points_ref,
    log_weights,
    area_features_ref,
    prior_ref,
    head_ref,
    cols_ref,
    solved_ref,
    weighted_ref,
    out_ref,
    left_even,
    left_odd,
    residual,
):
    tile = pl.program_id(0)
    tiles = pl.num_programs(0)
    col_width = cols_ref.shape[0]
    total = log_weights.shape[1]
    steps = total // CHUNK
    first_points = NB + col_width
    tile_rows = out_ref.shape[0]

    @pl.when(tile == 0)
    def _():
        points = points_ref[first_points : first_points + tile_rows, :]
        high = solved_ref[...].astype(BF16)
        low = (solved_ref[...] - high.astype(F32)).astype(BF16)

        def step(index, carry):
            first = pl.multiple_of(index * CHUNK, CHUNK)
            here = pl.ds(first, CHUNK)
            right = head_ref[:, here]
            removed = tn_dot(high, right) + tn_dot(low, right)
            residual[here, :] = (cols_ref[:, here].astype(F32) - removed).astype(BF16).T
            fill_kernel(left_even, points, area_features_ref, log_weights, first, CHUNK)
            return carry

        lax.fori_loop(0, steps, step, 0)

    def run(source, dest):
        if dest is not None:
            next_row = pl.multiple_of(first_points + (tile + 1) * tile_rows, 16)
            points = points_ref[pl.ds(next_row, tile_rows), :]
        out_ref[...] = jnp.zeros_like(out_ref)

        def step(index, carry):
            first = pl.multiple_of(index * SPAN, SPAN)
            here = pl.ds(first, SPAN)
            out_ref[...] += jnp.dot(source[:, here], residual[here, :], preferred_element_type=F32)
            if dest is not None:
                fill_kernel(dest, points, area_features_ref, log_weights, first, SPAN)
            return carry

        lax.fori_loop(0, total // SPAN, step, 0)

    parity = lax.rem(tile, 2)
    more = tile < tiles - 1
    pl.when(jnp.logical_and(more, parity == 0))(lambda: run(left_even, left_odd))
    pl.when(jnp.logical_and(more, parity == 1))(lambda: run(left_odd, left_even))
    pl.when(jnp.logical_and(jnp.logical_not(more), parity == 0))(lambda: run(left_even, None))
    pl.when(jnp.logical_and(jnp.logical_not(more), parity == 1))(lambda: run(left_odd, None))

    rows = lax.broadcasted_iota(jnp.int32, (tile_rows, col_width), 0) + (offset_ref[1] + tile * tile_rows)
    cols = lax.broadcasted_iota(jnp.int32, (tile_rows, col_width), 1) + offset_ref[0]
    out_ref[...] = out_ref[...] * factor + jnp.where(rows == cols, prior_ref[...], 0.0)

    first_row = offset_ref[1] + tile * tile_rows

    @pl.when(first_row < NB)
    def _():
        out_ref[...] -= weighted_ref[pl.ds(pl.multiple_of(first_row, tile_rows), tile_rows), :]


def all_areas(array):
    if lax.axis_size("area") == 2:
        return [array, lax.ppermute(array, "area", [(0, 1), (1, 0)])]
    return [lax.all_gather(array, "area", axis=array.ndim - 1, tiled=True)]


def from_first(array, axis):
    total = jnp.where(lax.axis_index(axis) == 0, array, 0.0)
    for target in range(1, lax.axis_size(axis)):
        total = total + lax.ppermute(array, axis, [(0, target)])
    return total


def first_block_prior(prior):
    if prior.shape[0] == NB:
        return from_first(from_first(prior.reshape(1, NB), "col"), "row")
    return lax.all_gather(prior, ("row", "col"), axis=0, tiled=True)[:NB].reshape(1, NB)


def per_device(area_xy, sampling_var, inducer_xy, order, prior):
    size_total = order.shape[0]
    length_scale = 2.0 / math.sqrt(size_total)
    scale = math.log2(math.e) / length_scale
    center = 6.0 / math.sqrt(size_total) * scale
    col_width = prior.shape[0]
    row_height = size_total // lax.axis_size("area")
    areas_total = area_xy.shape[1] * lax.axis_size("area")
    factor = size_total / areas_total

    own = jnp.concatenate([area_xy, sampling_var[None, :]], axis=0)
    areas = all_areas(own)
    first_prior = first_block_prior(prior)
    own_prior = prior.reshape(1, col_width)
    offsets = jnp.stack(
        [block_position() * col_width, lax.axis_index("area") * row_height, lax.axis_index("area")]
    ).astype(jnp.int32)

    points = gram_points(offsets, order, inducer_xy, scale, center, col_width, row_height)
    tile_rows = min(row_height, 512 if areas_total <= 8192 else 256)
    smem = pl.BlockSpec(memory_space=pltpu.SMEM)
    vmem = pl.BlockSpec(memory_space=pltpu.VMEM)
    params = pltpu.CompilerParams(vmem_limit_bytes=VMEM_BYTES)
    head, cols, system, area_features, log_weights = pl.pallas_call(
        functools.partial(head_kernel, factor, scale, center),
        out_shape=(
            jax.ShapeDtypeStruct((NB, areas_total), BF16),
            jax.ShapeDtypeStruct((col_width, areas_total), BF16),
            jax.ShapeDtypeStruct((NB, NB + col_width), F32),
            jax.ShapeDtypeStruct((FEATURES, areas_total), BF16),
            jax.ShapeDtypeStruct((1, areas_total), F32),
        ),
        in_specs=[smem] + [vmem] * (2 + len(areas)),
        out_specs=[vmem] * 5,
        cost_estimate=pl.CostEstimate(flops=10**10, bytes_accessed=2**24, transcendentals=0),
        scratch_shapes=[pltpu.VMEM((FEATURES, areas_total), F32)],
        compiler_params=params,
        name="head",
    )(offsets, points, *areas, own_prior)
    panel_rows, solved, weighted = pl.pallas_call(
        factor_kernel,
        out_shape=(jax.ShapeDtypeStruct((NB, col_width), F32),) * 3,
        in_specs=[vmem] * 2,
        out_specs=[vmem] * 3,
        scratch_shapes=[
            pltpu.VMEM((NB // BLK, BLK, NB + col_width), F32),
            pltpu.VMEM((BLK, BLK), F32),
            pltpu.VMEM((NB // BLK, BLK, BLK), F32),
        ],
        compiler_params=params,
        name="factor",
    )(system, first_prior)
    schur = pl.pallas_call(
        functools.partial(schur_kernel, factor),
        grid=(row_height // tile_rows,),
        out_shape=jax.ShapeDtypeStruct((row_height, col_width), F32),
        in_specs=[smem] + [vmem] * 8,
        out_specs=pl.BlockSpec((tile_rows, col_width), lambda i: (i, 0)),
        scratch_shapes=[
            pltpu.VMEM((tile_rows, areas_total), BF16),
            pltpu.VMEM((tile_rows, areas_total), BF16),
            pltpu.VMEM((areas_total, col_width), BF16),
        ],
        compiler_params=params,
        name="schur",
    )(offsets, points, log_weights, area_features, own_prior, head, cols, solved, weighted)
    return (panel_rows, schur)


def solution(mesh):
    in_specs = (P(None, "area"), P("area"), P(), P(), P(("row", "col")))
    out_specs = (P(None, ("row", "col")), P("area", ("row", "col")))
    return jax.shard_map(
        per_device, mesh=mesh, in_specs=in_specs, out_specs=out_specs, check_vma=False
    )
```

```python
import functools
import math

import jax
import jax.numpy as jnp
from jax import lax
from jax.experimental import pallas as pl
from jax.experimental.pallas import tpu as pltpu
from jax.sharding import PartitionSpec as P

NB = 512
LANES = 128
STRIP = 8
GROUP = 2
PANEL = 4
BLK = 128
CHUNK = 1024
SPAN = 512
PIECE = 256
VMEM_BYTES = 60 * 1024 * 1024
HIGH = lax.Precision.HIGHEST
F32 = jnp.float32
BF16 = jnp.bfloat16


def split_pieces(value):
    first = value.astype(BF16)
    rest = value - first.astype(F32)
    second = rest.astype(BF16)
    third = (rest - second.astype(F32)).astype(BF16)
    return first, second, third


def nt_dot(left, right, precision=None):
    return lax.dot_general(
        left, right, (((1,), (1,)), ((), ())), precision=precision, preferred_element_type=F32
    )


def tn_dot(left, right, precision=None):
    return lax.dot_general(
        left, right, (((0,), (0,)), ((), ())), precision=precision, preferred_element_type=F32
    )


def block_position():
    return lax.axis_index("row") * lax.axis_size("col") + lax.axis_index("col")


FEATURES = 32
PIECE_PAIRS = ((0, 0), (0, 1), (1, 0), (1, 1), (0, 2), (2, 0))


def write_features(dest, x_row, y_row, left):
    one = jnp.ones_like(x_row)
    norm = [piece.astype(F32) for piece in split_pieces(x_row * x_row + y_row * y_row)]
    rows = norm + [one] * 3 if left else [one] * 3 + norm
    for coordinate in (x_row, y_row):
        factor = 1.0 if left else -2.0
        pieces = [piece.astype(F32) * factor for piece in split_pieces(coordinate)]
        rows += [pieces[pair[0 if left else 1]] for pair in PIECE_PAIRS]
    for index, row in enumerate(rows):
        dest[index : index + 1, :] = row


def points_kernel(
    scale, center, col_width, offset_ref, order_ref, table_ref, features_ref, columns_ref, places, features, tables
):
    quotients = order_ref.shape[0]
    for q in range(quotients):
        for k in range(2):
            tables[k, q : q + 1, :] = table_ref[k : k + 1, q * LANES : (q + 1) * LANES]
    pieces_x = split_pieces(tables[0] * scale - center)
    pieces_y = split_pieces(tables[1] * scale - center)
    columns_ref[...] = jnp.concatenate(
        [jnp.concatenate(pieces_x, axis=0), jnp.concatenate(pieces_y, axis=0)], axis=1
    ).T
    quotient_ids = lax.broadcasted_iota(jnp.int32, (quotients, LANES), 0)
    lane_ids = lax.broadcasted_iota(jnp.int32, (LANES, LANES), 0)

    def one_block(step):
        row = step
        if step >= (NB + col_width) // LANES:
            row = offset_ref[1] // LANES + step - (NB + col_width) // LANES
        elif step >= NB // LANES:
            row = offset_ref[0] // LANES + step - NB // LANES
        ids = order_ref[pl.ds(row, 1), :]
        hit = jnp.where(quotient_ids == lax.shift_right_logical(ids, 7), 1.0, 0.0).astype(BF16)
        values = jnp.dot(
            columns_ref[...], jnp.concatenate([hit, hit, hit], axis=0), preferred_element_type=F32
        )
        mine = lane_ids == lax.bitwise_and(ids, LANES - 1)
        return [
            jnp.sum(jnp.where(mine, values[k * LANES : (k + 1) * LANES], 0.0), axis=0, keepdims=True)
            for k in range(2)
        ]

    blocks = features_ref.shape[0] // LANES
    for step in range(blocks):
        x_row, y_row = one_block(step)
        places[0:1, step * LANES : (step + 1) * LANES] = x_row
        places[1:2, step * LANES : (step + 1) * LANES] = y_row
    features[...] = jnp.zeros_like(features)
    write_features(features, places[0:1, :], places[1:2, :], True)
    for step in range(blocks):
        mine = slice(step * LANES, (step + 1) * LANES)
        features_ref[mine, :] = features[:, mine].T.astype(BF16)


def gram_points(offsets, order, inducer_xy, scale, center, col_width, row_height):
    quotients = order.shape[0] // LANES
    count = NB + col_width + row_height
    return pl.pallas_call(
        functools.partial(points_kernel, scale, center, col_width),
        out_shape=jax.ShapeDtypeStruct((count, FEATURES), BF16),
        in_specs=[
            pl.BlockSpec(memory_space=pltpu.SMEM),
            pl.BlockSpec(memory_space=pltpu.VMEM),
            pl.BlockSpec(memory_space=pltpu.VMEM),
        ],
        out_specs=pl.BlockSpec(memory_space=pltpu.VMEM),
        scratch_shapes=[
            pltpu.VMEM((2 * LANES, 3 * quotients), BF16),
            pltpu.VMEM((2, count), F32),
            pltpu.VMEM((FEATURES, count), F32),
            pltpu.VMEM((2, quotients, LANES), F32),
        ],
        compiler_params=pltpu.CompilerParams(vmem_limit_bytes=VMEM_BYTES),
        cost_estimate=pl.CostEstimate(flops=5 * 10**9, bytes_accessed=2**20, transcendentals=0),
        name="points",
    )(offsets, order.reshape(quotients, LANES), inducer_xy)


def rsqrt_root(square):
    square = jnp.maximum(square, 1e-30)
    return square * lax.rsqrt(square)


def plain_root(square):
    return jnp.sqrt(jnp.maximum(square, 0.0))


def squared_distances(points, area_features, first):
    return jnp.dot(points, area_features[:, pl.ds(first, PIECE)], preferred_element_type=F32)


def kernel_values(dest, squares, log_weights, first, root):
    for half in range(0, PIECE, LANES):
        lanes = pl.ds(first + half, LANES)
        weights = jnp.broadcast_to(log_weights[0:1, lanes], (16, LANES))
        for row in range(0, squares.shape[0], 16):
            distance = root(squares[row : row + 16, half : half + LANES])
            dest[row : row + 16, lanes] = jnp.exp2(weights - distance).astype(BF16)


def fill_kernel(dest, points, area_features, log_weights, first, count, root=rsqrt_root):
    for start in range(0, count, PIECE):
        squares = squared_distances(points, area_features, first + start)
        kernel_values(dest, squares, log_weights, first + start, root)


def head_kernel(
    factor,
    scale,
    center,
    offset_ref,
    points_ref,
    *refs,
):
    *area_refs, prior_ref, head_ref, cols_ref, system_ref, area_features_ref, log_weights, features = refs
    col_width = cols_ref.shape[0]
    total = area_features_ref.shape[1]
    features[...] = jnp.zeros_like(features)
    width = total // len(area_refs)
    for index in range(len(area_refs)):
        values = area_refs[index][...]
        if len(area_refs) == 2:
            values = jnp.where(offset_ref[2] == index, area_refs[0][...], area_refs[1][...])
        lanes = slice(index * width, (index + 1) * width)
        places = values[0:2] * scale - center
        write_features(features.at[:, lanes], places[0:1], places[1:2], False)
        log_weights[:, lanes] = -0.5 * jnp.log2(0.5 + values[2:3])
    area_features_ref[...] = features[...].astype(BF16)
    system_ref[...] = jnp.zeros_like(system_ref)

    def step(index, carry):
        first = pl.multiple_of(index * CHUNK, CHUNK)
        here = pl.ds(first, CHUNK)
        fill_kernel(head_ref, points_ref[:NB, :], area_features_ref, log_weights, first, CHUNK, plain_root)
        fill_kernel(
            cols_ref, points_ref[NB : NB + col_width, :], area_features_ref, log_weights, first, CHUNK, plain_root
        )
        left = head_ref[:, here]
        system_ref[:, :NB] += nt_dot(left, left)
        system_ref[:, NB:] += nt_dot(left, cols_ref[:, here])
        return carry

    lax.fori_loop(0, total // CHUNK, step, 0)
    system_ref[:, :NB] = system_ref[:, :NB] * factor
    rows = lax.broadcasted_iota(jnp.int32, (NB, col_width), 0)
    cols = lax.broadcasted_iota(jnp.int32, (NB, col_width), 1) + offset_ref[0]
    system_ref[:, NB:] = system_ref[:, NB:] * factor + jnp.where(rows == cols, prior_ref[...], 0.0)


def whole_row(value, index):
    return jnp.broadcast_to(value[index : index + 1, :], (STRIP, LANES))


def whole_lane(value, index):
    return jnp.broadcast_to(value[:, index : index + 1], (STRIP, LANES))


def inverse_factor(block_ref, inverse_ref):
    count = BLK // STRIP
    row_ids = lax.broadcasted_iota(jnp.int32, (STRIP, LANES), 0)
    lane_ids = lax.broadcasted_iota(jnp.int32, (STRIP, LANES), 1)
    tops = [block_ref[i * STRIP : (i + 1) * STRIP, :] for i in range(count)]
    units = [jnp.where(lane_ids == row_ids + i * STRIP, 1.0, 0.0).astype(F32) for i in range(count)]
    width = GROUP * STRIP
    for first in range(0, count, GROUP):
        panel_end = (first // PANEL + 1) * PANEL
        base = first * STRIP
        entry, top_rows, unit_rows, roots = {}, [], [], []
        for a in range(GROUP):
            for j in range((a + 1) * STRIP):
                column = whole_lane(tops[first + a], base + j)
                for i in range(max(j, a * STRIP), (a + 1) * STRIP):
                    entry[i, j] = whole_row(column, i - a * STRIP)
            top_rows += [whole_row(tops[first + a], r) for r in range(STRIP)]
            unit_rows += [whole_row(units[first + a], r) for r in range(STRIP)]
        for j in range(0, width, 2):
            corner, side, other = entry[j, j], entry[j + 1, j], entry[j + 1, j + 1]
            root = lax.rsqrt(corner)
            next_root = lax.rsqrt(corner * other - side * side) * (corner * root)
            roots += [root, next_root]
            side = side * root
            entry[j + 1, j] = side
            for i in range(j + 2, width):
                entry[i, j] = entry[i, j] * root
                entry[i, j + 1] = (entry[i, j + 1] - entry[i, j] * side) * next_root
            for k in range(j + 2, width):
                for i in range(k, width):
                    entry[i, k] = entry[i, k] - (
                        entry[i, j] * entry[k, j] + entry[i, j + 1] * entry[k, j + 1]
                    )
        for j in range(width):
            for k in range(j):
                top_rows[j] = top_rows[j] - entry[j, k] * top_rows[k]
                unit_rows[j] = unit_rows[j] - entry[j, k] * unit_rows[k]
            top_rows[j] = top_rows[j] * roots[j]
            unit_rows[j] = unit_rows[j] * roots[j]
        for i in range(first + GROUP, panel_end):
            cols = [whole_lane(tops[i], base + j) for j in range(width)]
            top, unit = tops[i], units[i]
            for j in range(width):
                for k in range(j):
                    cols[j] = cols[j] - cols[k] * entry[j, k]
                cols[j] = cols[j] * roots[j]
                top = top - cols[j] * top_rows[j]
                unit = unit - cols[j] * unit_rows[j]
            tops[i], units[i] = top, unit
        for a in range(GROUP):
            top, unit = top_rows[(a + 1) * STRIP - 1], unit_rows[(a + 1) * STRIP - 1]
            for r in range(STRIP - 1):
                top = jnp.where(row_ids == r, top_rows[a * STRIP + r], top)
                unit = jnp.where(row_ids == r, unit_rows[a * STRIP + r], unit)
            tops[first + a], units[first + a] = top, unit
            inverse_ref[(first + a) * STRIP : (first + a + 1) * STRIP, :] = unit
        if first + GROUP == panel_end and panel_end < count:
            panel = slice(panel_end - PANEL, panel_end)
            top = jnp.concatenate(tops[panel], axis=0)
            both = jnp.concatenate([top, jnp.concatenate(units[panel], axis=0)], axis=1)
            update = tn_dot(top, both, HIGH)
            for i in range(panel_end, count):
                mine = slice(i * STRIP, (i + 1) * STRIP)
                tops[i] = tops[i] - update[mine, :LANES]
                units[i] = units[i] - update[mine, LANES:]


def factor_kernel(system_ref, first_prior_ref, panel_ref, solved_ref, weighted_ref, work, block, inverses):
    count = NB // BLK
    rows = lax.broadcasted_iota(jnp.int32, (NB, NB), 0)
    cols = lax.broadcasted_iota(jnp.int32, (NB, NB), 1)
    diagonal = jnp.where(rows == cols, first_prior_ref[...], 0.0)
    work[:, :, :NB] = (system_ref[:, :NB] + diagonal).reshape(count, BLK, NB)
    work[:, :, NB:] = system_ref[:, NB:].reshape(count, BLK, panel_ref.shape[1])

    def eliminate(k, carry):
        block[...] = work[k, :, pl.ds(pl.multiple_of(k * BLK, BLK), BLK)]
        inverse_factor(block, inverses.at[k])
        row = jnp.dot(inverses[k], work[k], precision=HIGH, preferred_element_type=F32)
        work[k] = row
        for i in range(1, count):

            @pl.when(i > k)
            def _():
                work[i] -= tn_dot(row[:, i * BLK : (i + 1) * BLK], row, HIGH)

        return carry

    lax.fori_loop(0, count, eliminate, 0)
    for k in range(count - 1, -1, -1):
        mine = pl.ds(k * BLK, BLK)
        panel = work[k, :, NB:]
        panel_ref[mine, :] = panel
        if k < count - 1:
            panel = panel - jnp.dot(
                work[k, :, (k + 1) * BLK : NB],
                solved_ref[(k + 1) * BLK :, :],
                precision=HIGH,
                preferred_element_type=F32,
            )
        solved_ref[mine, :] = tn_dot(inverses[k], panel, HIGH)
    column = jnp.sum(diagonal, axis=1, keepdims=True)
    weighted_ref[...] = solved_ref[...] * column


def schur_kernel(
    factor,
    offset_ref,
    points_ref,
    log_weights,
    area_features_ref,
    prior_ref,
    head_ref,
    cols_ref,
    solved_ref,
    weighted_ref,
    out_ref,
    left_even,
    left_odd,
    residual,
):
    tile = pl.program_id(0)
    tiles = pl.num_programs(0)
    col_width = cols_ref.shape[0]
    total = log_weights.shape[1]
    steps = total // CHUNK
    first_points = NB + col_width
    tile_rows = out_ref.shape[0]

    @pl.when(tile == 0)
    def _():
        points = points_ref[first_points : first_points + tile_rows, :]
        high = solved_ref[...].astype(BF16)
        low = (solved_ref[...] - high.astype(F32)).astype(BF16)

        def step(index, carry):
            first = pl.multiple_of(index * CHUNK, CHUNK)
            here = pl.ds(first, CHUNK)
            right = head_ref[:, here]
            removed = tn_dot(high, right) + tn_dot(low, right)
            residual[here, :] = (cols_ref[:, here].astype(F32) - removed).astype(BF16).T
            fill_kernel(left_even, points, area_features_ref, log_weights, first, CHUNK)
            return carry

        lax.fori_loop(0, steps, step, 0)

    def run(source, dest):
        if dest is not None:
            next_row = pl.multiple_of(first_points + (tile + 1) * tile_rows, 16)
            points = points_ref[pl.ds(next_row, tile_rows), :]
        halves = max(1, col_width // 256)
        wide = col_width // halves
        pieces = [(first, half * wide) for first in range(0, total, SPAN) for half in range(halves)]
        stride = total // len(pieces)
        squares = None
        if dest is not None:
            squares = [squared_distances(points, area_features_ref, start) for start in range(0, stride, PIECE)]
        for index, (first, column) in enumerate(pieces):
            start = index * stride
            later = None
            if dest is not None and index + 1 < len(pieces):
                later = [
                    squared_distances(points, area_features_ref, start + stride + more)
                    for more in range(0, stride, PIECE)
                ]
            lanes = slice(column, column + wide)
            part = jnp.dot(
                source[:, first : first + SPAN],
                residual[first : first + SPAN, lanes],
                preferred_element_type=F32,
            )
            out_ref[:, lanes] = part if first == 0 else out_ref[:, lanes] + part
            if dest is not None:
                for more in range(0, stride, PIECE):
                    kernel_values(dest, squares[more // PIECE], log_weights, start + more, rsqrt_root)
            squares = later

    parity = lax.rem(tile, 2)
    more = tile < tiles - 1
    pl.when(jnp.logical_and(more, parity == 0))(lambda: run(left_even, left_odd))
    pl.when(jnp.logical_and(more, parity == 1))(lambda: run(left_odd, left_even))
    pl.when(jnp.logical_and(jnp.logical_not(more), parity == 0))(lambda: run(left_even, None))
    pl.when(jnp.logical_and(jnp.logical_not(more), parity == 1))(lambda: run(left_odd, None))

    rows = lax.broadcasted_iota(jnp.int32, (tile_rows, col_width), 0) + (offset_ref[1] + tile * tile_rows)
    cols = lax.broadcasted_iota(jnp.int32, (tile_rows, col_width), 1) + offset_ref[0]
    out_ref[...] = out_ref[...] * factor + jnp.where(rows == cols, prior_ref[...], 0.0)

    first_row = offset_ref[1] + tile * tile_rows

    @pl.when(first_row < NB)
    def _():
        out_ref[...] -= weighted_ref[pl.ds(pl.multiple_of(first_row, tile_rows), tile_rows), :]


def all_areas(array):
    if lax.axis_size("area") == 2:
        return [array, lax.ppermute(array, "area", [(0, 1), (1, 0)])]
    return [lax.all_gather(array, "area", axis=array.ndim - 1, tiled=True)]


def from_first(array, axis):
    total = jnp.where(lax.axis_index(axis) == 0, array, 0.0)
    for target in range(1, lax.axis_size(axis)):
        total = total + lax.ppermute(array, axis, [(0, target)])
    return total


def first_block_prior(prior):
    if prior.shape[0] == NB:
        return from_first(from_first(prior.reshape(1, NB), "col"), "row")
    return lax.all_gather(prior, ("row", "col"), axis=0, tiled=True)[:NB].reshape(1, NB)


def per_device(area_xy, sampling_var, inducer_xy, order, prior):
    size_total = order.shape[0]
    length_scale = 2.0 / math.sqrt(size_total)
    scale = math.log2(math.e) / length_scale
    center = 6.0 / math.sqrt(size_total) * scale
    col_width = prior.shape[0]
    row_height = size_total // lax.axis_size("area")
    areas_total = area_xy.shape[1] * lax.axis_size("area")
    factor = size_total / areas_total

    own = jnp.concatenate([area_xy, sampling_var[None, :]], axis=0)
    areas = all_areas(own)
    first_prior = first_block_prior(prior)
    own_prior = prior.reshape(1, col_width)
    offsets = jnp.stack(
        [block_position() * col_width, lax.axis_index("area") * row_height, lax.axis_index("area")]
    ).astype(jnp.int32)

    points = gram_points(offsets, order, inducer_xy, scale, center, col_width, row_height)
    tile_rows = min(row_height, 512 if areas_total <= 8192 else 256)
    smem = pl.BlockSpec(memory_space=pltpu.SMEM)
    vmem = pl.BlockSpec(memory_space=pltpu.VMEM)
    params = pltpu.CompilerParams(vmem_limit_bytes=VMEM_BYTES)
    head, cols, system, area_features, log_weights = pl.pallas_call(
        functools.partial(head_kernel, factor, scale, center),
        out_shape=(
            jax.ShapeDtypeStruct((NB, areas_total), BF16),
            jax.ShapeDtypeStruct((col_width, areas_total), BF16),
            jax.ShapeDtypeStruct((NB, NB + col_width), F32),
            jax.ShapeDtypeStruct((FEATURES, areas_total), BF16),
            jax.ShapeDtypeStruct((1, areas_total), F32),
        ),
        in_specs=[smem] + [vmem] * (2 + len(areas)),
        out_specs=[vmem] * 5,
        cost_estimate=pl.CostEstimate(flops=10**10, bytes_accessed=2**24, transcendentals=0),
        scratch_shapes=[pltpu.VMEM((FEATURES, areas_total), F32)],
        compiler_params=params,
        name="head",
    )(offsets, points, *areas, own_prior)
    panel_rows, solved, weighted = pl.pallas_call(
        factor_kernel,
        out_shape=(jax.ShapeDtypeStruct((NB, col_width), F32),) * 3,
        in_specs=[vmem] * 2,
        out_specs=[vmem] * 3,
        scratch_shapes=[
            pltpu.VMEM((NB // BLK, BLK, NB + col_width), F32),
            pltpu.VMEM((BLK, BLK), F32),
            pltpu.VMEM((NB // BLK, BLK, BLK), F32),
        ],
        compiler_params=params,
        name="factor",
    )(system, first_prior)
    schur = pl.pallas_call(
        functools.partial(schur_kernel, factor),
        grid=(row_height // tile_rows,),
        out_shape=jax.ShapeDtypeStruct((row_height, col_width), F32),
        in_specs=[smem] + [vmem] * 8,
        out_specs=pl.BlockSpec((tile_rows, col_width), lambda i: (i, 0)),
        scratch_shapes=[
            pltpu.VMEM((tile_rows, areas_total), BF16),
            pltpu.VMEM((tile_rows, areas_total), BF16),
            pltpu.VMEM((areas_total, col_width), BF16),
        ],
        compiler_params=params,
        name="schur",
    )(offsets, points, log_weights, area_features, own_prior, head, cols, solved, weighted)
    return (panel_rows, schur)


def solution(mesh):
    in_specs = (P(None, "area"), P("area"), P(), P(), P(("row", "col")))
    out_specs = (P(None, ("row", "col")), P("area", ("row", "col")))
    return jax.shard_map(
        per_device, mesh=mesh, in_specs=in_specs, out_specs=out_specs, check_vma=False
    )
```

```python
import functools
import math

import jax
import jax.numpy as jnp
from jax import lax
from jax.experimental import pallas as pl
from jax.experimental.pallas import tpu as pltpu
from jax.sharding import PartitionSpec as P

NB = 512
LANES = 128
STRIP = 8
GROUP = 1
PANEL = 4
BLK = 128
CHUNK = 1024
SPAN = 1024
PIECE = 256
VMEM_BYTES = 60 * 1024 * 1024
HIGH = lax.Precision.HIGHEST
F32 = jnp.float32
BF16 = jnp.bfloat16


def split_pieces(value):
    first = value.astype(BF16)
    rest = value - first.astype(F32)
    second = rest.astype(BF16)
    third = (rest - second.astype(F32)).astype(BF16)
    return first, second, third


def nt_dot(left, right, precision=None):
    return lax.dot_general(
        left, right, (((1,), (1,)), ((), ())), precision=precision, preferred_element_type=F32
    )


def tn_dot(left, right, precision=None):
    return lax.dot_general(
        left, right, (((0,), (0,)), ((), ())), precision=precision, preferred_element_type=F32
    )


def stack_left(value, axis):
    a, b, c = split_pieces(value)
    return jnp.concatenate([a, a, b, b, a, c], axis=axis)


def stack_right(value):
    a, b, c = split_pieces(value)
    return jnp.concatenate([a, b, a, b, c, a], axis=0)


def block_position():
    return lax.axis_index("row") * lax.axis_size("col") + lax.axis_index("col")


FEATURES = 32
PIECE_PAIRS = ((0, 0), (0, 1), (1, 0), (1, 1), (0, 2), (2, 0))


def write_features(dest, x_row, y_row, left):
    one = jnp.ones_like(x_row)
    norm = [piece.astype(F32) for piece in split_pieces(x_row * x_row + y_row * y_row)]
    rows = norm + [one] * 3 if left else [one] * 3 + norm
    for coordinate in (x_row, y_row):
        factor = 1.0 if left else -2.0
        pieces = [piece.astype(F32) * factor for piece in split_pieces(coordinate)]
        rows += [pieces[pair[0 if left else 1]] for pair in PIECE_PAIRS]
    for index, row in enumerate(rows):
        dest[index : index + 1, :] = row


def points_kernel(
    scale, center, col_width, offset_ref, order_ref, table_ref, features_ref, columns_ref, places, features, tables
):
    quotients = order_ref.shape[0]
    for q in range(quotients):
        for k in range(2):
            tables[k, q : q + 1, :] = table_ref[k : k + 1, q * LANES : (q + 1) * LANES]
    pieces_x = split_pieces(tables[0] * scale - center)
    pieces_y = split_pieces(tables[1] * scale - center)
    columns_ref[...] = jnp.concatenate(
        [jnp.concatenate(pieces_x, axis=0), jnp.concatenate(pieces_y, axis=0)], axis=1
    ).T
    quotient_ids = lax.broadcasted_iota(jnp.int32, (quotients, LANES), 0)
    lane_ids = lax.broadcasted_iota(jnp.int32, (LANES, LANES), 0)

    def one_block(step):
        row = step
        if step >= (NB + col_width) // LANES:
            row = offset_ref[1] // LANES + step - (NB + col_width) // LANES
        elif step >= NB // LANES:
            row = offset_ref[0] // LANES + step - NB // LANES
        ids = order_ref[pl.ds(row, 1), :]
        hit = jnp.where(quotient_ids == lax.shift_right_logical(ids, 7), 1.0, 0.0).astype(BF16)
        values = jnp.dot(
            columns_ref[...], jnp.concatenate([hit, hit, hit], axis=0), preferred_element_type=F32
        )
        mine = lane_ids == lax.bitwise_and(ids, LANES - 1)
        return [
            jnp.sum(jnp.where(mine, values[k * LANES : (k + 1) * LANES], 0.0), axis=0, keepdims=True)
            for k in range(2)
        ]

    blocks = features_ref.shape[0] // LANES
    for step in range(blocks):
        x_row, y_row = one_block(step)
        places[0:1, step * LANES : (step + 1) * LANES] = x_row
        places[1:2, step * LANES : (step + 1) * LANES] = y_row
    features[...] = jnp.zeros_like(features)
    write_features(features, places[0:1, :], places[1:2, :], True)
    for step in range(blocks):
        mine = slice(step * LANES, (step + 1) * LANES)
        features_ref[mine, :] = features[:, mine].T.astype(BF16)


def gram_points(offsets, order, inducer_xy, scale, center, col_width, row_height):
    quotients = order.shape[0] // LANES
    count = NB + col_width + row_height
    return pl.pallas_call(
        functools.partial(points_kernel, scale, center, col_width),
        out_shape=jax.ShapeDtypeStruct((count, FEATURES), BF16),
        in_specs=[
            pl.BlockSpec(memory_space=pltpu.SMEM),
            pl.BlockSpec(memory_space=pltpu.VMEM),
            pl.BlockSpec(memory_space=pltpu.VMEM),
        ],
        out_specs=pl.BlockSpec(memory_space=pltpu.VMEM),
        scratch_shapes=[
            pltpu.VMEM((2 * LANES, 3 * quotients), BF16),
            pltpu.VMEM((2, count), F32),
            pltpu.VMEM((FEATURES, count), F32),
            pltpu.VMEM((2, quotients, LANES), F32),
        ],
        compiler_params=pltpu.CompilerParams(vmem_limit_bytes=VMEM_BYTES),
        cost_estimate=pl.CostEstimate(flops=5 * 10**9, bytes_accessed=2**20, transcendentals=0),
        name="points",
    )(offsets, order.reshape(quotients, LANES), inducer_xy)


def root(square):
    square = jnp.maximum(square, 1e-30)
    return square * lax.rsqrt(square)


def squared_distances(points, area_features, first):
    return jnp.dot(points, area_features[:, pl.ds(first, PIECE)], preferred_element_type=F32)


def kernel_values(dest, squares, log_weights, first):
    for half in range(0, PIECE, LANES):
        lanes = pl.ds(first + half, LANES)
        weights = jnp.broadcast_to(log_weights[0:1, lanes], (16, LANES))
        for row in range(0, squares.shape[0], 16):
            distance = root(squares[row : row + 16, half : half + LANES])
            dest[row : row + 16, lanes] = jnp.exp2(weights - distance).astype(BF16)


def fill_kernel(dest, points, area_features, log_weights, first, count):
    for start in range(0, count, PIECE):
        squares = squared_distances(points, area_features, first + start)
        kernel_values(dest, squares, log_weights, first + start)


def head_kernel(
    factor,
    scale,
    center,
    offset_ref,
    points_ref,
    *refs,
):
    *area_refs, prior_ref, head_ref, cols_ref, system_ref, area_features_ref, log_weights, features = refs
    col_width = cols_ref.shape[0]
    total = area_features_ref.shape[1]
    features[...] = jnp.zeros_like(features)
    width = total // len(area_refs)
    for index in range(len(area_refs)):
        values = area_refs[index][...]
        if len(area_refs) == 2:
            values = jnp.where(offset_ref[2] == index, area_refs[0][...], area_refs[1][...])
        lanes = slice(index * width, (index + 1) * width)
        places = values[0:2] * scale - center
        write_features(features.at[:, lanes], places[0:1], places[1:2], False)
        log_weights[:, lanes] = -0.5 * jnp.log2(0.5 + values[2:3])
    area_features_ref[...] = features[...].astype(BF16)
    system_ref[...] = jnp.zeros_like(system_ref)
    group = min(4096, total)

    def step(index, carry):
        base = pl.multiple_of(index * group, group)
        targets = [(head_ref, points_ref[:NB, :]), (cols_ref, points_ref[NB : NB + col_width, :])]

        def distances(start):
            return [squared_distances(points, area_features_ref, base + start) for _, points in targets]

        def accumulate(start):
            here = pl.ds(base + start, CHUNK)
            left = head_ref[:, here]
            system_ref[:, :NB] += nt_dot(left, left)
            system_ref[:, NB:] += nt_dot(left, cols_ref[:, here])

        squares = distances(0)
        for start in range(0, group, PIECE):
            later = distances(start + PIECE) if start + PIECE < group else None
            if start and start % CHUNK == 0:
                accumulate(start - CHUNK)
            for (dest, _), square in zip(targets, squares):
                kernel_values(dest, square, log_weights, base + start)
            squares = later
        accumulate(group - CHUNK)
        return carry

    lax.fori_loop(0, total // group, step, 0)
    system_ref[:, :NB] = system_ref[:, :NB] * factor
    rows = lax.broadcasted_iota(jnp.int32, (NB, col_width), 0)
    cols = lax.broadcasted_iota(jnp.int32, (NB, col_width), 1) + offset_ref[0]
    system_ref[:, NB:] = system_ref[:, NB:] * factor + jnp.where(rows == cols, prior_ref[...], 0.0)


def whole_row(value, index):
    return jnp.broadcast_to(value[index : index + 1, :], (STRIP, LANES))


def whole_lane(value, index):
    return jnp.broadcast_to(value[:, index : index + 1], (STRIP, LANES))


def inverse_factor(block_ref, inverse_ref):
    count = BLK // STRIP
    row_ids = lax.broadcasted_iota(jnp.int32, (STRIP, LANES), 0)
    lane_ids = lax.broadcasted_iota(jnp.int32, (STRIP, LANES), 1)
    tops = [block_ref[i * STRIP : (i + 1) * STRIP, :] for i in range(count)]
    units = [jnp.where(lane_ids == row_ids + i * STRIP, 1.0, 0.0).astype(F32) for i in range(count)]
    width = GROUP * STRIP
    for first in range(0, count, GROUP):
        panel_end = (first // PANEL + 1) * PANEL
        base = first * STRIP
        entry, top_rows, unit_rows, roots = {}, [], [], []
        for a in range(GROUP):
            for j in range((a + 1) * STRIP):
                column = whole_lane(tops[first + a], base + j)
                for i in range(max(j, a * STRIP), (a + 1) * STRIP):
                    entry[i, j] = whole_row(column, i - a * STRIP)
            top_rows += [whole_row(tops[first + a], r) for r in range(STRIP)]
            unit_rows += [whole_row(units[first + a], r) for r in range(STRIP)]
        for j in range(0, width, 2):
            corner, side, other = entry[j, j], entry[j + 1, j], entry[j + 1, j + 1]
            root = lax.rsqrt(corner)
            next_root = lax.rsqrt(corner * other - side * side) * (corner * root)
            roots += [root, next_root]
            side = side * root
            entry[j + 1, j] = side
            for i in range(j + 2, width):
                entry[i, j] = entry[i, j] * root
                entry[i, j + 1] = (entry[i, j + 1] - entry[i, j] * side) * next_root
            for k in range(j + 2, width):
                for i in range(k, width):
                    entry[i, k] = entry[i, k] - (
                        entry[i, j] * entry[k, j] + entry[i, j + 1] * entry[k, j + 1]
                    )
        for j in range(width):
            for k in range(j):
                top_rows[j] = top_rows[j] - entry[j, k] * top_rows[k]
                unit_rows[j] = unit_rows[j] - entry[j, k] * unit_rows[k]
            top_rows[j] = top_rows[j] * roots[j]
            unit_rows[j] = unit_rows[j] * roots[j]
        for i in range(first + GROUP, panel_end):
            cols = [whole_lane(tops[i], base + j) for j in range(width)]
            top, unit = tops[i], units[i]
            for j in range(width):
                for k in range(j):
                    cols[j] = cols[j] - cols[k] * entry[j, k]
                cols[j] = cols[j] * roots[j]
                top = top - cols[j] * top_rows[j]
                unit = unit - cols[j] * unit_rows[j]
            tops[i], units[i] = top, unit
        for a in range(GROUP):
            top, unit = top_rows[(a + 1) * STRIP - 1], unit_rows[(a + 1) * STRIP - 1]
            for r in range(STRIP - 1):
                top = jnp.where(row_ids == r, top_rows[a * STRIP + r], top)
                unit = jnp.where(row_ids == r, unit_rows[a * STRIP + r], unit)
            tops[first + a], units[first + a] = top, unit
            inverse_ref[(first + a) * STRIP : (first + a + 1) * STRIP, :] = unit
        if first + GROUP == panel_end and panel_end < count:
            panel = slice(panel_end - PANEL, panel_end)
            top = jnp.concatenate(tops[panel], axis=0)
            both = jnp.concatenate([top, jnp.concatenate(units[panel], axis=0)], axis=1)
            update = tn_dot(top, both, HIGH)
            for i in range(panel_end, count):
                mine = slice(i * STRIP, (i + 1) * STRIP)
                tops[i] = tops[i] - update[mine, :LANES]
                units[i] = units[i] - update[mine, LANES:]


def factor_kernel(system_ref, first_prior_ref, panel_ref, solved_ref, weighted_ref, work, block, inverses, right):
    count = NB // BLK
    rows = lax.broadcasted_iota(jnp.int32, (NB, NB), 0)
    cols = lax.broadcasted_iota(jnp.int32, (NB, NB), 1)
    diagonal = jnp.where(rows == cols, first_prior_ref[...], 0.0)
    work[:, :, :NB] = (system_ref[:, :NB] + diagonal).reshape(count, BLK, NB)
    work[:, :, NB:] = system_ref[:, NB:].reshape(count, BLK, panel_ref.shape[1])

    def eliminate(k, carry):
        block[...] = work[k, :, pl.ds(pl.multiple_of(k * BLK, BLK), BLK)]
        inverse_factor(block, inverses.at[k])
        row = jnp.dot(
            stack_left(inverses[k], 1), stack_right(work[k]), preferred_element_type=F32
        )
        work[k] = row
        right[...] = stack_right(row)
        for i in range(1, count):

            @pl.when(i > k)
            def _():
                left = stack_left(row[:, i * BLK : (i + 1) * BLK].T, 1)
                work[i] -= jnp.dot(left, right[...], preferred_element_type=F32)

        return carry

    lax.fori_loop(0, count, eliminate, 0)
    for k in range(count - 1, -1, -1):
        mine = pl.ds(k * BLK, BLK)
        panel = work[k, :, NB:]
        panel_ref[mine, :] = panel
        if k < count - 1:
            panel = panel - jnp.dot(
                stack_left(work[k, :, (k + 1) * BLK : NB], 1),
                stack_right(solved_ref[(k + 1) * BLK :, :]),
                preferred_element_type=F32,
            )
        solved_ref[mine, :] = jnp.dot(
            stack_left(inverses[k].T, 1), stack_right(panel), preferred_element_type=F32
        )
    column = jnp.sum(diagonal, axis=1, keepdims=True)
    weighted_ref[...] = solved_ref[...] * column


def schur_kernel(
    factor,
    offset_ref,
    points_ref,
    log_weights,
    area_features_ref,
    prior_ref,
    head_ref,
    cols_ref,
    solved_ref,
    weighted_ref,
    out_ref,
    left_even,
    left_odd,
    residual,
):
    tile = pl.program_id(0)
    tiles = pl.num_programs(0)
    col_width = cols_ref.shape[0]
    total = log_weights.shape[1]
    steps = total // CHUNK
    first_points = NB + col_width
    tile_rows = out_ref.shape[0]

    @pl.when(tile == 0)
    def _():
        points = points_ref[first_points : first_points + tile_rows, :]
        transposed = solved_ref[...].T
        high = transposed.astype(BF16)
        low = (transposed - high.astype(F32)).astype(BF16)

        def step(index, carry):
            first = pl.multiple_of(index * CHUNK, CHUNK)
            here = pl.ds(first, CHUNK)
            right = head_ref[:, here]
            removed = jnp.dot(high, right, preferred_element_type=F32)
            removed += jnp.dot(low, right, preferred_element_type=F32)
            residual[here, :] = (cols_ref[:, here].astype(F32) - removed).astype(BF16).T
            fill_kernel(left_even, points, area_features_ref, log_weights, first, CHUNK)
            return carry

        lax.fori_loop(0, steps, step, 0)

    def run(source, dest):
        if dest is not None:
            next_row = pl.multiple_of(first_points + (tile + 1) * tile_rows, 16)
            points = points_ref[pl.ds(next_row, tile_rows), :]
        halves = max(1, col_width // 256)
        wide = col_width // halves
        pieces = [(first, half * wide) for first in range(0, total, SPAN) for half in range(halves)]
        stride = total // len(pieces)
        squares = None
        if dest is not None:
            squares = [squared_distances(points, area_features_ref, start) for start in range(0, stride, PIECE)]
        for index, (first, column) in enumerate(pieces):
            start = index * stride
            later = None
            if dest is not None and index + 1 < len(pieces):
                later = [
                    squared_distances(points, area_features_ref, start + stride + more)
                    for more in range(0, stride, PIECE)
                ]
            lanes = slice(column, column + wide)
            part = jnp.dot(
                source[:, first : first + SPAN],
                residual[first : first + SPAN, lanes],
                preferred_element_type=F32,
            )
            out_ref[:, lanes] = part if first == 0 else out_ref[:, lanes] + part
            if dest is not None:
                for more in range(0, stride, PIECE):
                    kernel_values(dest, squares[more // PIECE], log_weights, start + more)
            squares = later

    parity = lax.rem(tile, 2)
    more = tile < tiles - 1
    pl.when(jnp.logical_and(more, parity == 0))(lambda: run(left_even, left_odd))
    pl.when(jnp.logical_and(more, parity == 1))(lambda: run(left_odd, left_even))
    pl.when(jnp.logical_and(jnp.logical_not(more), parity == 0))(lambda: run(left_even, None))
    pl.when(jnp.logical_and(jnp.logical_not(more), parity == 1))(lambda: run(left_odd, None))

    rows = lax.broadcasted_iota(jnp.int32, (tile_rows, col_width), 0) + (offset_ref[1] + tile * tile_rows)
    cols = lax.broadcasted_iota(jnp.int32, (tile_rows, col_width), 1) + offset_ref[0]
    out_ref[...] = out_ref[...] * factor + jnp.where(rows == cols, prior_ref[...], 0.0)

    first_row = offset_ref[1] + tile * tile_rows

    @pl.when(first_row < NB)
    def _():
        out_ref[...] -= weighted_ref[pl.ds(pl.multiple_of(first_row, tile_rows), tile_rows), :]


def all_areas(array):
    if lax.axis_size("area") == 2:
        return [array, lax.ppermute(array, "area", [(0, 1), (1, 0)])]
    return [lax.all_gather(array, "area", axis=array.ndim - 1, tiled=True)]


def from_first(array, axis):
    total = jnp.where(lax.axis_index(axis) == 0, array, 0.0)
    for target in range(1, lax.axis_size(axis)):
        total = total + lax.ppermute(array, axis, [(0, target)])
    return total


def first_block_prior(prior):
    if prior.shape[0] == NB:
        return from_first(from_first(prior.reshape(1, NB), "col"), "row")
    return lax.all_gather(prior, ("row", "col"), axis=0, tiled=True)[:NB].reshape(1, NB)


def per_device(area_xy, sampling_var, inducer_xy, order, prior):
    size_total = order.shape[0]
    length_scale = 2.0 / math.sqrt(size_total)
    scale = math.log2(math.e) / length_scale
    center = 6.0 / math.sqrt(size_total) * scale
    col_width = prior.shape[0]
    row_height = size_total // lax.axis_size("area")
    areas_total = area_xy.shape[1] * lax.axis_size("area")
    factor = size_total / areas_total

    own = jnp.concatenate([area_xy, sampling_var[None, :]], axis=0)
    areas = all_areas(own)
    first_prior = first_block_prior(prior)
    own_prior = prior.reshape(1, col_width)
    offsets = jnp.stack(
        [block_position() * col_width, lax.axis_index("area") * row_height, lax.axis_index("area")]
    ).astype(jnp.int32)

    points = gram_points(offsets, order, inducer_xy, scale, center, col_width, row_height)
    tile_rows = min(row_height, 512 if areas_total <= 8192 else 256)
    smem = pl.BlockSpec(memory_space=pltpu.SMEM)
    vmem = pl.BlockSpec(memory_space=pltpu.VMEM)
    params = pltpu.CompilerParams(vmem_limit_bytes=VMEM_BYTES)
    head, cols, system, area_features, log_weights = pl.pallas_call(
        functools.partial(head_kernel, factor, scale, center),
        out_shape=(
            jax.ShapeDtypeStruct((NB, areas_total), BF16),
            jax.ShapeDtypeStruct((col_width, areas_total), BF16),
            jax.ShapeDtypeStruct((NB, NB + col_width), F32),
            jax.ShapeDtypeStruct((FEATURES, areas_total), BF16),
            jax.ShapeDtypeStruct((1, areas_total), F32),
        ),
        in_specs=[smem] + [vmem] * (2 + len(areas)),
        out_specs=[vmem] * 5,
        cost_estimate=pl.CostEstimate(flops=10**10, bytes_accessed=2**24, transcendentals=0),
        scratch_shapes=[pltpu.VMEM((FEATURES, areas_total), F32)],
        compiler_params=params,
        name="head",
    )(offsets, points, *areas, own_prior)
    panel_rows, solved, weighted = pl.pallas_call(
        factor_kernel,
        out_shape=(jax.ShapeDtypeStruct((NB, col_width), F32),) * 3,
        in_specs=[vmem] * 2,
        out_specs=[vmem] * 3,
        scratch_shapes=[
            pltpu.VMEM((NB // BLK, BLK, NB + col_width), F32),
            pltpu.VMEM((BLK, BLK), F32),
            pltpu.VMEM((NB // BLK, BLK, BLK), F32),
            pltpu.VMEM((6 * BLK, NB + col_width), BF16),
        ],
        compiler_params=params,
        name="factor",
    )(system, first_prior)
    schur = pl.pallas_call(
        functools.partial(schur_kernel, factor),
        grid=(row_height // tile_rows,),
        out_shape=jax.ShapeDtypeStruct((row_height, col_width), F32),
        in_specs=[smem] + [vmem] * 8,
        out_specs=pl.BlockSpec((tile_rows, col_width), lambda i: (i, 0)),
        scratch_shapes=[
            pltpu.VMEM((tile_rows, areas_total), BF16),
            pltpu.VMEM((tile_rows, areas_total), BF16),
            pltpu.VMEM((areas_total, col_width), BF16),
        ],
        compiler_params=params,
        name="schur",
    )(offsets, points, log_weights, area_features, own_prior, head, cols, solved, weighted)
    return (panel_rows, schur)


def solution(mesh):
    in_specs = (P(None, "area"), P("area"), P(), P(), P(("row", "col")))
    out_specs = (P(None, ("row", "col")), P("area", ("row", "col")))
    return jax.shard_map(
        per_device, mesh=mesh, in_specs=in_specs, out_specs=out_specs, check_vma=False
    )
```

```python
import functools
import math

import jax
import jax.numpy as jnp
from jax import lax
from jax.experimental import pallas as pl
from jax.experimental.pallas import tpu as pltpu
from jax.sharding import PartitionSpec as P

NB = 512
LANES = 128
STRIP = 8
GROUP = 1
PANEL = 4
BLK = 128
CHUNK = 1024
SPAN = 512
PIECE = 256
VMEM_BYTES = 60 * 1024 * 1024
HIGH = lax.Precision.HIGHEST
F32 = jnp.float32
BF16 = jnp.bfloat16


def split_pieces(value):
    first = value.astype(BF16)
    rest = value - first.astype(F32)
    second = rest.astype(BF16)
    third = (rest - second.astype(F32)).astype(BF16)
    return first, second, third


def nt_dot(left, right, precision=None):
    return lax.dot_general(
        left, right, (((1,), (1,)), ((), ())), precision=precision, preferred_element_type=F32
    )


def tn_dot(left, right, precision=None):
    return lax.dot_general(
        left, right, (((0,), (0,)), ((), ())), precision=precision, preferred_element_type=F32
    )


def stack_left(value, axis):
    a, b, c = split_pieces(value)
    return jnp.concatenate([a, a, b, b, a, c], axis=axis)


def stack_right(value):
    a, b, c = split_pieces(value)
    return jnp.concatenate([a, b, a, b, c, a], axis=0)


def block_position():
    return lax.axis_index("row") * lax.axis_size("col") + lax.axis_index("col")


FEATURES = 32
PIECE_PAIRS = ((0, 0), (0, 1), (1, 0), (1, 1), (0, 2), (2, 0))


def write_features(dest, x_row, y_row, left):
    one = jnp.ones_like(x_row)
    norm = [piece.astype(F32) for piece in split_pieces(x_row * x_row + y_row * y_row)]
    rows = norm + [one] * 3 if left else [one] * 3 + norm
    for coordinate in (x_row, y_row):
        factor = 1.0 if left else -2.0
        pieces = [piece.astype(F32) * factor for piece in split_pieces(coordinate)]
        rows += [pieces[pair[0 if left else 1]] for pair in PIECE_PAIRS]
    for index, row in enumerate(rows):
        dest[index : index + 1, :] = row


def points_kernel(
    scale, center, col_width, offset_ref, order_ref, table_ref, features_ref, columns_ref, places, features, tables
):
    quotients = order_ref.shape[0]
    for q in range(quotients):
        for k in range(2):
            tables[k, q : q + 1, :] = table_ref[k : k + 1, q * LANES : (q + 1) * LANES]
    pieces_x = split_pieces(tables[0] * scale - center)
    pieces_y = split_pieces(tables[1] * scale - center)
    columns_ref[...] = jnp.concatenate(
        [jnp.concatenate(pieces_x, axis=0), jnp.concatenate(pieces_y, axis=0)], axis=1
    ).T
    quotient_ids = lax.broadcasted_iota(jnp.int32, (quotients, LANES), 0)
    lane_ids = lax.broadcasted_iota(jnp.int32, (LANES, LANES), 0)

    def one_block(step):
        row = step
        if step >= (NB + col_width) // LANES:
            row = offset_ref[1] // LANES + step - (NB + col_width) // LANES
        elif step >= NB // LANES:
            row = offset_ref[0] // LANES + step - NB // LANES
        ids = order_ref[pl.ds(row, 1), :]
        hit = jnp.where(quotient_ids == lax.shift_right_logical(ids, 7), 1.0, 0.0).astype(BF16)
        values = jnp.dot(
            columns_ref[...], jnp.concatenate([hit, hit, hit], axis=0), preferred_element_type=F32
        )
        mine = lane_ids == lax.bitwise_and(ids, LANES - 1)
        return [
            jnp.sum(jnp.where(mine, values[k * LANES : (k + 1) * LANES], 0.0), axis=0, keepdims=True)
            for k in range(2)
        ]

    blocks = features_ref.shape[0] // LANES
    for step in range(blocks):
        x_row, y_row = one_block(step)
        places[0:1, step * LANES : (step + 1) * LANES] = x_row
        places[1:2, step * LANES : (step + 1) * LANES] = y_row
    features[...] = jnp.zeros_like(features)
    write_features(features, places[0:1, :], places[1:2, :], True)
    for step in range(blocks):
        mine = slice(step * LANES, (step + 1) * LANES)
        features_ref[mine, :] = features[:, mine].T.astype(BF16)


def gram_points(offsets, order, inducer_xy, scale, center, col_width, row_height):
    quotients = order.shape[0] // LANES
    count = NB + col_width + row_height
    return pl.pallas_call(
        functools.partial(points_kernel, scale, center, col_width),
        out_shape=jax.ShapeDtypeStruct((count, FEATURES), BF16),
        in_specs=[
            pl.BlockSpec(memory_space=pltpu.SMEM),
            pl.BlockSpec(memory_space=pltpu.VMEM),
            pl.BlockSpec(memory_space=pltpu.VMEM),
        ],
        out_specs=pl.BlockSpec(memory_space=pltpu.VMEM),
        scratch_shapes=[
            pltpu.VMEM((2 * LANES, 3 * quotients), BF16),
            pltpu.VMEM((2, count), F32),
            pltpu.VMEM((FEATURES, count), F32),
            pltpu.VMEM((2, quotients, LANES), F32),
        ],
        compiler_params=pltpu.CompilerParams(vmem_limit_bytes=VMEM_BYTES),
        cost_estimate=pl.CostEstimate(flops=5 * 10**9, bytes_accessed=2**20, transcendentals=0),
        name="points",
    )(offsets, order.reshape(quotients, LANES), inducer_xy)


def root(square):
    square = jnp.maximum(square, 1e-30)
    return square * lax.rsqrt(square)


def squared_distances(points, area_features, first):
    return jnp.dot(points, area_features[:, pl.ds(first, PIECE)], preferred_element_type=F32)


def kernel_values(dest, squares, log_weights, first):
    for half in range(0, PIECE, LANES):
        lanes = pl.ds(first + half, LANES)
        weights = jnp.broadcast_to(log_weights[0:1, lanes], (16, LANES))
        for row in range(0, squares.shape[0], 16):
            distance = root(squares[row : row + 16, half : half + LANES])
            dest[row : row + 16, lanes] = jnp.exp2(weights - distance).astype(BF16)


def fill_kernel(dest, points, area_features, log_weights, first, count):
    for start in range(0, count, PIECE):
        squares = squared_distances(points, area_features, first + start)
        kernel_values(dest, squares, log_weights, first + start)


def head_kernel(
    factor,
    scale,
    center,
    offset_ref,
    points_ref,
    *refs,
):
    *area_refs, prior_ref, head_ref, cols_ref, system_ref, area_features_ref, log_weights, features = refs
    col_width = cols_ref.shape[0]
    total = area_features_ref.shape[1]
    features[...] = jnp.zeros_like(features)
    width = total // len(area_refs)
    for index in range(len(area_refs)):
        values = area_refs[index][...]
        if len(area_refs) == 2:
            values = jnp.where(offset_ref[2] == index, area_refs[0][...], area_refs[1][...])
        lanes = slice(index * width, (index + 1) * width)
        places = values[0:2] * scale - center
        write_features(features.at[:, lanes], places[0:1], places[1:2], False)
        log_weights[:, lanes] = -0.5 * jnp.log2(0.5 + values[2:3])
    area_features_ref[...] = features[...].astype(BF16)
    system_ref[...] = jnp.zeros_like(system_ref)
    group = min(4096, total)

    def step(index, carry):
        base = pl.multiple_of(index * group, group)
        targets = [(head_ref, points_ref[:NB, :]), (cols_ref, points_ref[NB : NB + col_width, :])]

        def distances(start):
            return [squared_distances(points, area_features_ref, base + start) for _, points in targets]

        def accumulate(start):
            here = pl.ds(base + start, CHUNK)
            left = head_ref[:, here]
            system_ref[:, :NB] += nt_dot(left, left)
            system_ref[:, NB:] += nt_dot(left, cols_ref[:, here])

        squares = distances(0)
        for start in range(0, group, PIECE):
            later = distances(start + PIECE) if start + PIECE < group else None
            if start and start % CHUNK == 0:
                accumulate(start - CHUNK)
            for (dest, _), square in zip(targets, squares):
                kernel_values(dest, square, log_weights, base + start)
            squares = later
        accumulate(group - CHUNK)
        return carry

    lax.fori_loop(0, total // group, step, 0)
    system_ref[:, :NB] = system_ref[:, :NB] * factor
    rows = lax.broadcasted_iota(jnp.int32, (NB, col_width), 0)
    cols = lax.broadcasted_iota(jnp.int32, (NB, col_width), 1) + offset_ref[0]
    system_ref[:, NB:] = system_ref[:, NB:] * factor + jnp.where(rows == cols, prior_ref[...], 0.0)


def whole_row(value, index):
    return jnp.broadcast_to(value[index : index + 1, :], (STRIP, LANES))


def whole_lane(value, index):
    return jnp.broadcast_to(value[:, index : index + 1], (STRIP, LANES))


def inverse_factor(block_ref, inverse_ref):
    count = BLK // STRIP
    row_ids = lax.broadcasted_iota(jnp.int32, (STRIP, LANES), 0)
    lane_ids = lax.broadcasted_iota(jnp.int32, (STRIP, LANES), 1)
    tops = [block_ref[i * STRIP : (i + 1) * STRIP, :] for i in range(count)]
    units = [jnp.where(lane_ids == row_ids + i * STRIP, 1.0, 0.0).astype(F32) for i in range(count)]
    width = GROUP * STRIP
    for first in range(0, count, GROUP):
        panel_end = (first // PANEL + 1) * PANEL
        base = first * STRIP
        entry, top_rows, unit_rows, roots = {}, [], [], []
        for a in range(GROUP):
            for j in range((a + 1) * STRIP):
                column = whole_lane(tops[first + a], base + j)
                for i in range(max(j, a * STRIP), (a + 1) * STRIP):
                    entry[i, j] = whole_row(column, i - a * STRIP)
            top_rows += [whole_row(tops[first + a], r) for r in range(STRIP)]
            unit_rows += [whole_row(units[first + a], r) for r in range(STRIP)]
        for j in range(0, width, 2):
            corner, side, other = entry[j, j], entry[j + 1, j], entry[j + 1, j + 1]
            root = lax.rsqrt(corner)
            next_root = lax.rsqrt(corner * other - side * side) * (corner * root)
            roots += [root, next_root]
            side = side * root
            entry[j + 1, j] = side
            for i in range(j + 2, width):
                entry[i, j] = entry[i, j] * root
                entry[i, j + 1] = (entry[i, j + 1] - entry[i, j] * side) * next_root
            for k in range(j + 2, width):
                for i in range(k, width):
                    entry[i, k] = entry[i, k] - (
                        entry[i, j] * entry[k, j] + entry[i, j + 1] * entry[k, j + 1]
                    )
        for j in range(width):
            for k in range(j):
                top_rows[j] = top_rows[j] - entry[j, k] * top_rows[k]
                unit_rows[j] = unit_rows[j] - entry[j, k] * unit_rows[k]
            top_rows[j] = top_rows[j] * roots[j]
            unit_rows[j] = unit_rows[j] * roots[j]
        for i in range(first + GROUP, panel_end):
            cols = [whole_lane(tops[i], base + j) for j in range(width)]
            top, unit = tops[i], units[i]
            for j in range(width):
                for k in range(j):
                    cols[j] = cols[j] - cols[k] * entry[j, k]
                cols[j] = cols[j] * roots[j]
                top = top - cols[j] * top_rows[j]
                unit = unit - cols[j] * unit_rows[j]
            tops[i], units[i] = top, unit
        for a in range(GROUP):
            top, unit = top_rows[(a + 1) * STRIP - 1], unit_rows[(a + 1) * STRIP - 1]
            for r in range(STRIP - 1):
                top = jnp.where(row_ids == r, top_rows[a * STRIP + r], top)
                unit = jnp.where(row_ids == r, unit_rows[a * STRIP + r], unit)
            tops[first + a], units[first + a] = top, unit
            inverse_ref[(first + a) * STRIP : (first + a + 1) * STRIP, :] = unit
        if first + GROUP == panel_end and panel_end < count:
            panel = slice(panel_end - PANEL, panel_end)
            top = jnp.concatenate(tops[panel], axis=0)
            both = jnp.concatenate([top, jnp.concatenate(units[panel], axis=0)], axis=1)
            update = tn_dot(top, both, HIGH)
            for i in range(panel_end, count):
                mine = slice(i * STRIP, (i + 1) * STRIP)
                tops[i] = tops[i] - update[mine, :LANES]
                units[i] = units[i] - update[mine, LANES:]


def factor_kernel(system_ref, first_prior_ref, panel_ref, solved_ref, weighted_ref, block, inverses, right):
    count = NB // BLK
    rows = lax.broadcasted_iota(jnp.int32, (NB, NB), 0)
    cols = lax.broadcasted_iota(jnp.int32, (NB, NB), 1)
    diagonal = jnp.where(rows == cols, first_prior_ref[...], 0.0)
    system_ref[:, :NB] = system_ref[:, :NB] + diagonal

    def eliminate(k, carry):
        mine = pl.ds(pl.multiple_of(k * BLK, BLK), BLK)
        block[...] = system_ref[mine, mine]
        inverse_factor(block, inverses.at[k])
        row = jnp.dot(
            stack_left(inverses[k], 1), stack_right(system_ref[mine, :]), preferred_element_type=F32
        )
        system_ref[mine, :] = row
        right[...] = stack_right(row)
        for i in range(1, count):

            @pl.when(i > k)
            def _():
                left = stack_left(row[:, i * BLK : (i + 1) * BLK].T, 1)
                system_ref[i * BLK : (i + 1) * BLK, :] -= jnp.dot(
                    left, right[...], preferred_element_type=F32
                )

        return carry

    lax.fori_loop(0, count, eliminate, 0)
    for k in range(count - 1, -1, -1):
        mine = pl.ds(k * BLK, BLK)
        panel = system_ref[mine, NB:]
        panel_ref[mine, :] = panel
        if k < count - 1:
            panel = panel - jnp.dot(
                stack_left(system_ref[mine, (k + 1) * BLK : NB], 1),
                stack_right(solved_ref[(k + 1) * BLK :, :]),
                preferred_element_type=F32,
            )
        solved_ref[mine, :] = jnp.dot(
            stack_left(inverses[k].T, 1), stack_right(panel), preferred_element_type=F32
        )
    column = jnp.sum(diagonal, axis=1, keepdims=True)
    weighted_ref[...] = solved_ref[...] * column


def schur_kernel(
    factor,
    offset_ref,
    points_ref,
    log_weights,
    area_features_ref,
    prior_ref,
    head_ref,
    cols_ref,
    solved_ref,
    weighted_ref,
    out_ref,
    left_even,
    left_odd,
    residual,
):
    tile = pl.program_id(0)
    tiles = pl.num_programs(0)
    col_width = cols_ref.shape[0]
    total = log_weights.shape[1]
    first_points = NB + col_width
    tile_rows = out_ref.shape[0]

    @pl.when(tile == 0)
    def _():
        points = points_ref[first_points : first_points + tile_rows, :]
        transposed = solved_ref[...].T
        high = transposed.astype(BF16)
        low = (transposed - high.astype(F32)).astype(BF16)

        group = min(4096, total)

        def step(index, carry):
            base = pl.multiple_of(index * group, group)
            squares = squared_distances(points, area_features_ref, base)
            for start in range(0, group, PIECE):
                later = None
                if start + PIECE < group:
                    later = squared_distances(points, area_features_ref, base + start + PIECE)
                if start % SPAN == 0:
                    here = pl.ds(base + start, SPAN)
                    right = head_ref[:, here]
                    removed = jnp.dot(high, right, preferred_element_type=F32)
                    removed += jnp.dot(low, right, preferred_element_type=F32)
                    residual[here, :] = (cols_ref[:, here].astype(F32) - removed).astype(BF16).T
                kernel_values(left_even, squares, log_weights, base + start)
                squares = later
            return carry

        lax.fori_loop(0, total // group, step, 0)

    def run(source, dest):
        if dest is not None:
            next_row = pl.multiple_of(first_points + (tile + 1) * tile_rows, 16)
            points = points_ref[pl.ds(next_row, tile_rows), :]
        halves = max(1, col_width // 256)
        wide = col_width // halves
        pieces = [(first, half * wide) for first in range(0, total, SPAN) for half in range(halves)]
        stride = total // len(pieces)
        squares = None
        if dest is not None:
            squares = [squared_distances(points, area_features_ref, start) for start in range(0, stride, PIECE)]
        for index, (first, column) in enumerate(pieces):
            start = index * stride
            later = None
            if dest is not None and index + 1 < len(pieces):
                later = [
                    squared_distances(points, area_features_ref, start + stride + more)
                    for more in range(0, stride, PIECE)
                ]
            lanes = slice(column, column + wide)
            part = jnp.dot(
                source[:, first : first + SPAN],
                residual[first : first + SPAN, lanes],
                preferred_element_type=F32,
            )
            out_ref[:, lanes] = part if first == 0 else out_ref[:, lanes] + part
            if dest is not None:
                for more in range(0, stride, PIECE):
                    kernel_values(dest, squares[more // PIECE], log_weights, start + more)
            squares = later

    parity = lax.rem(tile, 2)
    more = tile < tiles - 1
    pl.when(jnp.logical_and(more, parity == 0))(lambda: run(left_even, left_odd))
    pl.when(jnp.logical_and(more, parity == 1))(lambda: run(left_odd, left_even))
    pl.when(jnp.logical_and(jnp.logical_not(more), parity == 0))(lambda: run(left_even, None))
    pl.when(jnp.logical_and(jnp.logical_not(more), parity == 1))(lambda: run(left_odd, None))

    rows = lax.broadcasted_iota(jnp.int32, (tile_rows, col_width), 0) + (offset_ref[1] + tile * tile_rows)
    cols = lax.broadcasted_iota(jnp.int32, (tile_rows, col_width), 1) + offset_ref[0]
    out_ref[...] = out_ref[...] * factor + jnp.where(rows == cols, prior_ref[...], 0.0)

    first_row = offset_ref[1] + tile * tile_rows

    @pl.when(first_row < NB)
    def _():
        out_ref[...] -= weighted_ref[pl.ds(pl.multiple_of(first_row, tile_rows), tile_rows), :]


def whole_kernel(factor, scale, center, offset_ref, points_ref, *refs):
    areas, rest = refs[:-18], refs[-18:]
    prior_ref, first_prior_ref, panel_ref, out_ref = rest[:4]
    head, cols, system, area_features, log_weights, features = rest[4:10]
    block, inverses, right, solved, weighted = rest[10:15]

    @pl.when(pl.program_id(0) == 0)
    def _():
        head_kernel(
            factor, scale, center, offset_ref, points_ref, *areas, prior_ref,
            head, cols, system, area_features, log_weights, features,
        )
        factor_kernel(system, first_prior_ref, panel_ref, solved, weighted, block, inverses, right)

    schur_kernel(
        factor, offset_ref, points_ref, log_weights, area_features, prior_ref,
        head, cols, solved, weighted, out_ref, *rest[15:],
    )


def all_areas(array):
    if lax.axis_size("area") == 2:
        return [array, lax.ppermute(array, "area", [(0, 1), (1, 0)])]
    return [lax.all_gather(array, "area", axis=array.ndim - 1, tiled=True)]


def from_first(array, axis):
    total = jnp.where(lax.axis_index(axis) == 0, array, 0.0)
    for target in range(1, lax.axis_size(axis)):
        total = total + lax.ppermute(array, axis, [(0, target)])
    return total


def first_block_prior(prior):
    if prior.shape[0] == NB:
        return from_first(from_first(prior.reshape(1, NB), "col"), "row")
    return lax.all_gather(prior, ("row", "col"), axis=0, tiled=True)[:NB].reshape(1, NB)


def per_device(area_xy, sampling_var, inducer_xy, order, prior):
    size_total = order.shape[0]
    length_scale = 2.0 / math.sqrt(size_total)
    scale = math.log2(math.e) / length_scale
    center = 6.0 / math.sqrt(size_total) * scale
    col_width = prior.shape[0]
    row_height = size_total // lax.axis_size("area")
    areas_total = area_xy.shape[1] * lax.axis_size("area")
    factor = size_total / areas_total

    own = jnp.concatenate([area_xy, sampling_var[None, :]], axis=0)
    areas = all_areas(own)
    first_prior = first_block_prior(prior)
    own_prior = prior.reshape(1, col_width)
    offsets = jnp.stack(
        [block_position() * col_width, lax.axis_index("area") * row_height, lax.axis_index("area")]
    ).astype(jnp.int32)

    points = gram_points(offsets, order, inducer_xy, scale, center, col_width, row_height)
    tile_rows = min(row_height, 512 if areas_total <= 8192 else 128)
    smem = pl.BlockSpec(memory_space=pltpu.SMEM)
    vmem = pl.BlockSpec(memory_space=pltpu.VMEM)
    params = pltpu.CompilerParams(vmem_limit_bytes=VMEM_BYTES)
    panel_rows, schur = pl.pallas_call(
        functools.partial(whole_kernel, factor, scale, center),
        grid=(row_height // tile_rows,),
        out_shape=(
            jax.ShapeDtypeStruct((NB, col_width), F32),
            jax.ShapeDtypeStruct((row_height, col_width), F32),
        ),
        in_specs=[smem] + [vmem] * (3 + len(areas)),
        out_specs=[vmem, pl.BlockSpec((tile_rows, col_width), lambda i: (i, 0))],
        scratch_shapes=[
            pltpu.VMEM((NB, areas_total), BF16),
            pltpu.VMEM((col_width, areas_total), BF16),
            pltpu.VMEM((NB, NB + col_width), F32),
            pltpu.VMEM((FEATURES, areas_total), BF16),
            pltpu.VMEM((1, areas_total), F32),
            pltpu.VMEM((FEATURES, areas_total), F32),
            pltpu.VMEM((BLK, BLK), F32),
            pltpu.VMEM((NB // BLK, BLK, BLK), F32),
            pltpu.VMEM((6 * BLK, NB + col_width), BF16),
            pltpu.VMEM((NB, col_width), F32),
            pltpu.VMEM((NB, col_width), F32),
            pltpu.VMEM((tile_rows, areas_total), BF16),
            pltpu.VMEM((tile_rows, areas_total), BF16),
            pltpu.VMEM((areas_total, col_width), BF16),
        ],
        compiler_params=params,
        cost_estimate=pl.CostEstimate(flops=5 * 10**10, bytes_accessed=2**24, transcendentals=0),
        name="schur",
    )(offsets, points, *areas, own_prior, first_prior)
    return (panel_rows, schur)


def solution(mesh):
    in_specs = (P(None, "area"), P("area"), P(), P(), P(("row", "col")))
    out_specs = (P(None, ("row", "col")), P("area", ("row", "col")))
    return jax.shard_map(
        per_device, mesh=mesh, in_specs=in_specs, out_specs=out_specs, check_vma=False
    )
```

```python
import functools
import math

import jax
import jax.numpy as jnp
import numpy as np
from jax import lax
from jax.experimental import pallas as pl
from jax.experimental.pallas import tpu as pltpu
from jax.sharding import PartitionSpec as P

NB = 512
LANES = 128
STRIP = 8
GROUP = 1
PANEL = 4
BLK = 128
CHUNK = 1024
SPAN = 512
PIECE = 256
POWER_EVERY = 3
LOWEST = -0.5 * math.log2(128.5) - 6 * math.sqrt(2) * math.log2(math.e)
HIGHEST = -0.5 * math.log2(8.5)
MIDDLE = (LOWEST + HIGHEST) / 2
REACH = (HIGHEST - LOWEST) / 2 + 0.01
VMEM_BYTES = 60 * 1024 * 1024
HIGH = lax.Precision.HIGHEST
F32 = jnp.float32
BF16 = jnp.bfloat16


def split_pieces(value):
    first = value.astype(BF16)
    rest = value - first.astype(F32)
    second = rest.astype(BF16)
    third = (rest - second.astype(F32)).astype(BF16)
    return first, second, third


def nt_dot(left, right, precision=None):
    return lax.dot_general(
        left, right, (((1,), (1,)), ((), ())), precision=precision, preferred_element_type=F32
    )


def tn_dot(left, right, precision=None):
    return lax.dot_general(
        left, right, (((0,), (0,)), ((), ())), precision=precision, preferred_element_type=F32
    )


def stack_left(value, axis):
    a, b, c = split_pieces(value)
    return jnp.concatenate([a, a, b, b, a, c], axis=axis)


def stack_right(value):
    a, b, c = split_pieces(value)
    return jnp.concatenate([a, b, a, b, c, a], axis=0)


def block_position():
    return lax.axis_index("row") * lax.axis_size("col") + lax.axis_index("col")


FEATURES = 32
PIECE_PAIRS = ((0, 0), (0, 1), (1, 0), (1, 1), (0, 2), (2, 0))


def write_features(dest, x_row, y_row, left):
    one = jnp.ones_like(x_row)
    norm = [piece.astype(F32) for piece in split_pieces(x_row * x_row + y_row * y_row)]
    rows = norm + [one] * 3 if left else [one] * 3 + norm
    for coordinate in (x_row, y_row):
        factor = 1.0 if left else -2.0
        pieces = [piece.astype(F32) * factor for piece in split_pieces(coordinate)]
        rows += [pieces[pair[0 if left else 1]] for pair in PIECE_PAIRS]
    for index, row in enumerate(rows):
        dest[index : index + 1, :] = row


def points_kernel(
    scale, center, col_width, offset_ref, order_ref, table_ref, features_ref, columns_ref, places, features, tables
):
    quotients = order_ref.shape[0]
    for q in range(quotients):
        for k in range(2):
            tables[k, q : q + 1, :] = table_ref[k : k + 1, q * LANES : (q + 1) * LANES]
    pieces_x = split_pieces(tables[0] * scale - center)
    pieces_y = split_pieces(tables[1] * scale - center)
    columns_ref[...] = jnp.concatenate(
        [jnp.concatenate(pieces_x, axis=0), jnp.concatenate(pieces_y, axis=0)], axis=1
    ).T
    quotient_ids = lax.broadcasted_iota(jnp.int32, (quotients, LANES), 0)
    lane_ids = lax.broadcasted_iota(jnp.int32, (LANES, LANES), 0)

    def one_block(step):
        row = step
        if step >= (NB + col_width) // LANES:
            row = offset_ref[1] // LANES + step - (NB + col_width) // LANES
        elif step >= NB // LANES:
            row = offset_ref[0] // LANES + step - NB // LANES
        ids = order_ref[pl.ds(row, 1), :]
        hit = jnp.where(quotient_ids == lax.shift_right_logical(ids, 7), 1.0, 0.0).astype(BF16)
        values = jnp.dot(
            columns_ref[...], jnp.concatenate([hit, hit, hit], axis=0), preferred_element_type=F32
        )
        mine = lane_ids == lax.bitwise_and(ids, LANES - 1)
        return [
            jnp.sum(jnp.where(mine, values[k * LANES : (k + 1) * LANES], 0.0), axis=0, keepdims=True)
            for k in range(2)
        ]

    blocks = features_ref.shape[0] // LANES
    for step in range(blocks):
        x_row, y_row = one_block(step)
        places[0:1, step * LANES : (step + 1) * LANES] = x_row
        places[1:2, step * LANES : (step + 1) * LANES] = y_row
    features[...] = jnp.zeros_like(features)
    write_features(features, places[0:1, :], places[1:2, :], True)
    for step in range(blocks):
        mine = slice(step * LANES, (step + 1) * LANES)
        features_ref[mine, :] = features[:, mine].T.astype(BF16)


def gram_points(offsets, order, inducer_xy, scale, center, col_width, row_height):
    quotients = order.shape[0] // LANES
    count = NB + col_width + row_height
    return pl.pallas_call(
        functools.partial(points_kernel, scale, center, col_width),
        out_shape=jax.ShapeDtypeStruct((count, FEATURES), BF16),
        in_specs=[
            pl.BlockSpec(memory_space=pltpu.SMEM),
            pl.BlockSpec(memory_space=pltpu.VMEM),
            pl.BlockSpec(memory_space=pltpu.VMEM),
        ],
        out_specs=pl.BlockSpec(memory_space=pltpu.VMEM),
        scratch_shapes=[
            pltpu.VMEM((2 * LANES, 3 * quotients), BF16),
            pltpu.VMEM((2, count), F32),
            pltpu.VMEM((FEATURES, count), F32),
            pltpu.VMEM((2, quotients, LANES), F32),
        ],
        compiler_params=pltpu.CompilerParams(vmem_limit_bytes=VMEM_BYTES),
        cost_estimate=pl.CostEstimate(flops=5 * 10**9, bytes_accessed=2**20, transcendentals=0),
        name="points",
    )(offsets, order.reshape(quotients, LANES), inducer_xy)


def root(square):
    square = jnp.maximum(square, 1e-30)
    return square * lax.rsqrt(square)


def power_coefficients():
    nodes = np.cos((np.arange(64) + 0.5) * np.pi / 64) * REACH
    fit = np.polynomial.Chebyshev.fit(nodes, np.exp2((MIDDLE + nodes) / 16), 5, domain=[-REACH, REACH])
    return [float(value) for value in fit.convert(kind=np.polynomial.Polynomial).coef]


def power_of_two(offset):
    coefficients = power_coefficients()
    value = coefficients[-1] * offset + coefficients[-2]
    for coefficient in coefficients[-3::-1]:
        value = value * offset + coefficient
    for _ in range(4):
        value = value * value
    return value


def squared_distances(points, area_features, first):
    return jnp.dot(points, area_features[:, pl.ds(first, PIECE)], preferred_element_type=F32)


def kernel_values(dest, squares, log_weights, first):
    for half in range(0, PIECE, LANES):
        lanes = pl.ds(first + half, LANES)
        weights = jnp.broadcast_to(log_weights[0:1, lanes], (16, LANES))
        shifted = weights - MIDDLE
        for row in range(0, squares.shape[0], 16):
            distance = root(squares[row : row + 16, half : half + LANES])
            if row // 16 % POWER_EVERY == POWER_EVERY - 1:
                value = power_of_two(shifted - distance)
            else:
                value = jnp.exp2(weights - distance)
            dest[row : row + 16, lanes] = value.astype(BF16)


def fill_kernel(dest, points, area_features, log_weights, first, count):
    for start in range(0, count, PIECE):
        squares = squared_distances(points, area_features, first + start)
        kernel_values(dest, squares, log_weights, first + start)


def head_kernel(
    factor,
    scale,
    center,
    offset_ref,
    points_ref,
    *refs,
):
    *area_refs, prior_ref, head_ref, cols_ref, system_ref, area_features_ref, log_weights, features = refs
    col_width = cols_ref.shape[0]
    total = area_features_ref.shape[1]
    features[...] = jnp.zeros_like(features)
    width = total // len(area_refs)
    for index in range(len(area_refs)):
        values = area_refs[index][...]
        if len(area_refs) == 2:
            values = jnp.where(offset_ref[2] == index, area_refs[0][...], area_refs[1][...])
        lanes = slice(index * width, (index + 1) * width)
        places = values[0:2] * scale - center
        write_features(features.at[:, lanes], places[0:1], places[1:2], False)
        log_weights[:, lanes] = -0.5 * jnp.log2(0.5 + values[2:3])
    area_features_ref[...] = features[...].astype(BF16)
    system_ref[...] = jnp.zeros_like(system_ref)
    group = min(4096, total)

    def step(index, carry):
        base = pl.multiple_of(index * group, group)
        targets = [(head_ref, points_ref[:NB, :]), (cols_ref, points_ref[NB : NB + col_width, :])]

        def distances(start):
            return [squared_distances(points, area_features_ref, base + start) for _, points in targets]

        def accumulate(start):
            here = pl.ds(base + start, CHUNK)
            left = head_ref[:, here]
            system_ref[:, :NB] += nt_dot(left, left)
            system_ref[:, NB:] += nt_dot(left, cols_ref[:, here])

        squares = distances(0)
        for start in range(0, group, PIECE):
            later = distances(start + PIECE) if start + PIECE < group else None
            if start and start % CHUNK == 0:
                accumulate(start - CHUNK)
            for (dest, _), square in zip(targets, squares):
                kernel_values(dest, square, log_weights, base + start)
            squares = later
        accumulate(group - CHUNK)
        return carry

    lax.fori_loop(0, total // group, step, 0)
    system_ref[:, :NB] = system_ref[:, :NB] * factor
    rows = lax.broadcasted_iota(jnp.int32, (NB, col_width), 0)
    cols = lax.broadcasted_iota(jnp.int32, (NB, col_width), 1) + offset_ref[0]
    system_ref[:, NB:] = system_ref[:, NB:] * factor + jnp.where(rows == cols, prior_ref[...], 0.0)


def whole_row(value, index):
    return jnp.broadcast_to(value[index : index + 1, :], (STRIP, LANES))


def whole_lane(value, index):
    return jnp.broadcast_to(value[:, index : index + 1], (STRIP, LANES))


def inverse_factor(block_ref, inverse_ref):
    count = BLK // STRIP
    row_ids = lax.broadcasted_iota(jnp.int32, (STRIP, LANES), 0)
    lane_ids = lax.broadcasted_iota(jnp.int32, (STRIP, LANES), 1)
    tops = [block_ref[i * STRIP : (i + 1) * STRIP, :] for i in range(count)]
    units = [jnp.where(lane_ids == row_ids + i * STRIP, 1.0, 0.0).astype(F32) for i in range(count)]
    width = GROUP * STRIP
    for first in range(0, count, GROUP):
        panel_end = (first // PANEL + 1) * PANEL
        base = first * STRIP
        entry, top_rows, unit_rows, roots = {}, [], [], []
        for a in range(GROUP):
            for j in range((a + 1) * STRIP):
                column = whole_lane(tops[first + a], base + j)
                for i in range(max(j, a * STRIP), (a + 1) * STRIP):
                    entry[i, j] = whole_row(column, i - a * STRIP)
            top_rows += [whole_row(tops[first + a], r) for r in range(STRIP)]
            unit_rows += [whole_row(units[first + a], r) for r in range(STRIP)]
        for j in range(0, width, 2):
            corner, side, other = entry[j, j], entry[j + 1, j], entry[j + 1, j + 1]
            root = lax.rsqrt(corner)
            next_root = lax.rsqrt(corner * other - side * side) * (corner * root)
            roots += [root, next_root]
            side = side * root
            entry[j + 1, j] = side
            for i in range(j + 2, width):
                entry[i, j] = entry[i, j] * root
                entry[i, j + 1] = (entry[i, j + 1] - entry[i, j] * side) * next_root
            for k in range(j + 2, width):
                for i in range(k, width):
                    entry[i, k] = entry[i, k] - (
                        entry[i, j] * entry[k, j] + entry[i, j + 1] * entry[k, j + 1]
                    )
        for j in range(width):
            for k in range(j):
                top_rows[j] = top_rows[j] - entry[j, k] * top_rows[k]
                unit_rows[j] = unit_rows[j] - entry[j, k] * unit_rows[k]
            top_rows[j] = top_rows[j] * roots[j]
            unit_rows[j] = unit_rows[j] * roots[j]
        for i in range(first + GROUP, panel_end):
            cols = [whole_lane(tops[i], base + j) for j in range(width)]
            top, unit = tops[i], units[i]
            for j in range(width):
                for k in range(j):
                    cols[j] = cols[j] - cols[k] * entry[j, k]
                cols[j] = cols[j] * roots[j]
                top = top - cols[j] * top_rows[j]
                unit = unit - cols[j] * unit_rows[j]
            tops[i], units[i] = top, unit
        for a in range(GROUP):
            top, unit = top_rows[(a + 1) * STRIP - 1], unit_rows[(a + 1) * STRIP - 1]
            for r in range(STRIP - 1):
                top = jnp.where(row_ids == r, top_rows[a * STRIP + r], top)
                unit = jnp.where(row_ids == r, unit_rows[a * STRIP + r], unit)
            tops[first + a], units[first + a] = top, unit
            inverse_ref[(first + a) * STRIP : (first + a + 1) * STRIP, :] = unit
        if first + GROUP == panel_end and panel_end < count:
            panel = slice(panel_end - PANEL, panel_end)
            top = jnp.concatenate(tops[panel], axis=0)
            both = jnp.concatenate([top, jnp.concatenate(units[panel], axis=0)], axis=1)
            update = tn_dot(top, both, HIGH)
            for i in range(panel_end, count):
                mine = slice(i * STRIP, (i + 1) * STRIP)
                tops[i] = tops[i] - update[mine, :LANES]
                units[i] = units[i] - update[mine, LANES:]


def factor_kernel(system_ref, first_prior_ref, panel_ref, solved_ref, weighted_ref, block, inverses, right):
    count = NB // BLK
    rows = lax.broadcasted_iota(jnp.int32, (NB, NB), 0)
    cols = lax.broadcasted_iota(jnp.int32, (NB, NB), 1)
    diagonal = jnp.where(rows == cols, first_prior_ref[...], 0.0)
    system_ref[:, :NB] = system_ref[:, :NB] + diagonal

    def eliminate(k, carry):
        mine = pl.ds(pl.multiple_of(k * BLK, BLK), BLK)
        block[...] = system_ref[mine, mine]
        inverse_factor(block, inverses.at[k])
        row = jnp.dot(
            stack_left(inverses[k], 1), stack_right(system_ref[mine, :]), preferred_element_type=F32
        )
        system_ref[mine, :] = row
        right[...] = stack_right(row)
        for i in range(1, count):

            @pl.when(i > k)
            def _():
                left = stack_left(row[:, i * BLK : (i + 1) * BLK].T, 1)
                system_ref[i * BLK : (i + 1) * BLK, :] -= jnp.dot(
                    left, right[...], preferred_element_type=F32
                )

        return carry

    lax.fori_loop(0, count, eliminate, 0)
    for k in range(count - 1, -1, -1):
        mine = pl.ds(k * BLK, BLK)
        panel = system_ref[mine, NB:]
        panel_ref[mine, :] = panel
        if k < count - 1:
            panel = panel - jnp.dot(
                stack_left(system_ref[mine, (k + 1) * BLK : NB], 1),
                stack_right(solved_ref[(k + 1) * BLK :, :]),
                preferred_element_type=F32,
            )
        solved_ref[mine, :] = jnp.dot(
            stack_left(inverses[k].T, 1), stack_right(panel), preferred_element_type=F32
        )
    column = jnp.sum(diagonal, axis=1, keepdims=True)
    weighted_ref[...] = solved_ref[...] * column


def schur_kernel(
    factor,
    offset_ref,
    points_ref,
    log_weights,
    area_features_ref,
    prior_ref,
    head_ref,
    cols_ref,
    solved_ref,
    weighted_ref,
    out_ref,
    left_even,
    left_odd,
    residual,
):
    tile = pl.program_id(0)
    tiles = pl.num_programs(0)
    col_width = cols_ref.shape[0]
    total = log_weights.shape[1]
    first_points = NB + col_width
    tile_rows = out_ref.shape[0]

    @pl.when(tile == 0)
    def _():
        points = points_ref[first_points : first_points + tile_rows, :]
        transposed = solved_ref[...].T
        high = transposed.astype(BF16)
        low = (transposed - high.astype(F32)).astype(BF16)

        group = min(4096, total)

        def step(index, carry):
            base = pl.multiple_of(index * group, group)
            squares = squared_distances(points, area_features_ref, base)
            for start in range(0, group, PIECE):
                later = None
                if start + PIECE < group:
                    later = squared_distances(points, area_features_ref, base + start + PIECE)
                if start % SPAN == 0:
                    here = pl.ds(base + start, SPAN)
                    right = head_ref[:, here]
                    removed = jnp.dot(high, right, preferred_element_type=F32)
                    removed += jnp.dot(low, right, preferred_element_type=F32)
                    residual[here, :] = (cols_ref[:, here].astype(F32) - removed).astype(BF16).T
                kernel_values(left_even, squares, log_weights, base + start)
                squares = later
            return carry

        lax.fori_loop(0, total // group, step, 0)

    def run(source, dest):
        if dest is not None:
            next_row = pl.multiple_of(first_points + (tile + 1) * tile_rows, 16)
            points = points_ref[pl.ds(next_row, tile_rows), :]
        halves = max(1, col_width // 256)
        wide = col_width // halves
        pieces = [(first, half * wide) for first in range(0, total, SPAN) for half in range(halves)]
        stride = total // len(pieces)
        squares = None
        if dest is not None:
            squares = [squared_distances(points, area_features_ref, start) for start in range(0, stride, PIECE)]
        for index, (first, column) in enumerate(pieces):
            start = index * stride
            later = None
            if dest is not None and index + 1 < len(pieces):
                later = [
                    squared_distances(points, area_features_ref, start + stride + more)
                    for more in range(0, stride, PIECE)
                ]
            lanes = slice(column, column + wide)
            part = jnp.dot(
                source[:, first : first + SPAN],
                residual[first : first + SPAN, lanes],
                preferred_element_type=F32,
            )
            out_ref[:, lanes] = part if first == 0 else out_ref[:, lanes] + part
            if dest is not None:
                for more in range(0, stride, PIECE):
                    kernel_values(dest, squares[more // PIECE], log_weights, start + more)
            squares = later

    parity = lax.rem(tile, 2)
    more = tile < tiles - 1
    pl.when(jnp.logical_and(more, parity == 0))(lambda: run(left_even, left_odd))
    pl.when(jnp.logical_and(more, parity == 1))(lambda: run(left_odd, left_even))
    pl.when(jnp.logical_and(jnp.logical_not(more), parity == 0))(lambda: run(left_even, None))
    pl.when(jnp.logical_and(jnp.logical_not(more), parity == 1))(lambda: run(left_odd, None))

    rows = lax.broadcasted_iota(jnp.int32, (tile_rows, col_width), 0) + (offset_ref[1] + tile * tile_rows)
    cols = lax.broadcasted_iota(jnp.int32, (tile_rows, col_width), 1) + offset_ref[0]
    out_ref[...] = out_ref[...] * factor + jnp.where(rows == cols, prior_ref[...], 0.0)

    first_row = offset_ref[1] + tile * tile_rows

    @pl.when(first_row < NB)
    def _():
        out_ref[...] -= weighted_ref[pl.ds(pl.multiple_of(first_row, tile_rows), tile_rows), :]


def whole_kernel(factor, scale, center, offset_ref, points_ref, *refs):
    areas, rest = refs[:-18], refs[-18:]
    prior_ref, first_prior_ref, panel_ref, out_ref = rest[:4]
    head, cols, system, area_features, log_weights, features = rest[4:10]
    block, inverses, right, solved, weighted = rest[10:15]

    @pl.when(pl.program_id(0) == 0)
    def _():
        head_kernel(
            factor, scale, center, offset_ref, points_ref, *areas, prior_ref,
            head, cols, system, area_features, log_weights, features,
        )
        factor_kernel(system, first_prior_ref, panel_ref, solved, weighted, block, inverses, right)

    schur_kernel(
        factor, offset_ref, points_ref, log_weights, area_features, prior_ref,
        head, cols, solved, weighted, out_ref, *rest[15:],
    )


def all_areas(array):
    if lax.axis_size("area") == 2:
        return [array, lax.ppermute(array, "area", [(0, 1), (1, 0)])]
    return [lax.all_gather(array, "area", axis=array.ndim - 1, tiled=True)]


def from_first(array, axis):
    total = jnp.where(lax.axis_index(axis) == 0, array, 0.0)
    for target in range(1, lax.axis_size(axis)):
        total = total + lax.ppermute(array, axis, [(0, target)])
    return total


def first_block_prior(prior):
    if prior.shape[0] == NB:
        return from_first(from_first(prior.reshape(1, NB), "col"), "row")
    return lax.all_gather(prior, ("row", "col"), axis=0, tiled=True)[:NB].reshape(1, NB)


def per_device(area_xy, sampling_var, inducer_xy, order, prior):
    size_total = order.shape[0]
    length_scale = 2.0 / math.sqrt(size_total)
    scale = math.log2(math.e) / length_scale
    center = 6.0 / math.sqrt(size_total) * scale
    col_width = prior.shape[0]
    row_height = size_total // lax.axis_size("area")
    areas_total = area_xy.shape[1] * lax.axis_size("area")
    factor = size_total / areas_total

    own = jnp.concatenate([area_xy, sampling_var[None, :]], axis=0)
    areas = all_areas(own)
    first_prior = first_block_prior(prior)
    own_prior = prior.reshape(1, col_width)
    offsets = jnp.stack(
        [block_position() * col_width, lax.axis_index("area") * row_height, lax.axis_index("area")]
    ).astype(jnp.int32)

    points = gram_points(offsets, order, inducer_xy, scale, center, col_width, row_height)
    tile_rows = min(row_height, 512 if areas_total <= 8192 else 128)
    smem = pl.BlockSpec(memory_space=pltpu.SMEM)
    vmem = pl.BlockSpec(memory_space=pltpu.VMEM)
    params = pltpu.CompilerParams(vmem_limit_bytes=VMEM_BYTES)
    panel_rows, schur = pl.pallas_call(
        functools.partial(whole_kernel, factor, scale, center),
        grid=(row_height // tile_rows,),
        out_shape=(
            jax.ShapeDtypeStruct((NB, col_width), F32),
            jax.ShapeDtypeStruct((row_height, col_width), F32),
        ),
        in_specs=[smem] + [vmem] * (3 + len(areas)),
        out_specs=[vmem, pl.BlockSpec((tile_rows, col_width), lambda i: (i, 0))],
        scratch_shapes=[
            pltpu.VMEM((NB, areas_total), BF16),
            pltpu.VMEM((col_width, areas_total), BF16),
            pltpu.VMEM((NB, NB + col_width), F32),
            pltpu.VMEM((FEATURES, areas_total), BF16),
            pltpu.VMEM((1, areas_total), F32),
            pltpu.VMEM((FEATURES, areas_total), F32),
            pltpu.VMEM((BLK, BLK), F32),
            pltpu.VMEM((NB // BLK, BLK, BLK), F32),
            pltpu.VMEM((6 * BLK, NB + col_width), BF16),
            pltpu.VMEM((NB, col_width), F32),
            pltpu.VMEM((NB, col_width), F32),
            pltpu.VMEM((tile_rows, areas_total), BF16),
            pltpu.VMEM((tile_rows, areas_total), BF16),
            pltpu.VMEM((areas_total, col_width), BF16),
        ],
        compiler_params=params,
        cost_estimate=pl.CostEstimate(flops=5 * 10**10, bytes_accessed=2**24, transcendentals=0),
        name="schur",
    )(offsets, points, *areas, own_prior, first_prior)
    return (panel_rows, schur)


def solution(mesh):
    in_specs = (P(None, "area"), P("area"), P(), P(), P(("row", "col")))
    out_specs = (P(None, ("row", "col")), P("area", ("row", "col")))
    return jax.shard_map(
        per_device, mesh=mesh, in_specs=in_specs, out_specs=out_specs, check_vma=False
    )
```

```python
import functools
import math

import jax
import jax.numpy as jnp
from jax import lax
from jax.experimental import pallas as pl
from jax.experimental.pallas import tpu as pltpu
from jax.sharding import PartitionSpec as P

NB = 512
LANES = 128
STRIP = 8
GROUP = 1
PANEL = 4
BLK = 128
CHUNK = 1024
SPAN = 512
PIECE = 256
VMEM_BYTES = 60 * 1024 * 1024
HIGH = lax.Precision.HIGHEST
F32 = jnp.float32
BF16 = jnp.bfloat16


def split_pieces(value):
    first = value.astype(BF16)
    rest = value - first.astype(F32)
    second = rest.astype(BF16)
    third = (rest - second.astype(F32)).astype(BF16)
    return first, second, third


def nt_dot(left, right, precision=None):
    return lax.dot_general(
        left, right, (((1,), (1,)), ((), ())), precision=precision, preferred_element_type=F32
    )


def tn_dot(left, right, precision=None):
    return lax.dot_general(
        left, right, (((0,), (0,)), ((), ())), precision=precision, preferred_element_type=F32
    )


def stack_left(value, axis):
    a, b, c = split_pieces(value)
    return jnp.concatenate([a, a, b, b, a, c], axis=axis)


def stack_right(value):
    a, b, c = split_pieces(value)
    return jnp.concatenate([a, b, a, b, c, a], axis=0)


def block_position():
    return lax.axis_index("row") * lax.axis_size("col") + lax.axis_index("col")


FEATURES = 32
PIECE_PAIRS = ((0, 0), (0, 1), (1, 0), (1, 1), (0, 2), (2, 0))


def write_features(dest, x_row, y_row, left):
    one = jnp.ones_like(x_row)
    norm = [piece.astype(F32) for piece in split_pieces(x_row * x_row + y_row * y_row)]
    rows = norm + [one] * 3 if left else [one] * 3 + norm
    for coordinate in (x_row, y_row):
        factor = 1.0 if left else -2.0
        pieces = [piece.astype(F32) * factor for piece in split_pieces(coordinate)]
        rows += [pieces[pair[0 if left else 1]] for pair in PIECE_PAIRS]
    for index, row in enumerate(rows):
        dest[index : index + 1, :] = row


def points_kernel(
    scale, center, col_width, offset_ref, order_ref, table_ref, features_ref, columns_ref, places, features, tables
):
    quotients = order_ref.shape[0]
    for q in range(quotients):
        for k in range(2):
            tables[k, q : q + 1, :] = table_ref[k : k + 1, q * LANES : (q + 1) * LANES]
    pieces_x = split_pieces(tables[0] * scale - center)
    pieces_y = split_pieces(tables[1] * scale - center)
    columns_ref[...] = jnp.concatenate(
        [jnp.concatenate(pieces_x, axis=0), jnp.concatenate(pieces_y, axis=0)], axis=1
    ).T
    quotient_ids = lax.broadcasted_iota(jnp.int32, (quotients, LANES), 0)
    lane_ids = lax.broadcasted_iota(jnp.int32, (LANES, LANES), 0)

    def one_block(step):
        row = step
        if step >= (NB + col_width) // LANES:
            row = offset_ref[1] // LANES + step - (NB + col_width) // LANES
        elif step >= NB // LANES:
            row = offset_ref[0] // LANES + step - NB // LANES
        ids = order_ref[pl.ds(row, 1), :]
        hit = jnp.where(quotient_ids == lax.shift_right_logical(ids, 7), 1.0, 0.0).astype(BF16)
        values = jnp.dot(
            columns_ref[...], jnp.concatenate([hit, hit, hit], axis=0), preferred_element_type=F32
        )
        mine = lane_ids == lax.bitwise_and(ids, LANES - 1)
        return [
            jnp.sum(jnp.where(mine, values[k * LANES : (k + 1) * LANES], 0.0), axis=0, keepdims=True)
            for k in range(2)
        ]

    blocks = features_ref.shape[0] // LANES
    for step in range(blocks):
        x_row, y_row = one_block(step)
        places[0:1, step * LANES : (step + 1) * LANES] = x_row
        places[1:2, step * LANES : (step + 1) * LANES] = y_row
    features[...] = jnp.zeros_like(features)
    write_features(features, places[0:1, :], places[1:2, :], True)
    for step in range(blocks):
        mine = slice(step * LANES, (step + 1) * LANES)
        features_ref[mine, :] = features[:, mine].T.astype(BF16)


def gram_points(offsets, order, inducer_xy, scale, center, col_width, row_height):
    quotients = order.shape[0] // LANES
    count = NB + col_width + row_height
    return pl.pallas_call(
        functools.partial(points_kernel, scale, center, col_width),
        out_shape=jax.ShapeDtypeStruct((count, FEATURES), BF16),
        in_specs=[
            pl.BlockSpec(memory_space=pltpu.SMEM),
            pl.BlockSpec(memory_space=pltpu.VMEM),
            pl.BlockSpec(memory_space=pltpu.VMEM),
        ],
        out_specs=pl.BlockSpec(memory_space=pltpu.VMEM),
        scratch_shapes=[
            pltpu.VMEM((2 * LANES, 3 * quotients), BF16),
            pltpu.VMEM((2, count), F32),
            pltpu.VMEM((FEATURES, count), F32),
            pltpu.VMEM((2, quotients, LANES), F32),
        ],
        compiler_params=pltpu.CompilerParams(vmem_limit_bytes=VMEM_BYTES),
        cost_estimate=pl.CostEstimate(flops=5 * 10**9, bytes_accessed=2**20, transcendentals=0),
        name="points",
    )(offsets, order.reshape(quotients, LANES), inducer_xy)


def root(square):
    square = jnp.maximum(square, 1e-30)
    return square * lax.rsqrt(square)


def squared_distances(points, area_features, first):
    return jnp.dot(points, area_features[:, pl.ds(first, PIECE)], preferred_element_type=F32)


def kernel_values(dest, squares, log_weights, first):
    for half in range(0, PIECE, LANES):
        lanes = pl.ds(first + half, LANES)
        weights = jnp.broadcast_to(log_weights[0:1, lanes], (16, LANES))
        for row in range(0, squares.shape[0], 16):
            distance = root(squares[row : row + 16, half : half + LANES])
            dest[row : row + 16, lanes] = jnp.exp2(weights - distance).astype(BF16)


def fill_kernel(dest, points, area_features, log_weights, first, count):
    for start in range(0, count, PIECE):
        squares = squared_distances(points, area_features, first + start)
        kernel_values(dest, squares, log_weights, first + start)


def head_kernel(
    factor,
    scale,
    center,
    offset_ref,
    points_ref,
    *refs,
):
    *area_refs, prior_ref, head_ref, cols_ref, system_ref, area_features_ref, log_weights, features = refs
    col_width = cols_ref.shape[0]
    total = area_features_ref.shape[1]
    features[...] = jnp.zeros_like(features)
    width = total // len(area_refs)
    for index in range(len(area_refs)):
        values = area_refs[index][...]
        if len(area_refs) == 2:
            values = jnp.where(offset_ref[2] == index, area_refs[0][...], area_refs[1][...])
        lanes = slice(index * width, (index + 1) * width)
        places = values[0:2] * scale - center
        write_features(features.at[:, lanes], places[0:1], places[1:2], False)
        log_weights[:, lanes] = -0.5 * jnp.log2(0.5 + values[2:3])
    area_features_ref[...] = features[...].astype(BF16)
    system_ref[...] = jnp.zeros_like(system_ref)
    group = min(4096, total)

    def step(index, carry):
        base = pl.multiple_of(index * group, group)
        targets = [(head_ref, points_ref[:NB, :]), (cols_ref, points_ref[NB : NB + col_width, :])]

        def distances(start):
            return [squared_distances(points, area_features_ref, base + start) for _, points in targets]

        def accumulate(start):
            here = pl.ds(base + start, CHUNK)
            left = head_ref[:, here]
            system_ref[:, :NB] += nt_dot(left, left)
            system_ref[:, NB:] += nt_dot(left, cols_ref[:, here])

        squares = distances(0)
        for start in range(0, group, PIECE):
            later = distances(start + PIECE) if start + PIECE < group else None
            if start and start % CHUNK == 0:
                accumulate(start - CHUNK)
            for (dest, _), square in zip(targets, squares):
                kernel_values(dest, square, log_weights, base + start)
            squares = later
        accumulate(group - CHUNK)
        return carry

    lax.fori_loop(0, total // group, step, 0)
    system_ref[:, :NB] = system_ref[:, :NB] * factor
    rows = lax.broadcasted_iota(jnp.int32, (NB, col_width), 0)
    cols = lax.broadcasted_iota(jnp.int32, (NB, col_width), 1) + offset_ref[0]
    system_ref[:, NB:] = system_ref[:, NB:] * factor + jnp.where(rows == cols, prior_ref[...], 0.0)


def whole_row(value, index):
    return jnp.broadcast_to(value[index : index + 1, :], (STRIP, LANES))


def whole_lane(value, index):
    return jnp.broadcast_to(value[:, index : index + 1], (STRIP, LANES))


def inverse_factor(block_ref, inverse_ref):
    count = BLK // STRIP
    row_ids = lax.broadcasted_iota(jnp.int32, (STRIP, LANES), 0)
    lane_ids = lax.broadcasted_iota(jnp.int32, (STRIP, LANES), 1)
    tops = [block_ref[i * STRIP : (i + 1) * STRIP, :] for i in range(count)]
    units = [jnp.where(lane_ids == row_ids + i * STRIP, 1.0, 0.0).astype(F32) for i in range(count)]
    width = GROUP * STRIP
    for first in range(0, count, GROUP):
        panel_end = (first // PANEL + 1) * PANEL
        base = first * STRIP
        entry, top_rows, unit_rows, roots = {}, [], [], []
        for a in range(GROUP):
            for j in range((a + 1) * STRIP):
                column = whole_lane(tops[first + a], base + j)
                for i in range(max(j, a * STRIP), (a + 1) * STRIP):
                    entry[i, j] = whole_row(column, i - a * STRIP)
            top_rows += [whole_row(tops[first + a], r) for r in range(STRIP)]
            unit_rows += [whole_row(units[first + a], r) for r in range(STRIP)]
        for j in range(0, width, 2):
            corner, side, other = entry[j, j], entry[j + 1, j], entry[j + 1, j + 1]
            root = lax.rsqrt(corner)
            next_root = lax.rsqrt(corner * other - side * side) * (corner * root)
            roots += [root, next_root]
            side = side * root
            entry[j + 1, j] = side
            for i in range(j + 2, width):
                entry[i, j] = entry[i, j] * root
                entry[i, j + 1] = (entry[i, j + 1] - entry[i, j] * side) * next_root
            for k in range(j + 2, width):
                for i in range(k, width):
                    entry[i, k] = entry[i, k] - (
                        entry[i, j] * entry[k, j] + entry[i, j + 1] * entry[k, j + 1]
                    )
        for j in range(width):
            for k in range(j):
                top_rows[j] = top_rows[j] - entry[j, k] * top_rows[k]
                unit_rows[j] = unit_rows[j] - entry[j, k] * unit_rows[k]
            top_rows[j] = top_rows[j] * roots[j]
            unit_rows[j] = unit_rows[j] * roots[j]
        for i in range(first + GROUP, panel_end):
            cols = [whole_lane(tops[i], base + j) for j in range(width)]
            top, unit = tops[i], units[i]
            for j in range(width):
                for k in range(j):
                    cols[j] = cols[j] - cols[k] * entry[j, k]
                cols[j] = cols[j] * roots[j]
                top = top - cols[j] * top_rows[j]
                unit = unit - cols[j] * unit_rows[j]
            tops[i], units[i] = top, unit
        for a in range(GROUP):
            top, unit = top_rows[(a + 1) * STRIP - 1], unit_rows[(a + 1) * STRIP - 1]
            for r in range(STRIP - 1):
                top = jnp.where(row_ids == r, top_rows[a * STRIP + r], top)
                unit = jnp.where(row_ids == r, unit_rows[a * STRIP + r], unit)
            tops[first + a], units[first + a] = top, unit
            inverse_ref[(first + a) * STRIP : (first + a + 1) * STRIP, :] = unit
        if first + GROUP == panel_end and panel_end < count:
            panel = slice(panel_end - PANEL, panel_end)
            top = jnp.concatenate(tops[panel], axis=0)
            both = jnp.concatenate([top, jnp.concatenate(units[panel], axis=0)], axis=1)
            update = tn_dot(top, both, HIGH)
            for i in range(panel_end, count):
                mine = slice(i * STRIP, (i + 1) * STRIP)
                tops[i] = tops[i] - update[mine, :LANES]
                units[i] = units[i] - update[mine, LANES:]


def factor_kernel(system_ref, first_prior_ref, panel_ref, solved_ref, weighted_ref, block, inverses, right):
    count = NB // BLK
    rows = lax.broadcasted_iota(jnp.int32, (NB, NB), 0)
    cols = lax.broadcasted_iota(jnp.int32, (NB, NB), 1)
    diagonal = jnp.where(rows == cols, first_prior_ref[...], 0.0)
    system_ref[:, :NB] = system_ref[:, :NB] + diagonal

    def eliminate(k, carry):
        mine = pl.ds(pl.multiple_of(k * BLK, BLK), BLK)
        block[...] = system_ref[mine, mine]
        inverse_factor(block, inverses.at[k])
        row = jnp.dot(
            stack_left(inverses[k], 1), stack_right(system_ref[mine, :]), preferred_element_type=F32
        )
        system_ref[mine, :] = row
        right[...] = stack_right(row)
        for i in range(1, count):

            @pl.when(i > k)
            def _():
                left = stack_left(row[:, i * BLK : (i + 1) * BLK].T, 1)
                system_ref[i * BLK : (i + 1) * BLK, :] -= jnp.dot(
                    left, right[...], preferred_element_type=F32
                )

        return carry

    lax.fori_loop(0, count, eliminate, 0)
    for k in range(count - 1, -1, -1):
        mine = pl.ds(k * BLK, BLK)
        panel = system_ref[mine, NB:]
        panel_ref[mine, :] = panel
        if k < count - 1:
            panel = panel - jnp.dot(
                stack_left(system_ref[mine, (k + 1) * BLK : NB], 1),
                stack_right(solved_ref[(k + 1) * BLK :, :]),
                preferred_element_type=F32,
            )
        solved_ref[mine, :] = jnp.dot(
            stack_left(inverses[k].T, 1), stack_right(panel), preferred_element_type=F32
        )
    column = jnp.sum(diagonal, axis=1, keepdims=True)
    weighted_ref[...] = solved_ref[...] * column


def schur_kernel(
    factor,
    offset_ref,
    points_ref,
    log_weights,
    area_features_ref,
    prior_ref,
    head_ref,
    cols_ref,
    solved_ref,
    weighted_ref,
    out_ref,
    left_even,
    left_odd,
    residual,
):
    tile = pl.program_id(0)
    tiles = pl.num_programs(0)
    col_width = cols_ref.shape[0]
    total = log_weights.shape[1]
    first_points = NB + col_width
    tile_rows = out_ref.shape[0]

    @pl.when(tile == 0)
    def _():
        points = points_ref[first_points : first_points + tile_rows, :]
        transposed = solved_ref[...].T
        high = transposed.astype(BF16)
        low = (transposed - high.astype(F32)).astype(BF16)

        group = min(4096, total)

        def step(index, carry):
            base = pl.multiple_of(index * group, group)
            squares = squared_distances(points, area_features_ref, base)
            for start in range(0, group, PIECE):
                later = None
                if start + PIECE < group:
                    later = squared_distances(points, area_features_ref, base + start + PIECE)
                if start % SPAN == 0:
                    here = pl.ds(base + start, SPAN)
                    right = head_ref[:, here]
                    removed = jnp.dot(high, right, preferred_element_type=F32)
                    removed += jnp.dot(low, right, preferred_element_type=F32)
                    left = cols_ref[:, here].astype(F32) - removed
                    residual[here, :] = (left * factor).astype(BF16).T
                kernel_values(left_even, squares, log_weights, base + start)
                squares = later
            return carry

        lax.fori_loop(0, total // group, step, 0)

    def run(source, dest):
        if dest is not None:
            next_row = pl.multiple_of(first_points + (tile + 1) * tile_rows, 16)
            points = points_ref[pl.ds(next_row, tile_rows), :]
        halves = max(1, col_width // 256)
        wide = col_width // halves
        pieces = [(first, half * wide) for first in range(0, total, SPAN) for half in range(halves)]
        stride = total // len(pieces)
        squares = None
        if dest is not None:
            squares = [squared_distances(points, area_features_ref, start) for start in range(0, stride, PIECE)]
        for index, (first, column) in enumerate(pieces):
            start = index * stride
            later = None
            if dest is not None and index + 1 < len(pieces):
                later = [
                    squared_distances(points, area_features_ref, start + stride + more)
                    for more in range(0, stride, PIECE)
                ]
            lanes = slice(column, column + wide)
            part = jnp.dot(
                source[:, first : first + SPAN],
                residual[first : first + SPAN, lanes],
                preferred_element_type=F32,
            )
            out_ref[:, lanes] = part if first == 0 else out_ref[:, lanes] + part
            if dest is not None:
                for more in range(0, stride, PIECE):
                    kernel_values(dest, squares[more // PIECE], log_weights, start + more)
            squares = later

    parity = lax.rem(tile, 2)
    more = tile < tiles - 1
    pl.when(jnp.logical_and(more, parity == 0))(lambda: run(left_even, left_odd))
    pl.when(jnp.logical_and(more, parity == 1))(lambda: run(left_odd, left_even))
    pl.when(jnp.logical_and(jnp.logical_not(more), parity == 0))(lambda: run(left_even, None))
    pl.when(jnp.logical_and(jnp.logical_not(more), parity == 1))(lambda: run(left_odd, None))

    first_row = offset_ref[1] + tile * tile_rows
    first_col = offset_ref[0]

    @pl.when(jnp.logical_and(first_row < first_col + col_width, first_col < first_row + tile_rows))
    def _():
        rows = lax.broadcasted_iota(jnp.int32, (tile_rows, col_width), 0) + first_row
        cols = lax.broadcasted_iota(jnp.int32, (tile_rows, col_width), 1) + first_col
        out_ref[...] += jnp.where(rows == cols, prior_ref[...], 0.0)

    @pl.when(first_row < NB)
    def _():
        out_ref[...] -= weighted_ref[pl.ds(pl.multiple_of(first_row, tile_rows), tile_rows), :]


def whole_kernel(factor, scale, center, offset_ref, points_ref, *refs):
    areas, rest = refs[:-18], refs[-18:]
    prior_ref, first_prior_ref, panel_ref, out_ref = rest[:4]
    head, cols, system, area_features, log_weights, features = rest[4:10]
    block, inverses, right, solved, weighted = rest[10:15]

    @pl.when(pl.program_id(0) == 0)
    def _():
        head_kernel(
            factor, scale, center, offset_ref, points_ref, *areas, prior_ref,
            head, cols, system, area_features, log_weights, features,
        )
        factor_kernel(system, first_prior_ref, panel_ref, solved, weighted, block, inverses, right)

    schur_kernel(
        factor, offset_ref, points_ref, log_weights, area_features, prior_ref,
        head, cols, solved, weighted, out_ref, *rest[15:],
    )


def all_areas(array):
    if lax.axis_size("area") == 2:
        return [array, lax.ppermute(array, "area", [(0, 1), (1, 0)])]
    return [lax.all_gather(array, "area", axis=array.ndim - 1, tiled=True)]


def from_first(array, axis):
    total = jnp.where(lax.axis_index(axis) == 0, array, 0.0)
    for target in range(1, lax.axis_size(axis)):
        total = total + lax.ppermute(array, axis, [(0, target)])
    return total


def first_block_prior(prior):
    if prior.shape[0] == NB:
        return from_first(from_first(prior.reshape(1, NB), "col"), "row")
    return lax.all_gather(prior, ("row", "col"), axis=0, tiled=True)[:NB].reshape(1, NB)


def per_device(area_xy, sampling_var, inducer_xy, order, prior):
    size_total = order.shape[0]
    length_scale = 2.0 / math.sqrt(size_total)
    scale = math.log2(math.e) / length_scale
    center = 6.0 / math.sqrt(size_total) * scale
    col_width = prior.shape[0]
    row_height = size_total // lax.axis_size("area")
    areas_total = area_xy.shape[1] * lax.axis_size("area")
    factor = size_total / areas_total

    own = jnp.concatenate([area_xy, sampling_var[None, :]], axis=0)
    areas = all_areas(own)
    first_prior = first_block_prior(prior)
    own_prior = prior.reshape(1, col_width)
    offsets = jnp.stack(
        [block_position() * col_width, lax.axis_index("area") * row_height, lax.axis_index("area")]
    ).astype(jnp.int32)

    points = gram_points(offsets, order, inducer_xy, scale, center, col_width, row_height)
    tile_rows = min(row_height, 512 if areas_total <= 8192 else 128)
    smem = pl.BlockSpec(memory_space=pltpu.SMEM)
    vmem = pl.BlockSpec(memory_space=pltpu.VMEM)
    params = pltpu.CompilerParams(vmem_limit_bytes=VMEM_BYTES)
    panel_rows, schur = pl.pallas_call(
        functools.partial(whole_kernel, factor, scale, center),
        grid=(row_height // tile_rows,),
        out_shape=(
            jax.ShapeDtypeStruct((NB, col_width), F32),
            jax.ShapeDtypeStruct((row_height, col_width), F32),
        ),
        in_specs=[smem] + [vmem] * (3 + len(areas)),
        out_specs=[vmem, pl.BlockSpec((tile_rows, col_width), lambda i: (i, 0))],
        scratch_shapes=[
            pltpu.VMEM((NB, areas_total), BF16),
            pltpu.VMEM((col_width, areas_total), BF16),
            pltpu.VMEM((NB, NB + col_width), F32),
            pltpu.VMEM((FEATURES, areas_total), BF16),
            pltpu.VMEM((1, areas_total), F32),
            pltpu.VMEM((FEATURES, areas_total), F32),
            pltpu.VMEM((BLK, BLK), F32),
            pltpu.VMEM((NB // BLK, BLK, BLK), F32),
            pltpu.VMEM((6 * BLK, NB + col_width), BF16),
            pltpu.VMEM((NB, col_width), F32),
            pltpu.VMEM((NB, col_width), F32),
            pltpu.VMEM((tile_rows, areas_total), BF16),
            pltpu.VMEM((tile_rows, areas_total), BF16),
            pltpu.VMEM((areas_total, col_width), BF16),
        ],
        compiler_params=params,
        cost_estimate=pl.CostEstimate(flops=5 * 10**10, bytes_accessed=2**24, transcendentals=0),
        name="schur",
    )(offsets, points, *areas, own_prior, first_prior)
    return (panel_rows, schur)


def solution(mesh):
    in_specs = (P(None, "area"), P("area"), P(), P(), P(("row", "col")))
    out_specs = (P(None, ("row", "col")), P("area", ("row", "col")))
    return jax.shard_map(
        per_device, mesh=mesh, in_specs=in_specs, out_specs=out_specs, check_vma=False
    )
```
